32 devices in a mesh: section: 2 (over core), ctx: 4 (over z), fsdp: 4 (over y, x).
Axes of the slice: x: 2, y: 2, z: 4, core: 2. Of those that a mesh axis runs over, the one named last changes fastest.
Arguments:
- tokens: bfloat16 [2, 4, 1024, 768], P(None, 'fsdp', 'ctx'), may hold values from -6 to 6
- cotangent: bfloat16 [2, 4, 1024, 768], P(None, 'fsdp', 'ctx'), may hold values from -6 to 6
- span_order: int32 [4], replicated, may hold values from 0 to 3, each once
- w_qkv: bfloat16 [2, 768, 2304], P('section', 'fsdp'), may hold values from -0.21875 to 0.21875
- w_out: bfloat16 [2, 768, 768], P('section', 'fsdp'), may hold values from -1.25 to 1.25
- w_up: bfloat16 [2, 768, 3072], P('section', 'fsdp'), may hold values from -0.3125 to 0.3125
- w_down: bfloat16 [2, 3072, 768], P('section', 'fsdp'), may hold values from -0.21875 to 0.21875
- norm_gains: bfloat16 [2, 2, 768], P('section', None, 'fsdp'), may hold values from 0.25 to 1.75
- bias_rows: bfloat16 [2, 6, 768], P('section', None, 'fsdp'), may hold values from -3 to 3
- bias_hidden: bfloat16 [2, 3072], P('section', 'fsdp'), may hold values from -3 to 3
Outputs:
- layer_outputs: bfloat16 [2, 2, 4, 1024, 768], P('section', None, 'fsdp', 'ctx')
- input_grads: float32 [2, 2, 4, 1024, 768], P('section', None, 'fsdp', 'ctx')
- grad_w_qkv: float32 [2, 768, 2304], P('section', 'fsdp')
- grad_w_out: float32 [2, 768, 768], P('section', 'fsdp')
- grad_w_up: float32 [2, 768, 3072], P('section', 'fsdp')
- grad_w_down: float32 [2, 3072, 768], P('section', 'fsdp')
- grad_norm_gains: float32 [2, 2, 768], P('section', None, 'fsdp')
- grad_bias_rows: float32 [2, 6, 768], P('section', None, 'fsdp')
- grad_bias_hidden: float32 [2, 3072], P('section', 'fsdp')
The draws below stay inside these ranges and needn't reach their ends.
Inputs may be any that keep to these rules, and one draw needn't show every extreme that they name: Ctx index c holds, in this order, span number span_order[c] and span number 2 * 4 - 1 - span_order[c] of 128 tokens of every sequence; each value appears once.
All inputs are finite; a program needn't handle non-finite values.
Results may differ from the reference program's by a relative error of at most 0.019.
Values may be sent and summed in bfloat16 or wider, within the bound.
No kernel may reach another device: no remote copies, remote signals or barrier semaphores. Data moves between devices by JAX's collectives and lax.ppermute only.
A program may use at most 192 MiB of HBM per device.

```python
import jax
import jax.numpy as jnp
from jax import lax

D = 768
HEADS = 12
HEAD_DIM = 64
FF = 3072
LENGTH = 1024
MICRO = 2
GROUPS = 4
N_CTX = 4


def block_levels(key, dims, cuts, smallest, top_value):
    loudness, own = 1.0, jax.random.fold_in(key, 6)
    for dim, shards_of in cuts:
        steps = jnp.exp(jax.random.uniform(jax.random.fold_in(own, dim), (shards_of,), jnp.float32, smallest / len(cuts), top_value / len(cuts)))
        loudness = loudness * jnp.repeat(steps, dims[dim] // shards_of).reshape([-1 if axis == dim else 1 for axis in range(len(dims))])
    return loudness


def normal_values(stream_key, shape, scale, reach, cuts=(), kind=jnp.bfloat16):
    values = jax.random.normal(stream_key, shape, jnp.float32) * scale
    if len(cuts) > 0:
        values = block_levels(stream_key, shape, cuts, -0.22, 0.18) * values
    return jnp.clip(values, min=-reach, max=reach).astype(kind)


def setup_inputs(seed: int = 0) -> dict:
    keys = jax.random.split(jax.random.key(seed), 11)
    tokens = normal_values(keys[0], (MICRO, GROUPS, LENGTH, D), 1.0, 6.0, ((1, 4), (2, 4)))
    cotangent = normal_values(keys[1], (MICRO, GROUPS, LENGTH, D), 1.0, 6.0, ((1, 4), (2, 4)))
    span_order = jax.random.permutation(keys[2], N_CTX).astype(jnp.int32)
    w_qkv = normal_values(keys[3], (2, D, 3 * D), D ** -0.5, 0.21875, ((0, 2), (1, 4)))
    w_out = normal_values(keys[4], (2, D, D), (D // 32) ** -0.5, 1.25, ((0, 2), (1, 4)))
    w_up = normal_values(keys[5], (2, D, FF), (D // 2) ** -0.5, 0.3125, ((0, 2), (1, 4)))
    w_down = normal_values(keys[6], (2, FF, D), (FF // 4) ** -0.5, 0.21875, ((0, 2), (1, 4)))
    norm_gains = jnp.clip(1.0 + 0.15 * jax.random.normal(keys[7], (2, 2, D), jnp.float32), 0.25, 1.75).astype(jnp.bfloat16)
    bias_rows = normal_values(keys[8], (2, 6, D), 0.5, 3.0, ((0, 2), (2, 4)))
    bias_hidden = normal_values(keys[9], (2, FF), 0.5, 3.0, ((0, 2), (1, 4)))
    return dict(tokens=tokens, cotangent=cotangent, span_order=span_order, w_qkv=w_qkv, w_out=w_out, w_up=w_up, w_down=w_down, norm_gains=norm_gains, bias_rows=bias_rows, bias_hidden=bias_hidden)


@jax.custom_vjp
def low(v):
    return lax.optimization_barrier(v.astype(jnp.bfloat16)).astype(jnp.float32)

@jax.custom_vjp
def low_back(v):
    return v

def low_keep(v):
    return (low(v), None)

def low_pass(kept, grad):
    return (grad,)

def back_keep(v):
    return (v, None)

def back_low(kept, grad):
    return (low(grad),)
low.defvjp(low_keep, low_pass)
low_back.defvjp(back_keep, back_low)
epsilon = 1e-05
highest = lax.Precision.HIGHEST

def positions(row_ids, span_order, span_len):
    cycle_size = span_order.shape[0]
    holder = row_ids // (2 * span_len)
    second = row_ids // span_len % 2
    lookup = lax.optimization_barrier(jnp.sum(jnp.where(holder[:, None] == jnp.arange(cycle_size, dtype=jnp.int32)[None, :], span_order[None, :], 0), axis=1))
    span_ids = jnp.where(second == 0, lookup, 2 * cycle_size - 1 - lookup)
    return (span_ids * span_len + row_ids % span_len).astype(jnp.int32)

def layer_norm(values, gain_row, shift_row):
    centred = values - lax.optimization_barrier(jnp.mean(values, axis=-1, keepdims=True))
    spread = lax.optimization_barrier(jnp.mean(centred * centred, axis=-1, keepdims=True))
    return centred * lax.rsqrt(spread + epsilon) * gain_row + shift_row

def high_dot(left, right):
    return jnp.dot(left, right, precision=highest)

def attention(queries, key_rows, value_rows, places):
    seq_len = queries.shape[0]
    block_len = min(512, seq_len)
    block_count = seq_len // block_len
    query_blocks = queries.reshape(block_count, block_len, HEADS, HEAD_DIM)
    place_blocks = places.reshape(block_count, block_len)

    def one_block(block_args):
        query_part, place_part = block_args
        scores = jnp.einsum('qhd,khd->hqk', query_part, key_rows, precision=highest) * 0.125
        scores = low_back(scores)
        allowed = places[None, None, :] <= place_part[None, :, None]
        scores = jnp.where(allowed, scores, -1e+30)
        row_top = lax.optimization_barrier(jnp.max(scores, axis=-1, keepdims=True))
        expd_scores = jnp.exp(scores - row_top)
        attn_probs = low(expd_scores / lax.optimization_barrier(jnp.sum(expd_scores, axis=-1, keepdims=True)))
        return jnp.einsum('hqk,khd->qhd', attn_probs, value_rows, precision=highest)
    mixed_blocks = lax.map(jax.checkpoint(one_block), (query_blocks, place_blocks))
    return mixed_blocks.reshape(seq_len, HEADS * HEAD_DIM)

def layer(layer_in, params, places):
    w_qkv, w_out, w_up, w_down, gain_rows, shift_rows, hidden_bias = params
    width = layer_in.shape[1]
    seq_len = layer_in.shape[0]
    normed = low(layer_norm(layer_in, gain_rows[0], shift_rows[0]))
    qkv_bias = jnp.concatenate([shift_rows[1], jnp.zeros_like(shift_rows[1]), shift_rows[2]])
    projected = low(low_back(high_dot(normed, w_qkv) + qkv_bias))
    queries = projected[:, :width].reshape(seq_len, HEADS, HEAD_DIM)
    key_rows = projected[:, width:2 * width].reshape(seq_len, HEADS, HEAD_DIM)
    value_rows = projected[:, 2 * width:].reshape(seq_len, HEADS, HEAD_DIM)
    mixed_out = low(low_back(attention(queries, key_rows, value_rows, places)))
    attn_branch = low_back(high_dot(mixed_out, w_out) + shift_rows[3])
    inner_sum = layer_in + attn_branch
    middle = low(layer_norm(inner_sum, gain_rows[1], shift_rows[4]))
    hidden_pre = low_back(high_dot(middle, w_up) + hidden_bias)
    activated = low(jax.nn.gelu(hidden_pre, approximate=True))
    return low(low_back(inner_sum + high_dot(activated, w_down) + shift_rows[5]))

def network(seq_in, probe_add, first_layer, second_layer, places):
    out_first = layer(seq_in, first_layer, places)
    out_second = layer(out_first + probe_add, second_layer, places)
    return (out_first, out_second)

def reference(tokens, cotangent, span_order, w_qkv, w_out, w_up, w_down, norm_gains, bias_rows, bias_hidden):
    span_len = LENGTH // (2 * N_CTX)
    places = positions(jnp.arange(LENGTH, dtype=jnp.int32), span_order, span_len)
    weights = tuple((array.astype(jnp.float32) for array in (w_qkv, w_out, w_up, w_down, norm_gains, bias_rows, bias_hidden)))
    seq_inputs = tokens.reshape(MICRO * GROUPS, LENGTH, D).astype(jnp.float32)
    seq_cots = cotangent.reshape(MICRO * GROUPS, LENGTH, D).astype(jnp.float32)

    def seq_step(carried, seq_item):
        seq_in, seq_cot = seq_item

        def run_net(values_in, probe_add, params):
            first_layer = tuple((weight[0] for weight in params))
            second_layer = tuple((weight[1] for weight in params))
            return network(values_in, probe_add, first_layer, second_layer, places)
        outputs, pull_back = jax.vjp(run_net, seq_in, jnp.zeros_like(seq_in), weights)
        grad_seq, grad_probe, grad_params = pull_back((jnp.zeros_like(outputs[0]), seq_cot))
        carried = tuple((total + part for total, part in zip(carried, grad_params)))
        return (carried, (outputs[0].astype(jnp.bfloat16), outputs[1].astype(jnp.bfloat16), grad_seq, grad_probe))
    initial = tuple((jnp.zeros_like(weight) for weight in weights))
    grad_sums, seq_results = lax.scan(seq_step, initial, (seq_inputs, seq_cots))
    full_shape = (MICRO, GROUPS, LENGTH, D)
    layer_outs = jnp.stack([seq_results[0].reshape(full_shape), seq_results[1].reshape(full_shape)])
    grad_inputs = jnp.stack([seq_results[2].reshape(full_shape), seq_results[3].reshape(full_shape)])
    return (layer_outs, grad_inputs, grad_sums[0], grad_sums[1], grad_sums[2], grad_sums[3], grad_sums[4], grad_sums[5], grad_sums[6])
```

```python
import functools

import jax
import jax.numpy as jnp
from jax import lax
from jax.experimental import pallas as pl
from jax.experimental.pallas import tpu as pltpu
from jax.sharding import PartitionSpec as P

HEADS = 12
EPS = 1e-05
GELU_C = 0.7978845608
GELU_A = 0.044715
LANES = 128
BF = jnp.bfloat16
F32 = jnp.float32


def dot(a, b, ca, cb):
    return lax.dot_general(a, b, (((ca,), (cb,)), ((), ())), preferred_element_type=F32)


def swap_cores(value):
    count = lax.axis_size("section")
    return lax.ppermute(value, "section", [(s, count - 1 - s) for s in range(count)])


def move_spans(order_ref, ctx, span, copy):
    for c in range(ctx):
        first = order_ref[c]
        for half, span_id in ((0, first), (1, 2 * ctx - 1 - first)):
            copy(c, half, pl.multiple_of(span_id * span, span))


def causal(scores, width, fill):
    depth = scores.shape[0]
    keys = lax.broadcasted_iota(jnp.int32, (width, width), 0)
    rows = lax.broadcasted_iota(jnp.int32, (width, width), 1)
    last = jnp.where(keys <= rows, scores[depth - width :], fill)
    if depth == width:
        return last
    return jnp.concatenate([scores[: depth - width], last], axis=0)


def attn_fwd_kernel(order_ref, qkv_ref, mixed_ref, sorted_ref, out_ref, lse_ref, *, heads, size, block):
    ctx, _, rows = qkv_ref.shape
    span = rows // 2
    feats = heads * size
    seq = ctx * rows

    def bring(c, half, place):
        sorted_ref[:, pl.ds(place, span)] = qkv_ref[c, :, half * span : (half + 1) * span]

    move_spans(order_ref, ctx, span, bring)
    lse_ref[...] = jnp.zeros_like(lse_ref)
    for h in range(heads):
        for start in range(0, seq, block):
            end = start + block
            q = sorted_ref[h * size : (h + 1) * size, start:end]
            k = sorted_ref[feats + h * size : feats + (h + 1) * size, :end]
            v = sorted_ref[2 * feats + h * size : 2 * feats + (h + 1) * size, :end]
            scores = causal(dot(k, q, 0, 0) * 0.125, block, -1e30)
            top = jnp.max(scores, axis=0, keepdims=True)
            weights = jnp.exp(scores - top)
            total = jnp.sum(weights, axis=0, keepdims=True)
            mixed = dot(v, weights.astype(BF), 1, 0) / total
            out_ref[h * size : (h + 1) * size, start:end] = mixed.astype(BF)
            lse_ref[h : h + 1, start:end] = top + jnp.log(total)

    def give(c, half, place):
        mixed_ref[c, :, half * span : (half + 1) * span] = out_ref[:, pl.ds(place, span)]

    move_spans(order_ref, ctx, span, give)


def attn_bwd_kernel(
    order_ref, dout_ref, sorted_ref, out_ref, lse_ref, grad_ref, dsort, gsort, gk, gv, *, heads, size, block
):
    ctx, _, rows = dout_ref.shape
    span = rows // 2
    feats = heads * size
    seq = ctx * rows

    def bring(c, half, place):
        dsort[:, pl.ds(place, span)] = dout_ref[c, :, half * span : (half + 1) * span]

    move_spans(order_ref, ctx, span, bring)
    for h in range(heads):
        own = slice(h * size, (h + 1) * size)
        gk[...] = jnp.zeros_like(gk)
        gv[...] = jnp.zeros_like(gv)
        for start in range(0, seq, block):
            end = start + block
            q = sorted_ref[own, start:end]
            k = sorted_ref[feats + h * size : feats + (h + 1) * size, :end]
            v = sorted_ref[2 * feats + h * size : 2 * feats + (h + 1) * size, :end]
            dout = dsort[own, start:end]
            delta = jnp.sum(
                dout.astype(F32) * out_ref[own, start:end].astype(F32), axis=0, keepdims=True
            )
            scores = dot(k, q, 0, 0) * 0.125 - lse_ref[h : h + 1, start:end]
            probs = jnp.exp(causal(scores, block, -1e30))
            dprobs = dot(v, dout, 0, 0)
            dscores = (probs * (dprobs - delta)).astype(BF)
            gsort[own, start:end] = (dot(k, dscores, 1, 0) * 0.125).astype(BF)
            gk[:, :end] += dot(q, dscores, 1, 1)
            gv[:, :end] += dot(dout, probs.astype(BF), 1, 1)
        gsort[feats + h * size : feats + (h + 1) * size, :] = (gk[...] * 0.125).astype(BF)
        gsort[2 * feats + h * size : 2 * feats + (h + 1) * size, :] = gv[...].astype(BF)

    def give(c, half, place):
        grad_ref[c, :, half * span : (half + 1) * span] = gsort[:, pl.ds(place, span)]

    move_spans(order_ref, ctx, span, give)


VMEM = pl.BlockSpec(memory_space=pltpu.VMEM)
SMEM = pl.BlockSpec(memory_space=pltpu.SMEM)
PARAMS = pltpu.CompilerParams(vmem_limit_bytes=48 * 1024 * 1024)


def widen(received, span_order):
    ctx, feats, rows = received.shape
    span = rows // 2
    holder = jnp.concatenate([span_order, 2 * ctx - 1 - span_order])
    source = jnp.concatenate([2 * jnp.arange(ctx), 2 * jnp.arange(ctx) + 1])
    place = jnp.zeros((2 * ctx,), jnp.int32).at[holder].set(source.astype(jnp.int32))
    flat = received.reshape(ctx, feats, 2, span).transpose(1, 0, 2, 3).reshape(feats, 2 * ctx, span)
    return jnp.take(flat, place, axis=1).reshape(1, feats, ctx * rows)


def narrow(wide, span_order, ctx):
    feats, seq = wide.shape[1:]
    span = seq // (2 * ctx)
    holder = jnp.stack([span_order, 2 * ctx - 1 - span_order], axis=1).reshape(-1)
    flat = jnp.take(wide.reshape(feats, 2 * ctx, span), holder, axis=1)
    return flat.reshape(feats, ctx, 2 * span).transpose(1, 0, 2)


def attention_forward(received, span_order, heads, size):
    ctx, _, rows = received.shape
    seq = ctx * rows
    narrow_spans = (rows // 2) % LANES != 0
    order = span_order
    if narrow_spans:
        received, order = widen(received, span_order), jnp.zeros((1,), jnp.int32)
    block = min(256, seq // 2)
    mixed, kept, out, lse = pl.pallas_call(
        functools.partial(attn_fwd_kernel, heads=heads, size=size, block=block),
        in_specs=[SMEM, VMEM],
        out_specs=[VMEM] * 4,
        out_shape=[
            jax.ShapeDtypeStruct((received.shape[0], heads * size, received.shape[2]), BF),
            jax.ShapeDtypeStruct((3 * heads * size, seq), BF),
            jax.ShapeDtypeStruct((heads * size, seq), BF),
            jax.ShapeDtypeStruct((8 * pl.cdiv(heads, 8), seq), F32),
        ],
        compiler_params=PARAMS,
        name="attn_fwd",
    )(order, received)
    if narrow_spans:
        mixed = narrow(mixed, span_order, ctx)
    return mixed, (kept, out, lse)


def attention_backward(dout, saved, span_order, heads, size):
    ctx, _, rows = dout.shape
    seq = ctx * rows
    kept, out, lse = saved
    narrow_spans = (rows // 2) % LANES != 0
    order = span_order
    if narrow_spans:
        dout, order = widen(dout, span_order), jnp.zeros((1,), jnp.int32)
    block = min(256, seq // 2)
    grad = pl.pallas_call(
        functools.partial(attn_bwd_kernel, heads=heads, size=size, block=block),
        in_specs=[SMEM, VMEM, VMEM, VMEM, VMEM],
        out_specs=VMEM,
        out_shape=jax.ShapeDtypeStruct((dout.shape[0], 3 * heads * size, dout.shape[2]), BF),
        scratch_shapes=[
            pltpu.VMEM((heads * size, seq), BF),
            pltpu.VMEM((3 * heads * size, seq), BF),
            pltpu.VMEM((size, seq), F32),
            pltpu.VMEM((size, seq), F32),
        ],
        compiler_params=PARAMS,
        name="attn_bwd",
    )(order, dout, kept, out, lse)
    if narrow_spans:
        grad = narrow(grad, span_order, ctx)
    return grad


def exchange(value):
    return lax.all_to_all(value, "ctx", split_axis=0, concat_axis=0, tiled=True)


def to_heads(value, blocks, ctx):
    rows = value.shape[1]
    size = value.shape[0] // (blocks * HEADS)
    held = pl.cdiv(HEADS, ctx)
    value = value.reshape(blocks, HEADS, size, rows)
    if held * ctx != HEADS:
        value = jnp.pad(value, ((0, 0), (0, held * ctx - HEADS), (0, 0), (0, 0)))
    value = value.reshape(blocks, ctx, held * size, rows).transpose(1, 0, 2, 3)
    return value.reshape(ctx, blocks * held * size, rows)


def from_heads(value, blocks, size):
    ctx, _, rows = value.shape
    held = pl.cdiv(HEADS, ctx)
    value = value.reshape(ctx, blocks, held * size, rows).transpose(1, 0, 2, 3)
    value = value.reshape(blocks, ctx * held, size, rows)[:, :HEADS]
    return value.reshape(blocks * HEADS * size, rows)


def normalised(values):
    centred = values - jnp.mean(values, axis=-1, keepdims=True)
    scale = lax.rsqrt(jnp.mean(centred * centred, axis=-1, keepdims=True) + EPS)
    return centred * scale, scale


def norm_back(unit, scale, upstream, gain):
    w = upstream * gain
    return (
        w - jnp.mean(w, axis=-1, keepdims=True) - unit * jnp.mean(w * unit, axis=-1, keepdims=True)
    ) * scale


def layer_forward(x, weights, vectors, span_order, ctx):
    w_qkv, w_out, w_up, w_down = weights
    gains, shifts, hidden_bias = vectors
    width = x.shape[1]
    size = width // HEADS
    held = pl.cdiv(HEADS, ctx)
    unit, scale = normalised(x)
    normed = (unit * gains[0] + shifts[0]).astype(BF)
    qkv_bias = jnp.concatenate([shifts[1], jnp.zeros_like(shifts[1]), shifts[2]])
    projected = (dot(w_qkv, normed, 0, 1) + qkv_bias[:, None]).astype(BF)
    received = exchange(to_heads(projected, 3, ctx))
    mixed, attn_saved = attention_forward(received, span_order, held, size)
    mixed = from_heads(exchange(mixed), 1, size)
    inner = x + dot(mixed, w_out, 0, 0) + shifts[3]
    unit2, scale2 = normalised(inner)
    middle = (unit2 * gains[1] + shifts[4]).astype(BF)
    hidden = dot(middle, w_up, 1, 0) + hidden_bias
    activated = (0.5 * hidden * (1.0 + jnp.tanh(GELU_C * (hidden + GELU_A * hidden**3)))).astype(BF)
    result = (inner + dot(activated, w_down, 1, 0) + shifts[5]).astype(BF)
    return result, (x, normed, attn_saved, mixed, inner, middle, hidden, activated)


def layer_backward(saved, grad_y, weights, vectors, span_order, ctx):
    x, normed, attn_saved, mixed, inner, middle, hidden, activated = saved
    w_qkv, w_out, w_up, w_down = weights
    gains, shifts, hidden_bias = vectors
    size = x.shape[1] // HEADS
    held = pl.cdiv(HEADS, ctx)
    grad_low = grad_y.astype(BF)
    grad_act = dot(grad_low, w_down, 1, 1)
    th = jnp.tanh(GELU_C * (hidden + GELU_A * hidden**3))
    slope = 0.5 * (1.0 + th) + 0.5 * hidden * (1.0 - th * th) * GELU_C * (
        1.0 + 3.0 * GELU_A * hidden * hidden
    )
    grad_hid = (grad_act * slope).astype(BF)
    up_mid = dot(grad_hid, w_up, 1, 1)
    unit2, scale2 = normalised(inner)
    grad_inner = grad_y + norm_back(unit2, scale2, up_mid, gains[1])
    grad_attn = grad_inner.astype(BF)
    grad_mixed = dot(w_out, grad_attn, 1, 1).astype(BF)
    dout = exchange(to_heads(grad_mixed, 1, ctx))
    grad_up = dot(middle, grad_hid, 0, 0)
    grad_down = dot(activated, grad_low, 0, 0)
    grad_out = dot(mixed, grad_attn, 1, 0)
    grad = exchange(attention_backward(dout, attn_saved, span_order, held, size))
    grad_qkv = from_heads(grad, 3, size)
    up_norm = dot(grad_qkv, w_qkv, 0, 1)
    unit, scale = normalised(x)
    grad_x = grad_inner + norm_back(unit, scale, up_norm, gains[0])
    grad_w_qkv = dot(normed, grad_qkv, 0, 1)
    width = x.shape[1]
    row_sums = jnp.sum(grad_qkv.astype(F32), axis=1)
    small = jnp.stack(
        [
            jnp.sum(up_norm * unit, axis=0),
            jnp.sum(up_mid * unit2, axis=0),
            jnp.sum(up_norm, axis=0),
            row_sums[:width],
            row_sums[2 * width :],
            jnp.sum(grad_attn.astype(F32), axis=0),
            jnp.sum(up_mid, axis=0),
            jnp.sum(grad_low.astype(F32), axis=0),
        ]
    )
    small_hidden = jnp.sum(grad_hid.astype(F32), axis=0)
    return grad_x, (grad_w_qkv, grad_out, grad_up, grad_down, small, small_hidden)


def columns_of_rows(value, parts):
    depth = value.shape[0] // parts
    return jnp.concatenate([value[i * depth : (i + 1) * depth] for i in range(parts)], axis=1)


def rows_of_columns(value, parts):
    width = value.shape[1] // parts
    return jnp.concatenate([value[:, i * width : (i + 1) * width] for i in range(parts)], axis=0)


def gather_weights(w_qkv, w_out, w_up, w_down, norm_gains, bias_rows, bias_hidden):
    axes = ("section", "fsdp")
    depth = w_qkv.shape[1]
    ratio = bias_hidden.shape[1] // depth
    small = jnp.concatenate([norm_gains[0], bias_rows[0], bias_hidden[0].reshape(ratio, depth)]).T
    small = jnp.pad(small, ((0, 0), (0, LANES - small.shape[1])))
    first = lax.all_gather(jnp.concatenate([w_qkv[0], small], axis=1), axes)
    second = lax.all_gather(jnp.concatenate([w_out[0], w_up[0]], axis=1), axes)
    third = lax.all_gather(w_down[0], axes)
    layers = w_qkv.shape[0] * lax.axis_size("section")
    fsdp = lax.axis_size("fsdp")
    width = depth * fsdp
    wide = w_qkv.shape[2]
    first = first.reshape(layers, width, -1)
    second = second.reshape(layers, width, -1)
    third = third.reshape(layers, -1, width)
    weights, vectors = [], []
    for s in range(layers):
        weights.append(
            (first[s, :, :wide], second[s, :, :width], second[s, :, width:], third[s])
        )
        table = first[s, :, wide:].T.astype(F32)
        gain_count, shift_count = norm_gains.shape[1], bias_rows.shape[1]
        hidden = table[gain_count + shift_count : gain_count + shift_count + ratio]
        hidden = hidden.reshape(ratio, fsdp, depth).transpose(1, 0, 2).reshape(-1)
        vectors.append(
            (table[:gain_count], table[gain_count : gain_count + shift_count], hidden)
        )
    return weights, vectors


def half(value, core):
    width = value.shape[-1] // 2
    return jnp.where(core == 0, value[..., :width], value[..., width:])


def reduce_pack(pack, small, core):
    kept, sent = half(pack, core), half(pack, 1 - core)
    if small is not None:
        kept = jnp.concatenate([kept, small], axis=1)
        sent = jnp.concatenate([sent, small], axis=1)
    total = kept + swap_cores(sent.astype(BF)).astype(F32)
    part = lax.psum_scatter(total.astype(BF), "fsdp", scatter_dimension=0, tiled=True)
    return lax.psum(part, "ctx")


def arranged_down(value, fsdp, ratio):
    full, width = value.shape
    depth = full // (fsdp * ratio)
    value = value.reshape(fsdp, ratio, depth, 2, width // 2).transpose(0, 2, 3, 1, 4)
    return value.reshape(fsdp * depth, ratio * width)


def body(
    tokens, cotangent, span_order, w_qkv, w_out, w_up, w_down, norm_gains, bias_rows, bias_hidden
):
    core = lax.axis_index("section")
    ctx = lax.axis_size("ctx")
    fsdp = lax.axis_size("fsdp")
    weights, vectors = gather_weights(
        w_qkv, w_out, w_up, w_down, norm_gains, bias_rows, bias_hidden
    )
    depth = w_qkv.shape[1]
    ratio = bias_hidden.shape[1] // depth
    own_tokens = jnp.where(core == 0, tokens[0, 0], tokens[1, 0]).astype(F32)
    own_cot = jnp.where(core == 0, cotangent[0, 0], cotangent[1, 0]).astype(F32)
    out0, saved0 = layer_forward(own_tokens, weights[0], vectors[0], span_order, ctx)
    out1, saved1 = layer_forward(out0.astype(F32), weights[1], vectors[1], span_order, ctx)
    other_out = swap_cores(jnp.where(core == 0, out1, out0))
    layer_outputs = jnp.where(
        core == 0, jnp.stack([out0, other_out]), jnp.stack([other_out, out1])
    )

    def reduced(grads):
        grad_w_qkv, grad_out, grad_up, grad_down, small, small_hidden = grads
        small_hidden = small_hidden.reshape(fsdp, ratio, depth).transpose(0, 2, 1)
        small = jnp.concatenate([small.T, small_hidden.reshape(fsdp * depth, ratio)], axis=1)
        count = small.shape[1]
        small = jnp.pad(small, ((0, 0), (0, LANES - count)))
        down = arranged_down(grad_down, fsdp, ratio)
        mid = down.shape[1] // 2
        up_mid = grad_up.shape[1] // 2
        early = jnp.concatenate(
            [grad_up[:, :up_mid], down[:, :mid], grad_up[:, up_mid:], down[:, mid:]], axis=1
        )
        q_mid, o_mid = grad_w_qkv.shape[1] // 2, grad_out.shape[1] // 2
        late = jnp.concatenate(
            [grad_w_qkv[:, :q_mid], grad_out[:, :o_mid], grad_w_qkv[:, q_mid:], grad_out[:, o_mid:]],
            axis=1,
        )
        return reduce_pack(early, None, core), reduce_pack(late, small, core)

    grad1, grads1 = layer_backward(saved1, own_cot, weights[1], vectors[1], span_order, ctx)
    early1, late1 = reduced(grads1)
    grad0, grads0 = layer_backward(
        saved0, grad1.astype(BF).astype(F32), weights[0], vectors[0], span_order, ctx
    )
    early0, late0 = reduced(grads0)
    other_grad = swap_cores(jnp.where(core == 0, grad1, grad0))
    input_grads = jnp.where(
        core == 0, jnp.stack([grad0, other_grad]), jnp.stack([other_grad, grad1])
    )
    own_early = jnp.where(core == 0, early0, early1)
    own_late = jnp.where(core == 0, late0, late1)
    other_early = swap_cores(jnp.where(core == 0, early1, early0))
    other_late = swap_cores(jnp.where(core == 0, late1, late0))

    def joined(own, other):
        return jnp.where(
            core == 0,
            jnp.concatenate([own, other], axis=1),
            jnp.concatenate([other, own], axis=1),
        ).astype(F32)

    up_half = w_up.shape[2] // 2
    qkv_half = w_qkv.shape[2] // 2
    out_half = w_out.shape[2] // 2
    late_half = qkv_half + out_half
    final_qkv = joined(own_late[:, :qkv_half], other_late[:, :qkv_half])
    final_out = joined(own_late[:, qkv_half:late_half], other_late[:, qkv_half:late_half])
    final_up = joined(own_early[:, :up_half], other_early[:, :up_half])
    final_down = joined(
        rows_of_columns(own_early[:, up_half:], ratio),
        rows_of_columns(other_early[:, up_half:], ratio),
    )
    table = own_late[:, late_half:].T.astype(F32)
    gain_count, shift_count = norm_gains.shape[1], bias_rows.shape[1]
    return (
        layer_outputs[None, :, None],
        input_grads[None, :, None],
        final_qkv[None],
        final_out[None],
        final_up[None],
        final_down[None],
        table[None, :gain_count],
        table[None, gain_count : gain_count + shift_count],
        table[gain_count + shift_count : gain_count + shift_count + ratio].reshape(1, -1),
    )


def solution(mesh):
    return jax.shard_map(
        body,
        mesh=mesh,
        in_specs=(
            P(None, "fsdp", "ctx", None),
            P(None, "fsdp", "ctx", None),
            P(),
            P("section", "fsdp", None),
            P("section", "fsdp", None),
            P("section", "fsdp", None),
            P("section", "fsdp", None),
            P("section", None, "fsdp"),
            P("section", None, "fsdp"),
            P("section", "fsdp"),
        ),
        out_specs=(
            P("section", None, "fsdp", "ctx", None),
            P("section", None, "fsdp", "ctx", None),
            P("section", "fsdp", None),
            P("section", "fsdp", None),
            P("section", "fsdp", None),
            P("section", "fsdp", None),
            P("section", None, "fsdp"),
            P("section", None, "fsdp"),
            P("section", "fsdp"),
        ),
        check_vma=False,
    )
```

```python
import functools

import jax
import jax.numpy as jnp
from jax import lax
from jax.experimental import pallas as pl
from jax.experimental.pallas import tpu as pltpu
from jax.sharding import PartitionSpec as P

HEADS = 12
EPS = 1e-05
GELU_C = 0.7978845608
GELU_A = 0.044715
LANES = 128
BF = jnp.bfloat16
F32 = jnp.float32
VMEM = pl.BlockSpec(memory_space=pltpu.VMEM)
SMEM = pl.BlockSpec(memory_space=pltpu.SMEM)
HBM = pl.BlockSpec(memory_space=pl.ANY)
PARAMS = pltpu.CompilerParams(vmem_limit_bytes=56 * 1024 * 1024)
GROUP = ("section", "ctx")
SHARDS = ("fsdp", "section")


def dot(a, b, ca, cb):
    return lax.dot_general(a, b, (((ca,), (cb,)), ((), ())), preferred_element_type=F32)


def shape(dims, dtype):
    return jax.ShapeDtypeStruct(dims, dtype)


def place_of(core, ctx_index):
    return core * lax.axis_size("ctx") + ctx_index


def exchange(pieces):
    ctx, cores = lax.axis_size("ctx"), lax.axis_size("section")
    half = ctx // cores
    moved = [pieces[0]]
    for d in range(1, ctx):
        pairs = []
        for base in range(cores):
            for g in range(ctx):
                t = (g + d) % ctx
                pairs.append(
                    (
                        place_of(g // half, base * half + g % half),
                        place_of(t // half, base * half + t % half),
                    )
                )
        moved.append(lax.ppermute(pieces[d], GROUP, pairs))
    return moved


def bring_rows(both, core, base):
    ctx, cores = lax.axis_size("ctx"), lax.axis_size("section")
    half = ctx // cores
    pairs = [
        (place_of(c, c * half + i), place_of(c, (1 - c) * half + i))
        for c in range(cores)
        for i in range(half)
    ]
    received = lax.ppermute(jnp.where(core == 0, both[1], both[0]), GROUP, pairs)
    own = jnp.where(core == 0, both[0], both[1])
    return jnp.where(core == base, own, received)


def return_rows(value, layer):
    ctx, cores = lax.axis_size("ctx"), lax.axis_size("section")
    half = ctx // cores
    return [
        lax.ppermute(
            value,
            GROUP,
            [(place_of(z // half, m * half + z % half), place_of(layer, z)) for z in range(ctx)],
        )
        for m in range(cores)
    ]


def normalised(values):
    centred = values - jnp.mean(values, axis=-1, keepdims=True)
    scale = lax.rsqrt(jnp.mean(centred * centred, axis=-1, keepdims=True) + EPS)
    return centred * scale, scale


def norm_back(unit, scale, upstream, gain):
    w = upstream * gain
    return (
        w - jnp.mean(w, axis=-1, keepdims=True) - unit * jnp.mean(w * unit, axis=-1, keepdims=True)
    ) * scale


def qkv_kernel(ids_ref, x_ref, vec_ref, pack_ref, *refs, parts, size):
    outs, (weight, whole, sem) = refs[:parts], refs[parts:]
    width = x_ref.shape[1]
    copy = pltpu.make_async_copy(pack_ref.at[:, : 3 * width], weight, sem.at[0])
    copy.start()
    unit, _ = normalised(x_ref[...].astype(F32))
    normed = (unit * vec_ref[0:1] + vec_ref[2:3]).astype(BF)
    copy.wait()
    held = outs[0].shape[0] // 3
    if parts * held != width:
        whole[...] = jnp.zeros_like(whole)
    for b in range(3):
        block = dot(normed, weight[:, b * width : (b + 1) * width], 1, 0)
        if b == 0:
            block = block + vec_ref[3:4]
        if b == 2:
            block = block + vec_ref[4:5]
        whole[b * parts * held : b * parts * held + width] = block.T.astype(BF)
    for d in range(parts):
        for b in range(3):
            first = pl.multiple_of(b * parts * held + ids_ref[d] * held, size)
            outs[d][b * held : (b + 1) * held] = whole[pl.ds(first, held)]


def qkv_project(ids, x, vec, pack, parts, size):
    rows, width = x.shape
    held = pl.cdiv(HEADS, parts) * size
    return pl.pallas_call(
        functools.partial(qkv_kernel, parts=parts, size=size),
        in_specs=[SMEM, VMEM, VMEM, HBM],
        out_specs=[VMEM] * parts,
        out_shape=[shape((3 * held, rows), BF)] * parts,
        scratch_shapes=[
            pltpu.VMEM((width, 3 * width), BF),
            pltpu.VMEM((3 * parts * held, rows), BF),
            pltpu.SemaphoreType.DMA((1,)),
        ],
        compiler_params=PARAMS,
        name="qkv_project",
    )(ids, x, vec, pack)


def spans_of(order_ref, which, count, span):
    first = order_ref[which]
    return (
        (0, pl.multiple_of(first * span, span)),
        (1, pl.multiple_of((2 * count - 1 - first) * span, span)),
    )


def causal(scores, width, fill):
    depth = scores.shape[0]
    keys = lax.broadcasted_iota(jnp.int32, (width, width), 0)
    rows = lax.broadcasted_iota(jnp.int32, (width, width), 1)
    last = jnp.where(keys <= rows, scores[depth - width :], fill)
    if depth == width:
        return last
    return jnp.concatenate([scores[: depth - width], last], axis=0)


def sort_in(order_ref, pieces, target):
    count = len(pieces)
    span = pieces[0].shape[1] // 2
    for d in range(count):
        for side, place in spans_of(order_ref, d, count, span):
            target[:, pl.ds(place, span)] = pieces[d][:, side * span : (side + 1) * span]


def sort_out(order_ref, source, pieces):
    count = len(pieces)
    span = pieces[0].shape[1] // 2
    for d in range(count):
        for side, place in spans_of(order_ref, count + d, count, span):
            pieces[d][:, side * span : (side + 1) * span] = source[:, pl.ds(place, span)]


def attn_fwd_kernel(order_ref, *refs, parts, heads, size, block):
    pieces, mixed, (sorted_ref, out_ref, lse_ref) = refs[:parts], refs[parts : 2 * parts], refs[2 * parts :]
    feats = heads * size
    seq = sorted_ref.shape[1]
    sort_in(order_ref, pieces, sorted_ref)
    lse_ref[...] = jnp.zeros_like(lse_ref)
    for h in range(heads):
        for start in range(0, seq, block):
            end = start + block
            q = sorted_ref[h * size : (h + 1) * size, start:end]
            k = sorted_ref[feats + h * size : feats + (h + 1) * size, :end]
            v = sorted_ref[2 * feats + h * size : 2 * feats + (h + 1) * size, :end]
            scores = causal(dot(k, q, 0, 0) * 0.125, block, -1e30)
            top = jnp.max(scores, axis=0, keepdims=True)
            weights = jnp.exp(scores - top)
            total = jnp.sum(weights, axis=0, keepdims=True)
            mixed_part = dot(v, weights.astype(BF), 1, 0) / total
            out_ref[h * size : (h + 1) * size, start:end] = mixed_part.astype(BF)
            lse_ref[h : h + 1, start:end] = top + jnp.log(total)
    sort_out(order_ref, out_ref, mixed)


def attn_bwd_kernel(order_ref, *refs, parts, heads, size, block):
    pieces, (sorted_ref, out_ref, lse_ref) = refs[:parts], refs[parts : parts + 3]
    grads, (dsort, gsort, gk, gv) = refs[parts + 3 : 2 * parts + 3], refs[2 * parts + 3 :]
    feats = heads * size
    seq = sorted_ref.shape[1]
    sort_in(order_ref, pieces, dsort)
    for h in range(heads):
        own = slice(h * size, (h + 1) * size)
        gk[...] = jnp.zeros_like(gk)
        gv[...] = jnp.zeros_like(gv)
        for start in range(0, seq, block):
            end = start + block
            q = sorted_ref[own, start:end]
            k = sorted_ref[feats + h * size : feats + (h + 1) * size, :end]
            v = sorted_ref[2 * feats + h * size : 2 * feats + (h + 1) * size, :end]
            dout = dsort[own, start:end]
            delta = jnp.sum(
                dout.astype(F32) * out_ref[own, start:end].astype(F32), axis=0, keepdims=True
            )
            scores = dot(k, q, 0, 0) * 0.125 - lse_ref[h : h + 1, start:end]
            probs = jnp.exp(causal(scores, block, -1e30))
            dprobs = dot(v, dout, 0, 0)
            dscores = (probs * (dprobs - delta)).astype(BF)
            gsort[own, start:end] = (dot(k, dscores, 1, 0) * 0.125).astype(BF)
            gk[:, :end] += dot(q, dscores, 1, 1)
            gv[:, :end] += dot(dout, probs.astype(BF), 1, 1)
        gsort[feats + h * size : feats + (h + 1) * size, :] = (gk[...] * 0.125).astype(BF)
        gsort[2 * feats + h * size : 2 * feats + (h + 1) * size, :] = gv[...].astype(BF)
    sort_out(order_ref, gsort, grads)


def widen(pieces, order):
    count = len(pieces)
    span = pieces[0].shape[1] // 2
    came = order[:count]
    holder = jnp.stack([came, 2 * count - 1 - came], axis=1).reshape(-1)
    place = jnp.argsort(holder)
    flat = jnp.concatenate(pieces, axis=1).reshape(-1, 2 * count, span)
    return [jnp.take(flat, place, axis=1).reshape(flat.shape[0], -1)]


def narrow(wide, order, count):
    feats, seq = wide.shape
    span = seq // (2 * count)
    goes = order[count:]
    holder = jnp.stack([goes, 2 * count - 1 - goes], axis=1).reshape(-1)
    flat = jnp.take(wide.reshape(feats, 2 * count, span), holder, axis=1)
    flat = flat.reshape(feats, count, 2 * span)
    return [flat[:, d] for d in range(count)]


def attention_forward(pieces, order, size):
    parts, rows = len(pieces), pieces[0].shape[1]
    seq = parts * rows
    heads = pieces[0].shape[0] // (3 * size)
    narrow_spans = (rows // 2) % LANES != 0
    ids, given = order, parts
    if narrow_spans:
        pieces, ids, given = widen(pieces, order), jnp.zeros((2,), jnp.int32), 1
    results = pl.pallas_call(
        functools.partial(
            attn_fwd_kernel, parts=given, heads=heads, size=size, block=min(256, seq // 2)
        ),
        in_specs=[SMEM] + [VMEM] * given,
        out_specs=[VMEM] * (given + 3),
        out_shape=[shape((heads * size, pieces[0].shape[1]), BF)] * given
        + [
            shape((3 * heads * size, seq), BF),
            shape((heads * size, seq), BF),
            shape((8 * pl.cdiv(heads, 8), seq), F32),
        ],
        compiler_params=PARAMS,
        name="attn_fwd",
    )(ids, *pieces)
    mixed = results[:given]
    if narrow_spans:
        mixed = narrow(mixed[0], order, parts)
    return mixed, tuple(results[given:])


def attention_backward(pieces, saved, order, size):
    parts, rows = len(pieces), pieces[0].shape[1]
    seq = parts * rows
    heads = pieces[0].shape[0] // size
    narrow_spans = (rows // 2) % LANES != 0
    ids, given = order, parts
    if narrow_spans:
        pieces, ids, given = widen(pieces, order), jnp.zeros((2,), jnp.int32), 1
    grads = pl.pallas_call(
        functools.partial(
            attn_bwd_kernel, parts=given, heads=heads, size=size, block=min(256, seq // 2)
        ),
        in_specs=[SMEM] + [VMEM] * (given + 3),
        out_specs=[VMEM] * given,
        out_shape=[shape((3 * heads * size, pieces[0].shape[1]), BF)] * given,
        scratch_shapes=[
            pltpu.VMEM((heads * size, seq), BF),
            pltpu.VMEM((3 * heads * size, seq), BF),
            pltpu.VMEM((size, seq), F32),
            pltpu.VMEM((size, seq), F32),
        ],
        compiler_params=PARAMS,
        name="attn_bwd",
    )(ids, *pieces, *saved)
    if narrow_spans:
        grads = narrow(grads[0], order, parts)
    return grads


def down_blocks(shards, ratio, depth):
    width = shards * depth
    for f in range(shards):
        for j in range(ratio):
            first = (f * ratio + j) * depth
            yield slice(first, first + depth), slice(f * depth, (f + 1) * depth), j * width


def rest_copies(pack, w_out, w_up, w_down, sems, shards, ratio):
    width = w_out.shape[0]
    depth = width // shards
    hidden = w_up.shape[1]
    out = [pltpu.make_async_copy(pack.at[:, :width], w_out, sems.at[0])]
    up = [pltpu.make_async_copy(pack.at[:, width : width + hidden], w_up, sems.at[1])]
    down = []
    for i, (rows, packed, column) in enumerate(down_blocks(shards, ratio, depth)):
        start = width + hidden + column
        down.append(
            pltpu.make_async_copy(
                pack.at[packed, start : start + width], w_down.at[rows], sems.at[2 + i]
            )
        )
    return out, up, down


def put_pieces(ids_ref, first, pieces, target):
    held = pieces[0].shape[0]
    for d, piece in enumerate(pieces):
        place = pl.multiple_of(ids_ref[first + d] * held, held)
        target[pl.ds(place, held)] = piece[...]


def mlp_kernel(ids_ref, x_ref, vec_ref, bias_ref, pack_ref, *refs, parts, shards, ratio):
    pieces = refs[:parts]
    result_ref, inner_ref, hidden_ref, mixed_ref = refs[parts : parts + 4]
    w_out, w_up, w_down, whole, sems = refs[parts + 4 :]
    width = x_ref.shape[1]
    out, up, down = rest_copies(pack_ref, w_out, w_up, w_down, sems, shards, ratio)
    for copy in out + up + down:
        copy.start()
    put_pieces(ids_ref, parts, pieces, whole)
    mixed_ref[...] = whole[:width]
    out[0].wait()
    inner = x_ref[...].astype(F32) + dot(whole[:width], w_out[...], 0, 0) + vec_ref[5:6]
    inner_ref[...] = inner
    unit, _ = normalised(inner)
    middle = (unit * vec_ref[1:2] + vec_ref[6:7]).astype(BF)
    up[0].wait()
    for copy in down:
        copy.wait()
    total = inner + vec_ref[7:8]
    for start in range(0, w_up.shape[1], width):
        cols = slice(start, start + width)
        hidden = dot(middle, w_up[:, cols], 1, 0) + bias_ref[:, cols]
        hidden_ref[:, cols] = hidden
        act = 0.5 * hidden * (1.0 + jnp.tanh(GELU_C * (hidden + GELU_A * hidden * hidden * hidden)))
        total = total + dot(act.astype(BF), w_down[cols], 1, 0)
    result_ref[...] = total.astype(BF)


def rest_scratch(width, hidden, shards, ratio):
    return [
        pltpu.VMEM((width, width), BF),
        pltpu.VMEM((width, hidden), BF),
        pltpu.VMEM((hidden, width), BF),
    ]


def mlp_forward(ids, x, vec, bias, pack, pieces, shards, ratio):
    parts = len(pieces)
    rows, width = x.shape
    hidden = ratio * width
    return pl.pallas_call(
        functools.partial(mlp_kernel, parts=parts, shards=shards, ratio=ratio),
        in_specs=[SMEM, VMEM, VMEM, VMEM, HBM] + [VMEM] * parts,
        out_specs=[VMEM] * 4,
        out_shape=[
            shape((rows, width), BF),
            shape((rows, width), F32),
            shape((rows, hidden), F32),
            shape((width, rows), BF),
        ],
        scratch_shapes=rest_scratch(width, hidden, shards, ratio)
        + [
            pltpu.VMEM((parts * pieces[0].shape[0], rows), BF),
            pltpu.SemaphoreType.DMA((2 + shards * ratio,)),
        ],
        compiler_params=PARAMS,
        name="mlp_forward",
    )(ids, x, vec, bias, pack, *pieces)


def mlp_back_kernel(
    ids_ref, grad_ref, inner_ref, hidden_ref, vec_ref, pack_ref, *refs, parts, shards, ratio
):
    outs = refs[:parts]
    ginner_ref, gattn_ref, ghid_ref, act_ref, middle_ref, small_ref, sbias_ref = refs[
        parts : parts + 7
    ]
    w_out, w_up, w_down, whole, sems = refs[parts + 7 :]
    width = grad_ref.shape[1]
    out, up, down = rest_copies(pack_ref, w_out, w_up, w_down, sems, shards, ratio)
    for copy in down + up + out:
        copy.start()
    grad_low = grad_ref[...].astype(BF)
    unit, scale = normalised(inner_ref[...])
    middle_ref[...] = (unit * vec_ref[1:2] + vec_ref[6:7]).astype(BF)
    for copy in down:
        copy.wait()
    up[0].wait()
    up_mid = jnp.zeros(unit.shape, F32)
    for start in range(0, w_up.shape[1], width):
        cols = slice(start, start + width)
        hidden = hidden_ref[:, cols]
        th = jnp.tanh(GELU_C * (hidden + GELU_A * hidden * hidden * hidden))
        act_ref[:, cols] = (0.5 * hidden * (1.0 + th)).astype(BF)
        slope = 0.5 * (1.0 + th) + 0.5 * hidden * (1.0 - th * th) * GELU_C * (
            1.0 + 3.0 * GELU_A * hidden * hidden
        )
        grad_hid = (dot(grad_low, w_down[cols], 1, 1) * slope).astype(BF)
        ghid_ref[:, cols] = grad_hid
        sbias_ref[:, cols] = jnp.sum(grad_hid.astype(F32), axis=0, keepdims=True)
        up_mid = up_mid + dot(grad_hid, w_up[:, cols], 1, 1)
    grad_inner = grad_ref[...].astype(F32) + norm_back(unit, scale, up_mid, vec_ref[1:2])
    ginner_ref[...] = grad_inner
    grad_attn = grad_inner.astype(BF)
    gattn_ref[...] = grad_attn
    out[0].wait()
    held = outs[0].shape[0]
    if parts * held != width:
        whole[...] = jnp.zeros_like(whole)
    whole[:width] = dot(w_out[...], grad_attn, 1, 1).astype(BF)
    for d in range(parts):
        outs[d][...] = whole[pl.ds(pl.multiple_of(ids_ref[d] * held, held), held)]
    small_ref[...] = jnp.concatenate(
        [
            jnp.sum(up_mid * unit, axis=0, keepdims=True),
            jnp.sum(grad_attn.astype(F32), axis=0, keepdims=True),
            jnp.sum(up_mid, axis=0, keepdims=True),
            jnp.sum(grad_low.astype(F32), axis=0, keepdims=True),
            jnp.zeros((4, width), F32),
        ],
        axis=0,
    )


def mlp_backward(ids, grad, inner, hidden, vec, pack, parts, size, shards, ratio):
    rows, width = inner.shape
    held = pl.cdiv(HEADS, parts) * size
    wide = ratio * width
    results = pl.pallas_call(
        functools.partial(mlp_back_kernel, parts=parts, shards=shards, ratio=ratio),
        in_specs=[SMEM, VMEM, VMEM, VMEM, VMEM, HBM],
        out_specs=[VMEM] * (parts + 7),
        out_shape=[shape((held, rows), BF)] * parts
        + [
            shape((rows, width), F32),
            shape((rows, width), BF),
            shape((rows, wide), BF),
            shape((rows, wide), BF),
            shape((rows, width), BF),
            shape((8, width), F32),
            shape((1, wide), F32),
        ],
        scratch_shapes=rest_scratch(width, wide, shards, ratio)
        + [
            pltpu.VMEM((parts * held, rows), BF),
            pltpu.SemaphoreType.DMA((2 + shards * ratio,)),
        ],
        compiler_params=PARAMS,
        name="mlp_backward",
    )(ids, grad, inner, hidden, vec, pack)
    return results[:parts], results[parts:]


def early_kernel(
    middle_ref, ghid_ref, act_ref, glow_ref, mixed_ref, gattn_ref, pack_ref, scratch, sems, *, shards, ratio
):
    width = middle_ref.shape[1]
    depth = width // shards
    hidden = ratio * width
    copies = []
    glow = glow_ref[...].astype(BF)

    def send(columns, i):
        copy = pltpu.make_async_copy(scratch.at[:, columns], pack_ref.at[:, columns], sems.at[i])
        copy.start()
        copies.append(copy)

    scratch[:, :width] = dot(mixed_ref[...], gattn_ref[...], 1, 0).astype(BF)
    send(slice(0, width), 0)
    for i in range(ratio):
        cols = slice(i * width, (i + 1) * width)
        block = dot(middle_ref[...], ghid_ref[:, cols], 0, 0).astype(BF)
        scratch[:, (i + 1) * width : (i + 2) * width] = block
        send(slice((i + 1) * width, (i + 2) * width), 1 + i)
    for f in range(shards):
        block = dot(act_ref[:, f * ratio * depth : (f + 1) * ratio * depth], glow, 0, 0).astype(BF)
        for j in range(ratio):
            start = width + hidden + j * width
            scratch[f * depth : (f + 1) * depth, start : start + width] = block[
                j * depth : (j + 1) * depth
            ]
    send(slice(width + hidden, width + 2 * hidden), 1 + ratio)
    for copy in copies:
        copy.wait()


def early_grads(middle, ghid, act, glow, mixed, gattn, shards, ratio):
    width = middle.shape[1]
    total = width * (1 + 2 * ratio)
    return pl.pallas_call(
        functools.partial(early_kernel, shards=shards, ratio=ratio),
        in_specs=[VMEM] * 6,
        out_specs=HBM,
        out_shape=shape((width, total), BF),
        scratch_shapes=[
            pltpu.VMEM((width, total), BF),
            pltpu.SemaphoreType.DMA((2 + ratio,)),
        ],
        compiler_params=PARAMS,
        name="early_grads",
    )(middle, ghid, act, glow, mixed, gattn)


def qkv_back_kernel(
    ids_ref, x_ref, ginner_ref, vec_ref, pack_ref, *refs, parts
):
    pieces = refs[:parts]
    gx_ref, small_ref, whole_ref = refs[parts : parts + 3]
    weight, whole, sem = refs[parts + 3 :]
    width = x_ref.shape[1]
    copy = pltpu.make_async_copy(pack_ref.at[:, : 3 * width], weight, sem.at[0])
    copy.start()
    held = pieces[0].shape[0] // 3
    for d, piece in enumerate(pieces):
        for b in range(3):
            place = pl.multiple_of(b * parts * held + ids_ref[parts + d] * held, held)
            whole[pl.ds(place, held)] = piece[b * held : (b + 1) * held]
    for b in range(3):
        whole_ref[b * width : (b + 1) * width] = whole[b * parts * held : b * parts * held + width]
    unit, scale = normalised(x_ref[...].astype(F32))
    copy.wait()
    up_norm = dot(weight[...], whole_ref[...], 1, 0).T
    gx_ref[...] = ginner_ref[...] + norm_back(unit, scale, up_norm, vec_ref[0:1])
    small_ref[...] = jnp.concatenate(
        [
            jnp.sum(up_norm * unit, axis=0, keepdims=True),
            jnp.sum(up_norm, axis=0, keepdims=True),
            jnp.zeros((6, width), F32),
        ],
        axis=0,
    )


def qkv_backward(ids, x, ginner, vec, pack, pieces):
    parts = len(pieces)
    rows, width = x.shape
    return pl.pallas_call(
        functools.partial(qkv_back_kernel, parts=parts),
        in_specs=[SMEM, VMEM, VMEM, VMEM, HBM] + [VMEM] * parts,
        out_specs=[VMEM] * 3,
        out_shape=[shape((rows, width), F32), shape((8, width), F32), shape((3 * width, rows), BF)],
        scratch_shapes=[
            pltpu.VMEM((width, 3 * width), BF),
            pltpu.VMEM((parts * pieces[0].shape[0], rows), BF),
            pltpu.SemaphoreType.DMA((1,)),
        ],
        compiler_params=PARAMS,
        name="qkv_backward",
    )(ids, x, ginner, vec, pack, *pieces)


def late_kernel(x_ref, vec_ref, grad_ref, small_ref, pack_ref, scratch, sems):
    width = x_ref.shape[1]
    copies = []
    unit, _ = normalised(x_ref[...].astype(F32))
    normed = (unit * vec_ref[0:1] + vec_ref[2:3]).T.astype(BF)
    for b in range(3):
        cols = slice(b * width, (b + 1) * width)
        rows = grad_ref[cols]
        scratch[:, cols] = dot(normed, rows, 1, 1).astype(BF)
        copy = pltpu.make_async_copy(scratch.at[:, cols], pack_ref.at[:, cols], sems.at[b])
        copy.start()
        copies.append(copy)
    last = slice(3 * width, 3 * width + LANES)
    scratch[:, last] = small_ref[...].astype(BF)
    copy = pltpu.make_async_copy(scratch.at[:, last], pack_ref.at[:, last], sems.at[3])
    copy.start()
    copies.append(copy)
    for copy in copies:
        copy.wait()


def late_grads(x, vec, grad_qkv, small):
    width = x.shape[1]
    return pl.pallas_call(
        late_kernel,
        in_specs=[VMEM] * 4,
        out_specs=HBM,
        out_shape=shape((width, 3 * width + LANES), BF),
        scratch_shapes=[
            pltpu.VMEM((width, 3 * width + LANES), BF),
            pltpu.SemaphoreType.DMA((4,)),
        ],
        compiler_params=PARAMS,
        name="late_grads",
    )(x, vec, grad_qkv, small)


def layer_forward(x, packs, vec, bias, ids, order, parts, size, shards, ratio):
    sent = qkv_project(ids, x, vec, packs[0], parts, size)
    mixed, attn_saved = attention_forward(exchange(sent), order, size)
    result, inner, hidden, mixed = mlp_forward(
        ids, x, vec, bias, packs[1], exchange(mixed), shards, ratio
    )
    return result, (x, attn_saved, inner, hidden, mixed)


def layer_backward(saved, grad, packs, vec, ids, order, parts, size, shards, ratio):
    x, attn_saved, inner, hidden, mixed = saved
    width = x.shape[1]
    depth = width // shards
    sent, (ginner, gattn, ghid, act, middle, small, sbias) = mlp_backward(
        ids, grad, inner, hidden, vec, packs[1], parts, size, shards, ratio
    )
    early = early_grads(middle, ghid, act, grad, mixed, gattn, shards, ratio)
    received = exchange(sent)
    *received, early = lax.optimization_barrier((*received, early))
    reduced = lax.psum_scatter(early, SHARDS, scatter_dimension=0, tiled=True)
    sent = attention_backward(received, attn_saved, order, size)
    grad_x, small2, grad_qkv = qkv_backward(ids, x, ginner, vec, packs[0], exchange(sent))
    sums = jnp.sum(grad_qkv.reshape(3, width, -1).astype(F32), axis=2)
    table = jnp.concatenate(
        [
            jnp.stack([small2[0], small[0], small2[1], sums[0], sums[2], small[1], small[2], small[3]]),
            sbias.reshape(shards, ratio, depth).transpose(1, 0, 2).reshape(ratio, width),
        ]
    )
    table = jnp.pad(table, ((0, LANES - table.shape[0]), (0, 0))).T
    late = late_grads(x, vec, grad_qkv, table)
    return grad_x, reduced, late


def blocks_to_columns(value, parts):
    depth = value.shape[0] // parts
    return [value[i * depth : (i + 1) * depth] for i in range(parts)]


def split_layers(pack, core):
    rows = pack.shape[0] // 2
    first, second = pack[:rows], pack[rows:]
    other = lax.ppermute(jnp.where(core == 0, second, first), "section", [(0, 1), (1, 0)])
    return jnp.where(core == 0, first, other), jnp.where(core == 0, other, second)


def gather(part):
    return lax.all_gather(part, SHARDS, axis=0, tiled=True)


def sum_over_ctx(value):
    count = lax.axis_size("ctx")
    index = lax.axis_index("ctx")
    rows = value.shape[0] // count
    pieces = value.reshape(count, rows, -1)

    def turned(d):
        return [(i, (i + d) % count) for i in range(count)]

    total = lax.dynamic_index_in_dim(pieces, index, 0, keepdims=False).astype(F32)
    for d in range(1, count):
        piece = lax.dynamic_index_in_dim(pieces, (index + d) % count, 0, keepdims=False)
        total = total + lax.ppermute(piece, "ctx", turned(d)).astype(F32)
    total = total.astype(BF)
    came = [lax.ppermute(total, "ctx", turned(d)) for d in range(count - 1, 0, -1)] + [total]
    ring = jnp.stack(came + came)
    start = (2 * count - 1 - index) % count
    return lax.dynamic_slice_in_dim(ring, start, count, 0).reshape(value.shape)


def body(
    tokens, cotangent, span_order, w_qkv, w_out, w_up, w_down, norm_gains, bias_rows, bias_hidden
):
    core = lax.axis_index("section")
    ctx = lax.axis_size("ctx")
    cores = lax.axis_size("section")
    shards = lax.axis_size("fsdp")
    half = ctx // cores
    base = lax.axis_index("ctx") // half
    member = core * half + lax.axis_index("ctx") % half
    depth = w_qkv.shape[1]
    width = depth * shards
    ratio = bias_hidden.shape[1] // depth
    size = width // HEADS
    gain_count, shift_count = norm_gains.shape[1], bias_rows.shape[1]

    steps = jnp.arange(ctx, dtype=jnp.int32)
    came, goes = (member - steps) % ctx, (member + steps) % ctx
    ids = jnp.concatenate([goes, came]).astype(jnp.int32)
    order = jnp.concatenate([span_order[came], span_order[goes]])

    small = jnp.concatenate([norm_gains[0], bias_rows[0], bias_hidden[0].reshape(ratio, depth)]).T
    small = jnp.pad(small, ((0, 0), (0, LANES - small.shape[1])))
    first = jnp.concatenate([w_qkv[0], small], axis=1)
    rest = jnp.concatenate([w_out[0], w_up[0]] + blocks_to_columns(w_down[0], ratio), axis=1)
    first0, first1 = split_layers(first, core)
    x = bring_rows(tokens[:, 0], core, base)
    rest0, rest1 = split_layers(rest, core)
    packs = []
    for a, b in ((first0, rest0), (first1, rest1)):
        packs.append((gather(a), gather(b)))
    vecs, biases = [], []
    for a, _ in packs:
        table = a[:, 3 * width :].T.astype(F32)
        vecs.append(table[:16])
        hidden = table[gain_count + shift_count : gain_count + shift_count + ratio]
        biases.append(hidden.reshape(ratio, shards, depth).transpose(1, 0, 2).reshape(1, -1))

    out0, saved0 = layer_forward(
        x, packs[0], vecs[0], biases[0], ids, order, ctx, size, shards, ratio
    )
    out1, saved1 = layer_forward(
        out0, packs[1], vecs[1], biases[1], ids, order, ctx, size, shards, ratio
    )
    cot = bring_rows(cotangent[:, 0], core, base)
    grad1, early1, late1 = layer_backward(
        saved1, cot, packs[1], vecs[1], ids, order, ctx, size, shards, ratio
    )
    late1 = lax.psum_scatter(late1, SHARDS, scatter_dimension=0, tiled=True)
    grad1_low = grad1.astype(BF)
    grad0, early0, late0 = layer_backward(
        saved0, grad1_low, packs[0], vecs[0], ids, order, ctx, size, shards, ratio
    )
    late0 = lax.psum_scatter(late0, SHARDS, scatter_dimension=0, tiled=True)

    def own_layer(value0, value1):
        return [
            jnp.where(core == 0, a, b)
            for a, b in zip(return_rows(value0, 0), return_rows(value1, 1))
        ]

    layer_outputs = jnp.stack(own_layer(out0, out1))
    input_grads = jnp.stack(own_layer(grad0.astype(BF), grad1_low)).astype(F32)

    def joined(part0, part1):
        part0, part1 = sum_over_ctx(part0), sum_over_ctx(part1)
        other = jnp.where(
            core == 0,
            lax.ppermute(part0, "section", [(1, 0)]),
            lax.ppermute(part1, "section", [(0, 1)]),
        )
        own = jnp.where(core == 0, part0, part1)
        return jnp.where(
            core == 0, jnp.concatenate([own, other]), jnp.concatenate([other, own])
        ).astype(F32)

    early = joined(early0, early1)
    late = joined(late0, late1)
    down = early[:, width * (1 + ratio) :]
    table = late[:, 3 * width :].T
    return (
        layer_outputs[None, :, None],
        input_grads[None, :, None],
        late[None, :, : 3 * width],
        early[None, :, :width],
        early[None, :, width : width * (1 + ratio)],
        jnp.concatenate([down[:, j * width : (j + 1) * width] for j in range(ratio)])[None],
        table[None, :gain_count],
        table[None, gain_count : gain_count + shift_count],
        table[gain_count + shift_count : gain_count + shift_count + ratio].reshape(1, -1),
    )


def solution(mesh):
    return jax.shard_map(
        body,
        mesh=mesh,
        in_specs=(
            P(None, "fsdp", "ctx", None),
            P(None, "fsdp", "ctx", None),
            P(),
            P("section", "fsdp", None),
            P("section", "fsdp", None),
            P("section", "fsdp", None),
            P("section", "fsdp", None),
            P("section", None, "fsdp"),
            P("section", None, "fsdp"),
            P("section", "fsdp"),
        ),
        out_specs=(
            P("section", None, "fsdp", "ctx", None),
            P("section", None, "fsdp", "ctx", None),
            P("section", "fsdp", None),
            P("section", "fsdp", None),
            P("section", "fsdp", None),
            P("section", "fsdp", None),
            P("section", None, "fsdp"),
            P("section", None, "fsdp"),
            P("section", "fsdp"),
        ),
        check_vma=False,
    )
```

```python
import functools

import jax
import jax.numpy as jnp
from jax import lax
from jax.experimental import pallas as pl
from jax.experimental.pallas import tpu as pltpu
from jax.sharding import PartitionSpec as P

HEADS = 12
EPS = 1e-05
GELU_C = 0.7978845608
GELU_A = 0.044715
LANES = 128
BF = jnp.bfloat16
F32 = jnp.float32
VMEM = pl.BlockSpec(memory_space=pltpu.VMEM)
SMEM = pl.BlockSpec(memory_space=pltpu.SMEM)
HBM = pl.BlockSpec(memory_space=pl.ANY)
PARAMS = pltpu.CompilerParams(vmem_limit_bytes=56 * 1024 * 1024)
GROUP = ("section", "ctx")
SHARDS = ("fsdp", "section")


def dot(a, b, ca, cb):
    return lax.dot_general(a, b, (((ca,), (cb,)), ((), ())), preferred_element_type=F32)


def shape(dims, dtype):
    return jax.ShapeDtypeStruct(dims, dtype)


def place_of(core, ctx_index):
    return core * lax.axis_size("ctx") + ctx_index


def exchange(pieces):
    ctx, cores = lax.axis_size("ctx"), lax.axis_size("section")
    half = ctx // cores
    moved = [pieces[0]]
    for d in range(1, ctx):
        pairs = []
        for base in range(cores):
            for g in range(ctx):
                t = (g + d) % ctx
                pairs.append(
                    (
                        place_of(g // half, base * half + g % half),
                        place_of(t // half, base * half + t % half),
                    )
                )
        moved.append(lax.ppermute(pieces[d], GROUP, pairs))
    return moved


def bring_rows(both, core, base):
    ctx, cores = lax.axis_size("ctx"), lax.axis_size("section")
    half = ctx // cores
    pairs = [
        (place_of(c, c * half + i), place_of(c, (1 - c) * half + i))
        for c in range(cores)
        for i in range(half)
    ]
    received = lax.ppermute(jnp.where(core == 0, both[1], both[0]), GROUP, pairs)
    own = jnp.where(core == 0, both[0], both[1])
    return jnp.where(core == base, own, received)


def return_rows(value, layer):
    ctx, cores = lax.axis_size("ctx"), lax.axis_size("section")
    half = ctx // cores
    return [
        lax.ppermute(
            value,
            GROUP,
            [(place_of(z // half, m * half + z % half), place_of(layer, z)) for z in range(ctx)],
        )
        for m in range(cores)
    ]


def normalised(values):
    centred = values - jnp.mean(values, axis=-1, keepdims=True)
    scale = lax.rsqrt(jnp.mean(centred * centred, axis=-1, keepdims=True) + EPS)
    return centred * scale, scale


def norm_back(unit, scale, upstream, gain):
    w = upstream * gain
    return (
        w - jnp.mean(w, axis=-1, keepdims=True) - unit * jnp.mean(w * unit, axis=-1, keepdims=True)
    ) * scale


def piece_places(ids_ref, parts, depth, slots):
    first = 2 * parts
    rows = depth // 2
    places = []
    for side in range(2):
        core = ids_ref[first + slots + side]
        for slot, start, count in (
            (0, 0, rows),
            (1, 0, rows),
            (2, 0, rows),
            (3, 0, rows // 2),
            (3, rows // 2, rows // 2),
        ):
            place = ids_ref[first + slot] * depth + core * rows + start
            places.append((pl.multiple_of(place, 16), count))
    return places


def qkv_kernel(ids_ref, x_ref, *refs, parts, size, shards):
    packs, refs = refs[:10], refs[10:]
    outs, (weight_ref, vec_ref), refs = refs[:parts], refs[parts : parts + 2], refs[parts + 2 :]
    weight, small, whole, sems = refs
    width = x_ref.shape[1]
    copies = []
    for i, (place, count) in enumerate(piece_places(ids_ref, parts, width // shards, shards)):
        for j, target, cols in (
            (0, small, slice(3 * width, 3 * width + LANES)),
            (1, weight, slice(0, 3 * width)),
        ):
            copies.append(
                pltpu.make_async_copy(
                    packs[i].at[:, cols], target.at[pl.ds(place, count)], sems.at[2 * i + j]
                )
            )
    for copy in copies:
        copy.start()
    unit, _ = normalised(x_ref[...].astype(F32))
    for copy in copies:
        copy.wait()
    keep = pltpu.make_async_copy(weight, weight_ref, sems.at[20])
    keep.start()
    vec = small[...].astype(F32).T
    vec_ref[...] = vec[:16]
    normed = (unit * vec[0:1] + vec[2:3]).astype(BF)
    held = outs[0].shape[0] // 3
    if parts * held != width:
        whole[...] = jnp.zeros_like(whole)
    for b in range(3):
        block = dot(normed, weight[:, b * width : (b + 1) * width], 1, 0)
        if b == 0:
            block = block + vec[3:4]
        if b == 2:
            block = block + vec[4:5]
        whole[b * parts * held : b * parts * held + width] = block.T.astype(BF)
    for d in range(parts):
        for b in range(3):
            first = pl.multiple_of(b * parts * held + ids_ref[d] * held, size)
            outs[d][b * held : (b + 1) * held] = whole[pl.ds(first, held)]
    keep.wait()


def qkv_project(ids, x, packs, parts, size, shards):
    rows, width = x.shape
    held = pl.cdiv(HEADS, parts) * size
    results = pl.pallas_call(
        functools.partial(qkv_kernel, parts=parts, size=size, shards=shards),
        in_specs=[SMEM, VMEM] + [HBM] * 10,
        out_specs=[VMEM] * parts + [HBM, VMEM],
        out_shape=[shape((3 * held, rows), BF)] * parts
        + [shape((width, 3 * width), BF), shape((16, width), F32)],
        scratch_shapes=[
            pltpu.VMEM((width, 3 * width), BF),
            pltpu.VMEM((width, LANES), BF),
            pltpu.VMEM((3 * parts * held, rows), BF),
            pltpu.SemaphoreType.DMA((21,)),
        ],
        compiler_params=PARAMS,
        name="qkv_project",
    )(ids, x, *packs)
    return results[:parts], results[parts], results[parts + 1]


def spans_of(order_ref, which, count, span):
    first = order_ref[which]
    return (
        (0, pl.multiple_of(first * span, span)),
        (1, pl.multiple_of((2 * count - 1 - first) * span, span)),
    )


def causal(scores, width, fill):
    depth = scores.shape[0]
    keys = lax.broadcasted_iota(jnp.int32, (width, width), 0)
    rows = lax.broadcasted_iota(jnp.int32, (width, width), 1)
    last = jnp.where(keys <= rows, scores[depth - width :], fill)
    if depth == width:
        return last
    return jnp.concatenate([scores[: depth - width], last], axis=0)


def sort_in(order_ref, pieces, target):
    count = len(pieces)
    span = pieces[0].shape[1] // 2
    for d in range(count):
        for side, place in spans_of(order_ref, d, count, span):
            target[:, pl.ds(place, span)] = pieces[d][:, side * span : (side + 1) * span]


def sort_out(order_ref, source, pieces):
    count = len(pieces)
    span = pieces[0].shape[1] // 2
    for d in range(count):
        for side, place in spans_of(order_ref, count + d, count, span):
            pieces[d][:, side * span : (side + 1) * span] = source[:, pl.ds(place, span)]


def attn_fwd_kernel(order_ref, *refs, parts, heads, size, block):
    pieces, mixed, (sorted_ref, out_ref, lse_ref) = refs[:parts], refs[parts : 2 * parts], refs[2 * parts :]
    feats = heads * size
    seq = sorted_ref.shape[1]
    sort_in(order_ref, pieces, sorted_ref)
    lse_ref[...] = jnp.zeros_like(lse_ref)
    for h in range(heads):
        for start in range(0, seq, block):
            end = start + block
            q = sorted_ref[h * size : (h + 1) * size, start:end]
            k = sorted_ref[feats + h * size : feats + (h + 1) * size, :end]
            v = sorted_ref[2 * feats + h * size : 2 * feats + (h + 1) * size, :end]
            scores = causal(dot(k, q, 0, 0) * 0.125, block, -1e30)
            top = jnp.max(scores, axis=0, keepdims=True)
            weights = jnp.exp(scores - top)
            total = jnp.sum(weights, axis=0, keepdims=True)
            mixed_part = dot(v, weights.astype(BF), 1, 0) / total
            out_ref[h * size : (h + 1) * size, start:end] = mixed_part.astype(BF)
            lse_ref[h : h + 1, start:end] = top + jnp.log(total)
    sort_out(order_ref, out_ref, mixed)


def attn_bwd_kernel(order_ref, *refs, parts, heads, size, block):
    pieces, (sorted_ref, out_ref, lse_ref) = refs[:parts], refs[parts : parts + 3]
    grads, (dsort, gsort, gk, gv) = refs[parts + 3 : 2 * parts + 3], refs[2 * parts + 3 :]
    feats = heads * size
    seq = sorted_ref.shape[1]
    sort_in(order_ref, pieces, dsort)
    for h in range(heads):
        own = slice(h * size, (h + 1) * size)
        gk[...] = jnp.zeros_like(gk)
        gv[...] = jnp.zeros_like(gv)
        for start in range(0, seq, block):
            end = start + block
            q = sorted_ref[own, start:end]
            k = sorted_ref[feats + h * size : feats + (h + 1) * size, :end]
            v = sorted_ref[2 * feats + h * size : 2 * feats + (h + 1) * size, :end]
            dout = dsort[own, start:end]
            delta = jnp.sum(
                dout.astype(F32) * out_ref[own, start:end].astype(F32), axis=0, keepdims=True
            )
            scores = dot(k, q, 0, 0) * 0.125 - lse_ref[h : h + 1, start:end]
            probs = jnp.exp(causal(scores, block, -1e30))
            dprobs = dot(v, dout, 0, 0)
            dscores = (probs * (dprobs - delta)).astype(BF)
            gsort[own, start:end] = (dot(k, dscores, 1, 0) * 0.125).astype(BF)
            gk[:, :end] += dot(q, dscores, 1, 1)
            gv[:, :end] += dot(dout, probs.astype(BF), 1, 1)
        gsort[feats + h * size : feats + (h + 1) * size, :] = (gk[...] * 0.125).astype(BF)
        gsort[2 * feats + h * size : 2 * feats + (h + 1) * size, :] = gv[...].astype(BF)
    sort_out(order_ref, gsort, grads)


def widen(pieces, order):
    count = len(pieces)
    span = pieces[0].shape[1] // 2
    came = order[:count]
    holder = jnp.stack([came, 2 * count - 1 - came], axis=1).reshape(-1)
    place = jnp.argsort(holder)
    flat = jnp.concatenate(pieces, axis=1).reshape(-1, 2 * count, span)
    return [jnp.take(flat, place, axis=1).reshape(flat.shape[0], -1)]


def narrow(wide, order, count):
    feats, seq = wide.shape
    span = seq // (2 * count)
    goes = order[count:]
    holder = jnp.stack([goes, 2 * count - 1 - goes], axis=1).reshape(-1)
    flat = jnp.take(wide.reshape(feats, 2 * count, span), holder, axis=1)
    flat = flat.reshape(feats, count, 2 * span)
    return [flat[:, d] for d in range(count)]


def attention_forward(pieces, order, size):
    parts, rows = len(pieces), pieces[0].shape[1]
    seq = parts * rows
    heads = pieces[0].shape[0] // (3 * size)
    narrow_spans = (rows // 2) % LANES != 0
    ids, given = order, parts
    if narrow_spans:
        pieces, ids, given = widen(pieces, order), jnp.zeros((2,), jnp.int32), 1
    results = pl.pallas_call(
        functools.partial(
            attn_fwd_kernel, parts=given, heads=heads, size=size, block=min(256, seq // 2)
        ),
        in_specs=[SMEM] + [VMEM] * given,
        out_specs=[VMEM] * (given + 3),
        out_shape=[shape((heads * size, pieces[0].shape[1]), BF)] * given
        + [
            shape((3 * heads * size, seq), BF),
            shape((heads * size, seq), BF),
            shape((8 * pl.cdiv(heads, 8), seq), F32),
        ],
        compiler_params=PARAMS,
        name="attn_fwd",
    )(ids, *pieces)
    mixed = results[:given]
    if narrow_spans:
        mixed = narrow(mixed[0], order, parts)
    return mixed, tuple(results[given:])


def attention_backward(pieces, saved, order, size):
    parts, rows = len(pieces), pieces[0].shape[1]
    seq = parts * rows
    heads = pieces[0].shape[0] // size
    narrow_spans = (rows // 2) % LANES != 0
    ids, given = order, parts
    if narrow_spans:
        pieces, ids, given = widen(pieces, order), jnp.zeros((2,), jnp.int32), 1
    grads = pl.pallas_call(
        functools.partial(
            attn_bwd_kernel, parts=given, heads=heads, size=size, block=min(256, seq // 2)
        ),
        in_specs=[SMEM] + [VMEM] * (given + 3),
        out_specs=[VMEM] * given,
        out_shape=[shape((3 * heads * size, pieces[0].shape[1]), BF)] * given,
        scratch_shapes=[
            pltpu.VMEM((heads * size, seq), BF),
            pltpu.VMEM((3 * heads * size, seq), BF),
            pltpu.VMEM((size, seq), F32),
            pltpu.VMEM((size, seq), F32),
        ],
        compiler_params=PARAMS,
        name="attn_bwd",
    )(ids, *pieces, *saved)
    if narrow_spans:
        grads = narrow(grads[0], order, parts)
    return grads


def down_blocks(shards, ratio, depth):
    width = shards * depth
    for f in range(shards):
        for j in range(ratio):
            first = (f * ratio + j) * depth
            yield slice(first, first + depth), slice(f * depth, (f + 1) * depth), j * width


def rest_copies(pack, w_out, w_up, w_down, sems, shards, ratio):
    width = w_out.shape[0]
    depth = width // shards
    hidden = w_up.shape[1]
    out = [pltpu.make_async_copy(pack.at[:, :width], w_out, sems.at[0])]
    up = [pltpu.make_async_copy(pack.at[:, width : width + hidden], w_up, sems.at[1])]
    down = []
    for i, (rows, packed, column) in enumerate(down_blocks(shards, ratio, depth)):
        start = width + hidden + column
        down.append(
            pltpu.make_async_copy(
                pack.at[packed, start : start + width], w_down.at[rows], sems.at[2 + i]
            )
        )
    return out, up, down


def put_pieces(ids_ref, first, pieces, target):
    held = pieces[0].shape[0]
    for d, piece in enumerate(pieces):
        place = pl.multiple_of(ids_ref[first + d] * held, held)
        target[pl.ds(place, held)] = piece[...]


def mlp_kernel(ids_ref, x_ref, vec_ref, bias_ref, pack_ref, *refs, parts, shards, ratio):
    pieces = refs[:parts]
    result_ref, inner_ref, hidden_ref, mixed_ref = refs[parts : parts + 4]
    w_out, w_up, w_down, whole, sems = refs[parts + 4 :]
    width = x_ref.shape[1]
    out, up, down = rest_copies(pack_ref, w_out, w_up, w_down, sems, shards, ratio)
    for copy in out + up + down:
        copy.start()
    put_pieces(ids_ref, parts, pieces, whole)
    mixed_ref[...] = whole[:width]
    out[0].wait()
    inner = x_ref[...].astype(F32) + dot(whole[:width], w_out[...], 0, 0) + vec_ref[5:6]
    inner_ref[...] = inner
    unit, _ = normalised(inner)
    middle = (unit * vec_ref[1:2] + vec_ref[6:7]).astype(BF)
    up[0].wait()
    for copy in down:
        copy.wait()
    total = inner + vec_ref[7:8]
    for start in range(0, w_up.shape[1], width):
        cols = slice(start, start + width)
        hidden = dot(middle, w_up[:, cols], 1, 0) + bias_ref[:, cols]
        hidden_ref[:, cols] = hidden
        act = 0.5 * hidden * (1.0 + jnp.tanh(GELU_C * (hidden + GELU_A * hidden * hidden * hidden)))
        total = total + dot(act.astype(BF), w_down[cols], 1, 0)
    result_ref[...] = total.astype(BF)


def rest_scratch(width, hidden, shards, ratio):
    return [
        pltpu.VMEM((width, width), BF),
        pltpu.VMEM((width, hidden), BF),
        pltpu.VMEM((hidden, width), BF),
    ]


def mlp_forward(ids, x, vec, bias, pack, pieces, shards, ratio):
    parts = len(pieces)
    rows, width = x.shape
    hidden = ratio * width
    return pl.pallas_call(
        functools.partial(mlp_kernel, parts=parts, shards=shards, ratio=ratio),
        in_specs=[SMEM, VMEM, VMEM, VMEM, HBM] + [VMEM] * parts,
        out_specs=[VMEM] * 4,
        out_shape=[
            shape((rows, width), BF),
            shape((rows, width), F32),
            shape((rows, hidden), F32),
            shape((width, rows), BF),
        ],
        scratch_shapes=rest_scratch(width, hidden, shards, ratio)
        + [
            pltpu.VMEM((parts * pieces[0].shape[0], rows), BF),
            pltpu.SemaphoreType.DMA((2 + shards * ratio,)),
        ],
        compiler_params=PARAMS,
        name="mlp_forward",
    )(ids, x, vec, bias, pack, *pieces)


def mlp_back_kernel(
    ids_ref, grad_ref, inner_ref, hidden_ref, vec_ref, pack_ref, *refs, parts, shards, ratio
):
    outs = refs[:parts]
    ginner_ref, gattn_ref, ghid_ref, act_ref, middle_ref, table_ref = refs[parts : parts + 6]
    w_out, w_up, w_down, whole, sems = refs[parts + 6 :]
    width = grad_ref.shape[1]
    out, up, down = rest_copies(pack_ref, w_out, w_up, w_down, sems, shards, ratio)
    for copy in down + up + out:
        copy.start()
    grad_low = grad_ref[...].astype(BF)
    unit, scale = normalised(inner_ref[...])
    middle_ref[...] = (unit * vec_ref[1:2] + vec_ref[6:7]).astype(BF)
    for copy in down:
        copy.wait()
    up[0].wait()
    up_mid = jnp.zeros(unit.shape, F32)
    depth = width // shards
    table_ref[...] = jnp.zeros_like(table_ref)
    for start in range(0, w_up.shape[1], width):
        cols = slice(start, start + width)
        hidden = hidden_ref[:, cols]
        th = jnp.tanh(GELU_C * (hidden + GELU_A * hidden * hidden * hidden))
        act_ref[:, cols] = (0.5 * hidden * (1.0 + th)).astype(BF)
        slope = 0.5 * (1.0 + th) + 0.5 * hidden * (1.0 - th * th) * GELU_C * (
            1.0 + 3.0 * GELU_A * hidden * hidden
        )
        grad_hid = (dot(grad_low, w_down[cols], 1, 1) * slope).astype(BF)
        ghid_ref[:, cols] = grad_hid
        sums = jnp.sum(grad_hid.astype(F32), axis=0, keepdims=True)
        for i in range(width // depth):
            f, j = divmod(start // depth + i, ratio)
            table_ref[8 + j : 9 + j, f * depth : (f + 1) * depth] = sums[:, i * depth : (i + 1) * depth]
        up_mid = up_mid + dot(grad_hid, w_up[:, cols], 1, 1)
    grad_inner = grad_ref[...].astype(F32) + norm_back(unit, scale, up_mid, vec_ref[1:2])
    ginner_ref[...] = grad_inner
    grad_attn = grad_inner.astype(BF)
    gattn_ref[...] = grad_attn
    out[0].wait()
    held = outs[0].shape[0]
    if parts * held != width:
        whole[...] = jnp.zeros_like(whole)
    whole[:width] = dot(w_out[...], grad_attn, 1, 1).astype(BF)
    for d in range(parts):
        outs[d][...] = whole[pl.ds(pl.multiple_of(ids_ref[d] * held, held), held)]
    table_ref[1:2] = jnp.sum(up_mid * unit, axis=0, keepdims=True)
    table_ref[5:6] = jnp.sum(grad_attn.astype(F32), axis=0, keepdims=True)
    table_ref[6:7] = jnp.sum(up_mid, axis=0, keepdims=True)
    table_ref[7:8] = jnp.sum(grad_low.astype(F32), axis=0, keepdims=True)


def mlp_backward(ids, grad, inner, hidden, vec, pack, parts, size, shards, ratio):
    rows, width = inner.shape
    held = pl.cdiv(HEADS, parts) * size
    wide = ratio * width
    results = pl.pallas_call(
        functools.partial(mlp_back_kernel, parts=parts, shards=shards, ratio=ratio),
        in_specs=[SMEM, VMEM, VMEM, VMEM, VMEM, HBM],
        out_specs=[VMEM] * (parts + 6),
        out_shape=[shape((held, rows), BF)] * parts
        + [
            shape((rows, width), F32),
            shape((rows, width), BF),
            shape((rows, wide), BF),
            shape((rows, wide), BF),
            shape((rows, width), BF),
            shape((LANES, width), F32),
        ],
        scratch_shapes=rest_scratch(width, wide, shards, ratio)
        + [
            pltpu.VMEM((parts * held, rows), BF),
            pltpu.SemaphoreType.DMA((2 + shards * ratio,)),
        ],
        compiler_params=PARAMS,
        name="mlp_backward",
    )(ids, grad, inner, hidden, vec, pack)
    return results[:parts], results[parts:]


def write_down(act_ref, glow_ref, pack, start, shards, ratio):
    width = glow_ref.shape[1]
    depth = width // shards
    glow = glow_ref[...].astype(BF)
    for f in range(shards):
        block = dot(act_ref[:, f * ratio * depth : (f + 1) * ratio * depth], glow, 0, 0).astype(BF)
        for j in range(ratio):
            first = start + j * width
            pack[f * depth : (f + 1) * depth, first : first + width] = block[
                j * depth : (j + 1) * depth
            ]


def send_sides(ids_ref, first, pack, start, count, targets, sems, offset, shards):
    depth = pack.shape[0] // shards
    rows = depth // 2
    copies = []
    for side in range(2):
        core = ids_ref[first + shards + side]
        for k in range(shards):
            place = pl.multiple_of(ids_ref[first + k] * depth + core * rows, 16)
            copies.append(
                pltpu.make_async_copy(
                    pack.at[pl.ds(place, rows), start : start + count],
                    targets[side].at[k],
                    sems.at[offset + side * shards + k],
                )
            )
    for copy in copies:
        copy.start()
    return copies


def early_kernel(
    ids_ref, middle_ref, ghid_ref, mixed_ref, gattn_ref, act_ref, glow_ref, *refs, parts, shards, ratio, apart
):
    if apart:
        outs, (scratch, sems) = refs[:4], refs[4:]
    else:
        pack_ref, scratch, sems = refs
    width = middle_ref.shape[1]
    main = (1 + ratio) * width
    copies = []

    def send(columns, i):
        copy = pltpu.make_async_copy(scratch.at[:, columns], pack_ref.at[:, columns], sems.at[i])
        copy.start()
        copies.append(copy)

    scratch[:, :width] = dot(mixed_ref[...], gattn_ref[...], 1, 0).astype(BF)
    for i in range(ratio):
        cols = slice(i * width, (i + 1) * width)
        block = dot(middle_ref[...], ghid_ref[:, cols], 0, 0).astype(BF)
        scratch[:, (i + 1) * width : (i + 2) * width] = block
    if apart:
        copies += send_sides(
            ids_ref, 2 * parts, scratch, 0, main, outs[:2], sems, 0, shards
        )
    else:
        send(slice(0, main), 0)
    write_down(act_ref, glow_ref, scratch, main, shards, ratio)
    if apart:
        copies += send_sides(
            ids_ref, 2 * parts, scratch, main, ratio * width, outs[2:], sems, 2 * shards, shards
        )
    else:
        send(slice(main, main + ratio * width), 1)
    for copy in copies:
        copy.wait()


def early_grads(ids, middle, ghid, mixed, gattn, act, grad, parts, shards, ratio, apart):
    width = middle.shape[1]
    main, hidden = (1 + ratio) * width, ratio * width
    rows = width // shards // 2
    up, down = shape((shards, rows, main), BF), shape((shards, rows, hidden), BF)
    return pl.pallas_call(
        functools.partial(early_kernel, parts=parts, shards=shards, ratio=ratio, apart=apart),
        in_specs=[SMEM] + [VMEM] * 6,
        out_specs=[HBM] * (4 if apart else 1),
        out_shape=[up, up, down, down] if apart else [shape((width, main + hidden), BF)],
        scratch_shapes=[
            pltpu.VMEM((width, main + hidden), BF),
            pltpu.SemaphoreType.DMA((4 * shards,)),
        ],
        compiler_params=PARAMS,
        name="early_grads",
    )(ids, middle, ghid, mixed, gattn, act, grad)


def qkv_back_kernel(
    ids_ref, x_ref, ginner_ref, vec_ref, table_ref, weight_hbm, *refs, parts, shards
):
    pieces, refs = refs[:parts], refs[parts:]
    gx_ref, keep_ref, send_ref, weight, whole, pack, sem = refs
    width = x_ref.shape[1]
    main = 3 * width + LANES
    copies = []
    copy = pltpu.make_async_copy(weight_hbm, weight, sem.at[0])
    copy.start()
    held = pieces[0].shape[0] // 3
    padded = parts * held
    for d, piece in enumerate(pieces):
        for b in range(3):
            place = pl.multiple_of(b * padded + ids_ref[parts + d] * held, held)
            whole[pl.ds(place, held)] = piece[b * held : (b + 1) * held]
    unit, scale = normalised(x_ref[...].astype(F32))
    normed = (unit * vec_ref[0:1] + vec_ref[2:3]).T.astype(BF)
    copy.wait()
    up_norm = jnp.zeros((width, x_ref.shape[0]), F32)
    sums = []
    for b in range(3):
        grads = whole[b * padded : b * padded + width]
        cols = slice(b * width, (b + 1) * width)
        up_norm = up_norm + dot(weight[:, cols], grads, 1, 0)
        pack[:, cols] = dot(normed, grads, 1, 1).astype(BF)
        sums.append(jnp.sum(grads.astype(F32), axis=1, keepdims=True))
    up_norm = up_norm.T
    gx_ref[...] = (ginner_ref[...] + norm_back(unit, scale, up_norm, vec_ref[0:1])).astype(BF)
    line = lax.broadcasted_iota(jnp.int32, table_ref.shape, 0)
    table = jnp.where(
        line == 0,
        jnp.sum(up_norm * unit, axis=0, keepdims=True),
        jnp.where(line == 2, jnp.sum(up_norm, axis=0, keepdims=True), table_ref[...]),
    ).T
    lane = lax.broadcasted_iota(jnp.int32, table.shape, 1)
    table = jnp.where(lane == 3, sums[0], jnp.where(lane == 4, sums[2], table))
    pack[:, 3 * width : main] = table.astype(BF)
    copies += send_sides(
        ids_ref, 2 * parts, pack, 0, main, (keep_ref, send_ref), sem, 1, shards
    )
    for copy in copies:
        copy.wait()


def qkv_backward(ids, x, ginner, vec, table, weight, pieces, shards):
    parts = len(pieces)
    rows, width = x.shape
    total = 3 * width + LANES
    part = shape((shards, width // shards // 2, total), BF)
    return pl.pallas_call(
        functools.partial(qkv_back_kernel, parts=parts, shards=shards),
        in_specs=[SMEM, VMEM, VMEM, VMEM, VMEM, HBM] + [VMEM] * parts,
        out_specs=[VMEM, HBM, HBM],
        out_shape=[shape((rows, width), BF), part, part],
        scratch_shapes=[
            pltpu.VMEM((width, 3 * width), BF),
            pltpu.VMEM((parts * pieces[0].shape[0], rows), BF),
            pltpu.VMEM((width, total), BF),
            pltpu.SemaphoreType.DMA((1 + 2 * shards,)),
        ],
        compiler_params=PARAMS,
        name="qkv_backward",
    )(ids, x, ginner, vec, table, weight, *pieces)


def layer_forward(x, packs, rest, ids, order, parts, size, shards, ratio):
    sent, weight, vec = qkv_project(ids, x, packs, parts, size, shards)
    width = x.shape[1]
    depth = width // shards
    bias = vec[8 : 8 + ratio].reshape(ratio, shards, depth).transpose(1, 0, 2).reshape(1, -1)
    mixed, attn_saved = attention_forward(exchange(sent), order, size)
    result, inner, hidden, mixed = mlp_forward(
        ids, x, vec, bias, rest, exchange(mixed), shards, ratio
    )
    return result, (x, weight, vec, attn_saved, inner, hidden, mixed)


def layer_backward(saved, grad, rest, ids, order, parts, size, shards, ratio, layer, background):
    x, weight, vec, attn_saved, inner, hidden, mixed = saved
    width = x.shape[1]
    depth = width // shards
    last = layer == 0
    sent, (ginner, gattn, ghid, act, middle, table) = mlp_backward(
        ids, grad, inner, hidden, vec, rest, parts, size, shards, ratio
    )
    sent = background.slot(sent)
    early = early_grads(ids, middle, ghid, mixed, gattn, act, grad, parts, shards, ratio, last)
    received = exchange(sent)
    both = background.slot([*received, *early])
    received, early = both[:parts], both[parts:]
    if last:
        tasks = [
            background.add(permuted_task(*early[:2], layer, (0, 1, 0), (0, 0, 0))),
            background.add(permuted_task(*early[2:], layer, (0, 1, 1), (0, 0, 0))),
        ]
    else:
        tasks = [background.add(offloaded_task(early[0], layer, 5, 1, (1, 1, 1)))]
    sent = attention_backward(received, attn_saved, order, size)
    sent = background.slot(sent)
    received = background.slot(exchange(sent))
    grad_x, keep, send = qkv_backward(
        ids, x, ginner, vec, table, weight, received, shards
    )
    grad_x, keep, send = background.slot([grad_x, keep, send])
    slack = ((0, 0, 0), (0, 0, 0)) if last else ((0, 1, 0), (1, 0, 0))
    tasks.append(background.add(permuted_task(keep, send, layer, *slack)))
    return grad_x, tasks


def blocks_to_columns(value, parts):
    depth = value.shape[0] // parts
    return [value[i * depth : (i + 1) * depth] for i in range(parts)]


def split_layers(pack, core):
    rows = pack.shape[0] // 2
    first, second = pack[:rows], pack[rows:]
    other = lax.ppermute(jnp.where(core == 0, second, first), "section", [(0, 1), (1, 0)])
    return jnp.where(core == 0, first, other), jnp.where(core == 0, other, second)


def gather(part):
    return lax.all_gather(part, SHARDS, axis=0, tiled=True)


def across(value, bit):
    count = lax.axis_size("fsdp")
    return lax.ppermute(value, "fsdp", [(i, i ^ bit) for i in range(count)])


def swap_cores(value):
    return lax.ppermute(value, "section", [(0, 1), (1, 0)])


def gather_pieces(part):
    rows = part.shape[0] // 2
    by_x, by_y = across(part, 1), across(part, 2)
    pieces = [part, by_x, by_y, across(by_x[:rows], 2), across(by_y[rows:], 1)]
    return pieces + [swap_cores(piece) for piece in pieces]


class Background:
    def __init__(self):
        self.tasks = []

    def add(self, task):
        entry = {"task": task, "result": None}
        entry["flight"] = next(task)
        self.tasks.append(entry)
        return entry

    def slot(self, values):
        waiting = [entry for entry in self.tasks if entry["flight"] is not None]
        flat = list(values)
        for entry in waiting:
            flat += entry["flight"]
        flat = list(lax.optimization_barrier(tuple(flat)))
        values, flat = flat[: len(values)], flat[len(values) :]
        for entry in waiting:
            count = len(entry["flight"])
            held, flat = flat[:count], flat[count:]
            try:
                entry["flight"] = entry["task"].send(held)
            except StopIteration as stop:
                entry["flight"], entry["result"] = None, stop.value
        return values

    def finish(self):
        while any(entry["flight"] is not None for entry in self.tasks):
            self.slot([])


def held(flight, slots):
    for _ in range(slots):
        yield []
    return (yield flight)


def permuted_task(keep, send, layer, slack, ctx_slack):
    (received,) = yield from held([swap_cores(send)], slack[0])
    rows = keep.shape[1] // 2

    def summed(slots, side):
        return sum_pair(keep[slots, side], received[slots, side])

    top, low = slice(0, rows), slice(rows, 2 * rows)
    by_x, by_y = yield from held(
        [across(summed(slice(1, 4, 2), top), 1), across(summed(slice(2, 4), low), 2)], slack[1]
    )
    first = sum_pair(summed(slice(0, 4, 2), top), by_x)
    second = sum_pair(summed(slice(0, 2), low), by_y)
    by_y, by_x = yield from held([across(first[1], 2), across(second[1], 1)], slack[2])
    value = jnp.concatenate([sum_pair(first[0], by_y), sum_pair(second[0], by_x)])
    return (yield from ctx_task(value, layer, ctx_slack))


def offloaded_task(pack, layer, wait, pause, ctx_slack):
    value = lax.psum_scatter(pack, SHARDS, scatter_dimension=0, tiled=True)
    (value,) = yield from held([value], wait)
    for _ in range(pause):
        yield []
    return (yield from ctx_task(value, layer, ctx_slack))


def ctx_task(value, layer, slack):
    if lax.axis_size("ctx") == 4:
        index = lax.axis_index("ctx")
        (received,) = yield from held([lax.ppermute(value, "ctx", [(0, 1), (3, 2)])], slack[0])
        value = sum_pair(value, received)
        (received,) = yield from held([lax.ppermute(value, "ctx", [(1, 2), (2, 1)])], slack[1])
        value = sum_pair(value, received)
        (received,) = yield from held([lax.ppermute(value, "ctx", [(1, 0), (2, 3)])], slack[2])
        value = jnp.where((index == 0) | (index == 3), received, value)
    else:
        value = lax.psum(value, "ctx")
    (other,) = yield [lax.ppermute(value, "section", [(1 - layer, layer)])]
    return value, other


def return_task(values, layers):
    flight = [moved for value, layer in zip(values, layers) for moved in return_rows(value, layer)]
    flight = yield flight
    return flight


def sum_pair(a, b):
    return (a.astype(F32) + b.astype(F32)).astype(BF)


def body(
    tokens, cotangent, span_order, w_qkv, w_out, w_up, w_down, norm_gains, bias_rows, bias_hidden
):
    core = lax.axis_index("section")
    ctx = lax.axis_size("ctx")
    cores = lax.axis_size("section")
    shards = lax.axis_size("fsdp")
    half = ctx // cores
    base = lax.axis_index("ctx") // half
    member = core * half + lax.axis_index("ctx") % half
    depth = w_qkv.shape[1]
    width = depth * shards
    ratio = bias_hidden.shape[1] // depth
    size = width // HEADS
    gain_count, shift_count = norm_gains.shape[1], bias_rows.shape[1]

    steps = jnp.arange(ctx, dtype=jnp.int32)
    came, goes = (member - steps) % ctx, (member + steps) % ctx
    shard = lax.axis_index("fsdp")
    slots = [shard ^ k for k in range(shards)] + [core, 1 - core]
    ids = jnp.concatenate([goes, came, jnp.stack(slots)]).astype(jnp.int32)
    order = jnp.concatenate([span_order[came], span_order[goes]])

    small = jnp.concatenate([norm_gains[0], bias_rows[0], bias_hidden[0].reshape(ratio, depth)]).T
    small = jnp.pad(small, ((0, 0), (0, LANES - small.shape[1])))
    first = jnp.concatenate([w_qkv[0], small], axis=1)
    rest = jnp.concatenate([w_out[0], w_up[0]] + blocks_to_columns(w_down[0], ratio), axis=1)
    first0, first1 = split_layers(first, core)
    x = bring_rows(tokens[:, 0], core, base)
    rest0, rest1 = split_layers(rest, core)
    first0, first1 = gather_pieces(first0), gather_pieces(first1)
    rest0, rest1 = gather(rest0), gather(rest1)
    sizes = (ids, order, ctx, size, shards, ratio)
    out0, saved0 = layer_forward(x, first0, rest0, *sizes)
    late_cot, out0 = lax.optimization_barrier((cotangent[:, 0], out0))
    out1, saved1 = layer_forward(out0, first1, rest1, *sizes)
    cot = bring_rows(late_cot, core, base)
    background = Background()
    outs = background.add(return_task([out0, out1], [0, 1]))
    grad1, reduced1 = layer_backward(saved1, cot, rest1, *sizes, 1, background)
    back1 = background.add(return_task([grad1], [1]))
    grad0, reduced0 = layer_backward(saved0, grad1, rest0, *sizes, 0, background)
    back0 = background.add(return_task([grad0], [0]))
    background.finish()

    def chosen(values0, values1):
        return jnp.stack([jnp.where(core == 0, a, b) for a, b in zip(values0, values1)])

    layer_outputs = chosen(outs["result"][:cores], outs["result"][cores:])
    input_grads = chosen(back0["result"], back1["result"]).astype(F32)

    def joined(pair0, pair1):
        return jnp.where(
            core == 0,
            jnp.concatenate([pair0[0], pair0[1]]),
            jnp.concatenate([pair1[1], pair1[0]]),
        ).astype(F32)

    (early0, down0, late0), (early1, late1) = [
        [entry["result"] for entry in reduced] for reduced in (reduced0, reduced1)
    ]
    main = (1 + ratio) * width
    early = joined(early0, [value[:, :main] for value in early1])
    late = joined(late0, late1)
    down = joined(down0, [value[:, main:] for value in early1])
    table = late[:, 3 * width :].T
    return (
        layer_outputs[None, :, None],
        input_grads[None, :, None],
        late[None, :, : 3 * width],
        early[None, :, :width],
        early[None, :, width:],
        jnp.concatenate([down[:, j * width : (j + 1) * width] for j in range(ratio)])[None],
        table[None, :gain_count],
        table[None, gain_count : gain_count + shift_count],
        table[gain_count + shift_count : gain_count + shift_count + ratio].reshape(1, -1),
    )


def solution(mesh):
    return jax.shard_map(
        body,
        mesh=mesh,
        in_specs=(
            P(None, "fsdp", "ctx", None),
            P(None, "fsdp", "ctx", None),
            P(),
            P("section", "fsdp", None),
            P("section", "fsdp", None),
            P("section", "fsdp", None),
            P("section", "fsdp", None),
            P("section", None, "fsdp"),
            P("section", None, "fsdp"),
            P("section", "fsdp"),
        ),
        out_specs=(
            P("section", None, "fsdp", "ctx", None),
            P("section", None, "fsdp", "ctx", None),
            P("section", "fsdp", None),
            P("section", "fsdp", None),
            P("section", "fsdp", None),
            P("section", "fsdp", None),
            P("section", None, "fsdp"),
            P("section", None, "fsdp"),
            P("section", "fsdp"),
        ),
        check_vma=False,
    )
```

```python
import functools

import jax
import jax.numpy as jnp
from jax import lax
from jax.experimental import pallas as pl
from jax.experimental.pallas import tpu as pltpu
from jax.sharding import PartitionSpec as P

HEADS = 12
EPS = 1e-05
GELU_C = 0.7978845608
GELU_A = 0.044715
LANES = 128
BF = jnp.bfloat16
F32 = jnp.float32
VMEM = pl.BlockSpec(memory_space=pltpu.VMEM)
SMEM = pl.BlockSpec(memory_space=pltpu.SMEM)
HBM = pl.BlockSpec(memory_space=pl.ANY)
PARAMS = pltpu.CompilerParams(vmem_limit_bytes=56 * 1024 * 1024)
GROUP = ("section", "ctx")
SHARDS = ("fsdp", "section")


def dot(a, b, ca, cb):
    return lax.dot_general(a, b, (((ca,), (cb,)), ((), ())), preferred_element_type=F32)


def shape(dims, dtype):
    return jax.ShapeDtypeStruct(dims, dtype)


def place_of(core, ctx_index):
    return core * lax.axis_size("ctx") + ctx_index


def exchange(pieces):
    ctx, cores = lax.axis_size("ctx"), lax.axis_size("section")
    half = ctx // cores
    moved = [pieces[0]]
    for d in range(1, ctx):
        pairs = []
        for base in range(cores):
            for g in range(ctx):
                t = (g + d) % ctx
                pairs.append(
                    (
                        place_of(g // half, base * half + g % half),
                        place_of(t // half, base * half + t % half),
                    )
                )
        moved.append(lax.ppermute(pieces[d], GROUP, pairs))
    return moved


def bring_rows(both, core, base):
    ctx, cores = lax.axis_size("ctx"), lax.axis_size("section")
    half = ctx // cores
    pairs = [
        (place_of(c, c * half + i), place_of(c, (1 - c) * half + i))
        for c in range(cores)
        for i in range(half)
    ]
    received = lax.ppermute(jnp.where(core == 0, both[1], both[0]), GROUP, pairs)
    own = jnp.where(core == 0, both[0], both[1])
    return jnp.where(core == base, own, received)


def return_rows(value, layer):
    ctx, cores = lax.axis_size("ctx"), lax.axis_size("section")
    half = ctx // cores
    return [
        lax.ppermute(
            value,
            GROUP,
            [(place_of(z // half, m * half + z % half), place_of(layer, z)) for z in range(ctx)],
        )
        for m in range(cores)
    ]


def normalised(values):
    centred = values - jnp.mean(values, axis=-1, keepdims=True)
    scale = lax.rsqrt(jnp.mean(centred * centred, axis=-1, keepdims=True) + EPS)
    return centred * scale, scale


def norm_back(unit, scale, upstream, gain):
    w = upstream * gain
    return (
        w - jnp.mean(w, axis=-1, keepdims=True) - unit * jnp.mean(w * unit, axis=-1, keepdims=True)
    ) * scale


def piece_places(ids_ref, parts, depth, slots):
    first = 2 * parts
    rows = depth // 2
    places = []
    for side in range(2):
        core = ids_ref[first + slots + side]
        for slot, start, count in (
            (0, 0, rows),
            (1, 0, rows),
            (2, 0, rows),
            (3, 0, rows // 2),
            (3, rows // 2, rows // 2),
        ):
            place = ids_ref[first + slot] * depth + core * rows + start
            places.append((pl.multiple_of(place, 16), count))
    return places


def qkv_kernel(ids_ref, x_ref, *refs, parts, size, shards):
    packs, refs = refs[:10], refs[10:]
    outs, (weight_ref, vec_ref), refs = refs[:parts], refs[parts : parts + 2], refs[parts + 2 :]
    weight, small, whole, sems = refs
    width = x_ref.shape[1]
    copies = []
    for i, (place, count) in enumerate(piece_places(ids_ref, parts, width // shards, shards)):
        for j, target, cols in (
            (0, small, slice(3 * width, 3 * width + LANES)),
            (1, weight, slice(0, 3 * width)),
        ):
            copies.append(
                pltpu.make_async_copy(
                    packs[i].at[:, cols], target.at[pl.ds(place, count)], sems.at[2 * i + j]
                )
            )
    for copy in copies:
        copy.start()
    unit, _ = normalised(x_ref[...].astype(F32))
    for copy in copies:
        copy.wait()
    keep = pltpu.make_async_copy(weight, weight_ref, sems.at[20])
    keep.start()
    vec = small[...].astype(F32).T
    vec_ref[...] = vec[:16]
    normed = (unit * vec[0:1] + vec[2:3]).astype(BF)
    held = outs[0].shape[0] // 3
    if parts * held != width:
        whole[...] = jnp.zeros_like(whole)
    for b in range(3):
        block = dot(normed, weight[:, b * width : (b + 1) * width], 1, 0)
        if b == 0:
            block = block + vec[3:4]
        if b == 2:
            block = block + vec[4:5]
        whole[b * parts * held : b * parts * held + width] = block.T.astype(BF)
    for d in range(parts):
        for b in range(3):
            first = pl.multiple_of(b * parts * held + ids_ref[d] * held, size)
            outs[d][b * held : (b + 1) * held] = whole[pl.ds(first, held)]
    keep.wait()


def qkv_project(ids, x, packs, parts, size, shards):
    rows, width = x.shape
    held = pl.cdiv(HEADS, parts) * size
    results = pl.pallas_call(
        functools.partial(qkv_kernel, parts=parts, size=size, shards=shards),
        in_specs=[SMEM, VMEM] + [HBM] * 10,
        out_specs=[VMEM] * parts + [HBM, VMEM],
        out_shape=[shape((3 * held, rows), BF)] * parts
        + [shape((width, 3 * width), BF), shape((16, width), F32)],
        scratch_shapes=[
            pltpu.VMEM((width, 3 * width), BF),
            pltpu.VMEM((width, LANES), BF),
            pltpu.VMEM((3 * parts * held, rows), BF),
            pltpu.SemaphoreType.DMA((21,)),
        ],
        compiler_params=PARAMS,
        name="qkv_project",
    )(ids, x, *packs)
    return results[:parts], results[parts], results[parts + 1]


def spans_of(order_ref, which, count, span):
    first = order_ref[which]
    return (
        (0, pl.multiple_of(first * span, span)),
        (1, pl.multiple_of((2 * count - 1 - first) * span, span)),
    )


def causal(scores, width, fill):
    depth = scores.shape[0]
    keys = lax.broadcasted_iota(jnp.int32, (width, width), 0)
    rows = lax.broadcasted_iota(jnp.int32, (width, width), 1)
    last = jnp.where(keys <= rows, scores[depth - width :], fill)
    if depth == width:
        return last
    return jnp.concatenate([scores[: depth - width], last], axis=0)


def sort_in(order_ref, pieces, target):
    count = len(pieces)
    span = pieces[0].shape[1] // 2
    for d in range(count):
        for side, place in spans_of(order_ref, d, count, span):
            target[:, pl.ds(place, span)] = pieces[d][:, side * span : (side + 1) * span]


def sort_out(order_ref, source, pieces):
    count = len(pieces)
    span = pieces[0].shape[1] // 2
    for d in range(count):
        for side, place in spans_of(order_ref, count + d, count, span):
            pieces[d][:, side * span : (side + 1) * span] = source[:, pl.ds(place, span)]


def attn_fwd_kernel(order_ref, *refs, parts, heads, size, block):
    pieces, mixed, (sorted_ref, out_ref, lse_ref) = refs[:parts], refs[parts : 2 * parts], refs[2 * parts :]
    feats = heads * size
    seq = sorted_ref.shape[1]
    sort_in(order_ref, pieces, sorted_ref)
    lse_ref[...] = jnp.zeros_like(lse_ref)
    for h in range(heads):
        for start in range(0, seq, block):
            end = start + block
            q = sorted_ref[h * size : (h + 1) * size, start:end]
            k = sorted_ref[feats + h * size : feats + (h + 1) * size, :end]
            v = sorted_ref[2 * feats + h * size : 2 * feats + (h + 1) * size, :end]
            scores = causal(dot(k, q, 0, 0) * 0.125, block, -1e30)
            top = jnp.max(scores, axis=0, keepdims=True)
            weights = jnp.exp(scores - top)
            total = jnp.sum(weights, axis=0, keepdims=True)
            mixed_part = dot(v, weights.astype(BF), 1, 0) / total
            out_ref[h * size : (h + 1) * size, start:end] = mixed_part.astype(BF)
            lse_ref[h : h + 1, start:end] = top + jnp.log(total)
    sort_out(order_ref, out_ref, mixed)


def attn_bwd_kernel(order_ref, *refs, parts, heads, size, block):
    pieces, (sorted_ref, out_ref, lse_ref) = refs[:parts], refs[parts : parts + 3]
    grads, (dsort, gsort, gk, gv) = refs[parts + 3 : 2 * parts + 3], refs[2 * parts + 3 :]
    feats = heads * size
    seq = sorted_ref.shape[1]
    sort_in(order_ref, pieces, dsort)
    for h in range(heads):
        own = slice(h * size, (h + 1) * size)
        gk[...] = jnp.zeros_like(gk)
        gv[...] = jnp.zeros_like(gv)
        for start in range(0, seq, block):
            end = start + block
            q = sorted_ref[own, start:end]
            k = sorted_ref[feats + h * size : feats + (h + 1) * size, :end]
            v = sorted_ref[2 * feats + h * size : 2 * feats + (h + 1) * size, :end]
            dout = dsort[own, start:end]
            delta = jnp.sum(
                dout.astype(F32) * out_ref[own, start:end].astype(F32), axis=0, keepdims=True
            )
            scores = dot(k, q, 0, 0) * 0.125 - lse_ref[h : h + 1, start:end]
            probs = jnp.exp(causal(scores, block, -1e30))
            dprobs = dot(v, dout, 0, 0)
            dscores = (probs * (dprobs - delta)).astype(BF)
            gsort[own, start:end] = (dot(k, dscores, 1, 0) * 0.125).astype(BF)
            gk[:, :end] += dot(q, dscores, 1, 1)
            gv[:, :end] += dot(dout, probs.astype(BF), 1, 1)
        gsort[feats + h * size : feats + (h + 1) * size, :] = (gk[...] * 0.125).astype(BF)
        gsort[2 * feats + h * size : 2 * feats + (h + 1) * size, :] = gv[...].astype(BF)
    sort_out(order_ref, gsort, grads)


def widen(pieces, order):
    count = len(pieces)
    span = pieces[0].shape[1] // 2
    came = order[:count]
    holder = jnp.stack([came, 2 * count - 1 - came], axis=1).reshape(-1)
    place = jnp.argsort(holder)
    flat = jnp.concatenate(pieces, axis=1).reshape(-1, 2 * count, span)
    return [jnp.take(flat, place, axis=1).reshape(flat.shape[0], -1)]


def narrow(wide, order, count):
    feats, seq = wide.shape
    span = seq // (2 * count)
    goes = order[count:]
    holder = jnp.stack([goes, 2 * count - 1 - goes], axis=1).reshape(-1)
    flat = jnp.take(wide.reshape(feats, 2 * count, span), holder, axis=1)
    flat = flat.reshape(feats, count, 2 * span)
    return [flat[:, d] for d in range(count)]


def attention_forward(pieces, order, size):
    parts, rows = len(pieces), pieces[0].shape[1]
    seq = parts * rows
    heads = pieces[0].shape[0] // (3 * size)
    narrow_spans = (rows // 2) % LANES != 0
    ids, given = order, parts
    if narrow_spans:
        pieces, ids, given = widen(pieces, order), jnp.zeros((2,), jnp.int32), 1
    results = pl.pallas_call(
        functools.partial(
            attn_fwd_kernel, parts=given, heads=heads, size=size, block=min(256, seq // 2)
        ),
        in_specs=[SMEM] + [VMEM] * given,
        out_specs=[VMEM] * (given + 3),
        out_shape=[shape((heads * size, pieces[0].shape[1]), BF)] * given
        + [
            shape((3 * heads * size, seq), BF),
            shape((heads * size, seq), BF),
            shape((8 * pl.cdiv(heads, 8), seq), F32),
        ],
        compiler_params=PARAMS,
        name="attn_fwd",
    )(ids, *pieces)
    mixed = results[:given]
    if narrow_spans:
        mixed = narrow(mixed[0], order, parts)
    return mixed, tuple(results[given:])


def attention_backward(pieces, saved, order, size):
    parts, rows = len(pieces), pieces[0].shape[1]
    seq = parts * rows
    heads = pieces[0].shape[0] // size
    narrow_spans = (rows // 2) % LANES != 0
    ids, given = order, parts
    if narrow_spans:
        pieces, ids, given = widen(pieces, order), jnp.zeros((2,), jnp.int32), 1
    grads = pl.pallas_call(
        functools.partial(
            attn_bwd_kernel, parts=given, heads=heads, size=size, block=min(256, seq // 2)
        ),
        in_specs=[SMEM] + [VMEM] * (given + 3),
        out_specs=[VMEM] * given,
        out_shape=[shape((3 * heads * size, pieces[0].shape[1]), BF)] * given,
        scratch_shapes=[
            pltpu.VMEM((heads * size, seq), BF),
            pltpu.VMEM((3 * heads * size, seq), BF),
            pltpu.VMEM((size, seq), F32),
            pltpu.VMEM((size, seq), F32),
        ],
        compiler_params=PARAMS,
        name="attn_bwd",
    )(ids, *pieces, *saved)
    if narrow_spans:
        grads = narrow(grads[0], order, parts)
    return grads


def down_blocks(shards, ratio, depth):
    width = shards * depth
    for f in range(shards):
        for j in range(ratio):
            first = (f * ratio + j) * depth
            yield slice(first, first + depth), slice(f * depth, (f + 1) * depth), j * width


def rest_copies(pack, w_out, w_up, w_down, sems, shards, ratio):
    width = w_out.shape[0]
    depth = width // shards
    hidden = w_up.shape[1]
    out = [pltpu.make_async_copy(pack.at[:, :width], w_out, sems.at[0])]
    up = [pltpu.make_async_copy(pack.at[:, width : width + hidden], w_up, sems.at[1])]
    down = []
    for i, (rows, packed, column) in enumerate(down_blocks(shards, ratio, depth)):
        start = width + hidden + column
        down.append(
            pltpu.make_async_copy(
                pack.at[packed, start : start + width], w_down.at[rows], sems.at[2 + i]
            )
        )
    return out, up, down


def put_pieces(ids_ref, first, pieces, target):
    held = pieces[0].shape[0]
    for d, piece in enumerate(pieces):
        place = pl.multiple_of(ids_ref[first + d] * held, held)
        target[pl.ds(place, held)] = piece[...]


def mlp_kernel(ids_ref, x_ref, vec_ref, bias_ref, pack_ref, *refs, parts, shards, ratio):
    pieces = refs[:parts]
    result_ref, inner_ref, hidden_ref, mixed_ref = refs[parts : parts + 4]
    w_out, w_up, w_down, whole, sems = refs[parts + 4 :]
    width = x_ref.shape[1]
    out, up, down = rest_copies(pack_ref, w_out, w_up, w_down, sems, shards, ratio)
    for copy in out + up + down:
        copy.start()
    put_pieces(ids_ref, parts, pieces, whole)
    mixed_ref[...] = whole[:width]
    out[0].wait()
    inner = x_ref[...].astype(F32) + dot(whole[:width], w_out[...], 0, 0) + vec_ref[5:6]
    inner_ref[...] = inner
    unit, _ = normalised(inner)
    middle = (unit * vec_ref[1:2] + vec_ref[6:7]).astype(BF)
    up[0].wait()
    for copy in down:
        copy.wait()
    total = inner + vec_ref[7:8]
    for start in range(0, w_up.shape[1], width):
        cols = slice(start, start + width)
        hidden = dot(middle, w_up[:, cols], 1, 0) + bias_ref[:, cols]
        hidden_ref[:, cols] = hidden
        act = 0.5 * hidden * (1.0 + jnp.tanh(GELU_C * (hidden + GELU_A * hidden * hidden * hidden)))
        total = total + dot(act.astype(BF), w_down[cols], 1, 0)
    result_ref[...] = total.astype(BF)


def rest_scratch(width, hidden, shards, ratio):
    return [
        pltpu.VMEM((width, width), BF),
        pltpu.VMEM((width, hidden), BF),
        pltpu.VMEM((hidden, width), BF),
    ]


def mlp_forward(ids, x, vec, bias, pack, pieces, shards, ratio):
    parts = len(pieces)
    rows, width = x.shape
    hidden = ratio * width
    return pl.pallas_call(
        functools.partial(mlp_kernel, parts=parts, shards=shards, ratio=ratio),
        in_specs=[SMEM, VMEM, VMEM, VMEM, HBM] + [VMEM] * parts,
        out_specs=[VMEM] * 4,
        out_shape=[
            shape((rows, width), BF),
            shape((rows, width), F32),
            shape((rows, hidden), F32),
            shape((width, rows), BF),
        ],
        scratch_shapes=rest_scratch(width, hidden, shards, ratio)
        + [
            pltpu.VMEM((parts * pieces[0].shape[0], rows), BF),
            pltpu.SemaphoreType.DMA((2 + shards * ratio,)),
        ],
        compiler_params=PARAMS,
        name="mlp_forward",
    )(ids, x, vec, bias, pack, *pieces)


def mlp_back_kernel(
    ids_ref, grad_ref, inner_ref, hidden_ref, vec_ref, pack_ref, *refs, parts, shards, ratio
):
    outs = refs[:parts]
    ginner_ref, gattn_ref, ghid_ref, act_ref, middle_ref, table_ref = refs[parts : parts + 6]
    w_out, w_up, w_down, whole, sems = refs[parts + 6 :]
    width = grad_ref.shape[1]
    out, up, down = rest_copies(pack_ref, w_out, w_up, w_down, sems, shards, ratio)
    for copy in down + up + out:
        copy.start()
    grad_low = grad_ref[...].astype(BF)
    unit, scale = normalised(inner_ref[...])
    middle_ref[...] = (unit * vec_ref[1:2] + vec_ref[6:7]).astype(BF)
    for copy in down:
        copy.wait()
    up[0].wait()
    up_mid = jnp.zeros(unit.shape, F32)
    depth = width // shards
    table_ref[...] = jnp.zeros_like(table_ref)
    for start in range(0, w_up.shape[1], width):
        cols = slice(start, start + width)
        hidden = hidden_ref[:, cols]
        th = jnp.tanh(GELU_C * (hidden + GELU_A * hidden * hidden * hidden))
        act_ref[:, cols] = (0.5 * hidden * (1.0 + th)).astype(BF)
        slope = 0.5 * (1.0 + th) + 0.5 * hidden * (1.0 - th * th) * GELU_C * (
            1.0 + 3.0 * GELU_A * hidden * hidden
        )
        grad_hid = (dot(grad_low, w_down[cols], 1, 1) * slope).astype(BF)
        ghid_ref[:, cols] = grad_hid
        sums = jnp.sum(grad_hid.astype(F32), axis=0, keepdims=True)
        for i in range(width // depth):
            f, j = divmod(start // depth + i, ratio)
            table_ref[8 + j : 9 + j, f * depth : (f + 1) * depth] = sums[:, i * depth : (i + 1) * depth]
        up_mid = up_mid + dot(grad_hid, w_up[:, cols], 1, 1)
    grad_inner = grad_ref[...].astype(F32) + norm_back(unit, scale, up_mid, vec_ref[1:2])
    ginner_ref[...] = grad_inner
    grad_attn = grad_inner.astype(BF)
    gattn_ref[...] = grad_attn
    out[0].wait()
    held = outs[0].shape[0]
    if parts * held != width:
        whole[...] = jnp.zeros_like(whole)
    whole[:width] = dot(w_out[...], grad_attn, 1, 1).astype(BF)
    for d in range(parts):
        outs[d][...] = whole[pl.ds(pl.multiple_of(ids_ref[d] * held, held), held)]
    table_ref[1:2] = jnp.sum(up_mid * unit, axis=0, keepdims=True)
    table_ref[5:6] = jnp.sum(grad_attn.astype(F32), axis=0, keepdims=True)
    table_ref[6:7] = jnp.sum(up_mid, axis=0, keepdims=True)
    table_ref[7:8] = jnp.sum(grad_low.astype(F32), axis=0, keepdims=True)


def mlp_backward(ids, grad, inner, hidden, vec, pack, parts, size, shards, ratio):
    rows, width = inner.shape
    held = pl.cdiv(HEADS, parts) * size
    wide = ratio * width
    results = pl.pallas_call(
        functools.partial(mlp_back_kernel, parts=parts, shards=shards, ratio=ratio),
        in_specs=[SMEM, VMEM, VMEM, VMEM, VMEM, HBM],
        out_specs=[VMEM] * (parts + 6),
        out_shape=[shape((held, rows), BF)] * parts
        + [
            shape((rows, width), F32),
            shape((rows, width), BF),
            shape((rows, wide), BF),
            shape((rows, wide), BF),
            shape((rows, width), BF),
            shape((LANES, width), F32),
        ],
        scratch_shapes=rest_scratch(width, wide, shards, ratio)
        + [
            pltpu.VMEM((parts * held, rows), BF),
            pltpu.SemaphoreType.DMA((2 + shards * ratio,)),
        ],
        compiler_params=PARAMS,
        name="mlp_backward",
    )(ids, grad, inner, hidden, vec, pack)
    return results[:parts], results[parts:]


def write_down(act_ref, glow_ref, pack, start, shards, ratio):
    width = glow_ref.shape[1]
    depth = width // shards
    glow = glow_ref[...].astype(BF)
    for f in range(shards):
        block = dot(act_ref[:, f * ratio * depth : (f + 1) * ratio * depth], glow, 0, 0).astype(BF)
        for j in range(ratio):
            first = start + j * width
            pack[f * depth : (f + 1) * depth, first : first + width] = block[
                j * depth : (j + 1) * depth
            ]


def send_sides(ids_ref, first, pack, start, count, targets, sems, offset, shards):
    depth = pack.shape[0] // shards
    rows = depth // 2
    copies = []
    for side in range(2):
        core = ids_ref[first + shards + side]
        for k in range(shards):
            place = pl.multiple_of(ids_ref[first + k] * depth + core * rows, 16)
            copies.append(
                pltpu.make_async_copy(
                    pack.at[pl.ds(place, rows), start : start + count],
                    targets[side].at[k],
                    sems.at[offset + side * shards + k],
                )
            )
    for copy in copies:
        copy.start()
    return copies


def early_kernel(
    ids_ref, middle_ref, ghid_ref, mixed_ref, gattn_ref, act_ref, glow_ref, *refs, parts, shards, ratio, apart
):
    if apart:
        outs, (scratch, sems) = refs[:2], refs[2:]
    else:
        pack_ref, scratch, sems = refs
    width = middle_ref.shape[1]
    main = (1 + ratio) * width
    copies = []

    def send(columns, i):
        copy = pltpu.make_async_copy(scratch.at[:, columns], pack_ref.at[:, columns], sems.at[i])
        copy.start()
        copies.append(copy)

    scratch[:, :width] = dot(mixed_ref[...], gattn_ref[...], 1, 0).astype(BF)
    for i in range(ratio):
        cols = slice(i * width, (i + 1) * width)
        block = dot(middle_ref[...], ghid_ref[:, cols], 0, 0).astype(BF)
        scratch[:, (i + 1) * width : (i + 2) * width] = block
    if not apart:
        send(slice(0, main), 0)
    write_down(act_ref, glow_ref, scratch, main, shards, ratio)
    if apart:
        copies += send_sides(
            ids_ref, 2 * parts, scratch, 0, main + ratio * width, outs, sems, 0, shards
        )
    else:
        send(slice(main, main + ratio * width), 1)
    for copy in copies:
        copy.wait()


def early_grads(ids, middle, ghid, mixed, gattn, act, grad, parts, shards, ratio, apart):
    width = middle.shape[1]
    main, hidden = (1 + ratio) * width, ratio * width
    rows = width // shards // 2
    side = shape((shards, rows, main + hidden), BF)
    return pl.pallas_call(
        functools.partial(early_kernel, parts=parts, shards=shards, ratio=ratio, apart=apart),
        in_specs=[SMEM] + [VMEM] * 6,
        out_specs=[HBM] * (2 if apart else 1),
        out_shape=[side, side] if apart else [shape((width, main + hidden), BF)],
        scratch_shapes=[
            pltpu.VMEM((width, main + hidden), BF),
            pltpu.SemaphoreType.DMA((2 + 2 * shards,)),
        ],
        compiler_params=PARAMS,
        name="early_grads",
    )(ids, middle, ghid, mixed, gattn, act, grad)


def qkv_back_kernel(
    ids_ref, x_ref, ginner_ref, vec_ref, table_ref, weight_hbm, *refs, parts, shards, apart
):
    pieces, refs = refs[:parts], refs[parts:]
    gx_ref, *outs, weight, whole, pack, sem = refs
    width = x_ref.shape[1]
    main = 3 * width + LANES
    copies = []
    copy = pltpu.make_async_copy(weight_hbm, weight, sem.at[0])
    copy.start()
    held = pieces[0].shape[0] // 3
    padded = parts * held
    for d, piece in enumerate(pieces):
        for b in range(3):
            place = pl.multiple_of(b * padded + ids_ref[parts + d] * held, held)
            whole[pl.ds(place, held)] = piece[b * held : (b + 1) * held]
    unit, scale = normalised(x_ref[...].astype(F32))
    normed = (unit * vec_ref[0:1] + vec_ref[2:3]).T.astype(BF)
    copy.wait()
    up_norm = jnp.zeros((width, x_ref.shape[0]), F32)
    sums = []
    for b in range(3):
        grads = whole[b * padded : b * padded + width]
        cols = slice(b * width, (b + 1) * width)
        up_norm = up_norm + dot(weight[:, cols], grads, 1, 0)
        pack[:, cols] = dot(normed, grads, 1, 1).astype(BF)
        sums.append(jnp.sum(grads.astype(F32), axis=1, keepdims=True))
    up_norm = up_norm.T
    gx_ref[...] = (ginner_ref[...] + norm_back(unit, scale, up_norm, vec_ref[0:1])).astype(BF)
    line = lax.broadcasted_iota(jnp.int32, table_ref.shape, 0)
    table = jnp.where(
        line == 0,
        jnp.sum(up_norm * unit, axis=0, keepdims=True),
        jnp.where(line == 2, jnp.sum(up_norm, axis=0, keepdims=True), table_ref[...]),
    ).T
    lane = lax.broadcasted_iota(jnp.int32, table.shape, 1)
    table = jnp.where(lane == 3, sums[0], jnp.where(lane == 4, sums[2], table))
    pack[:, 3 * width : main] = table.astype(BF)
    if apart:
        copies += send_sides(ids_ref, 2 * parts, pack, 0, main, outs, sem, 1, shards)
    else:
        copies.append(pltpu.make_async_copy(pack, outs[0], sem.at[1]))
        copies[0].start()
    for copy in copies:
        copy.wait()


def qkv_backward(ids, x, ginner, vec, table, weight, pieces, shards, apart):
    parts = len(pieces)
    rows, width = x.shape
    total = 3 * width + LANES
    part = shape((shards, width // shards // 2, total), BF)
    outs = [part, part] if apart else [shape((width, total), BF)]
    return pl.pallas_call(
        functools.partial(qkv_back_kernel, parts=parts, shards=shards, apart=apart),
        in_specs=[SMEM, VMEM, VMEM, VMEM, VMEM, HBM] + [VMEM] * parts,
        out_specs=[VMEM] + [HBM] * len(outs),
        out_shape=[shape((rows, width), BF)] + outs,
        scratch_shapes=[
            pltpu.VMEM((width, 3 * width), BF),
            pltpu.VMEM((parts * pieces[0].shape[0], rows), BF),
            pltpu.VMEM((width, total), BF),
            pltpu.SemaphoreType.DMA((1 + 2 * shards,)),
        ],
        compiler_params=PARAMS,
        name="qkv_backward",
    )(ids, x, ginner, vec, table, weight, *pieces)


def layer_forward(x, packs, rest, ids, order, parts, size, shards, ratio, back=None):
    sent, weight, vec = qkv_project(ids, x, packs, parts, size, shards)
    width = x.shape[1]
    depth = width // shards
    bias = vec[8 : 8 + ratio].reshape(ratio, shards, depth).transpose(1, 0, 2).reshape(1, -1)
    received = exchange(sent)
    returned = None
    if back is not None:
        *received, back = lax.optimization_barrier((*received, back))
        returned = return_rows(back, 0)
    mixed, attn_saved = attention_forward(received, order, size)
    received = exchange(mixed)
    if back is not None:
        tied = lax.optimization_barrier((*received, *returned))
        received, returned = tied[:parts], tied[parts:]
    result, inner, hidden, mixed = mlp_forward(
        ids, x, vec, bias, rest, received, shards, ratio
    )
    return result, (x, weight, vec, attn_saved, inner, hidden, mixed), returned


def layer_backward(saved, grad, rest, ids, order, parts, size, shards, ratio, layer, background):
    x, weight, vec, attn_saved, inner, hidden, mixed = saved
    last = layer == 0
    column = (1 + ratio) * x.shape[1]
    sent, (ginner, gattn, ghid, act, middle, table) = mlp_backward(
        ids, grad, inner, hidden, vec, rest, parts, size, shards, ratio
    )
    received = exchange(background.slot("A", sent))
    early = early_grads(ids, middle, ghid, mixed, gattn, act, grad, parts, shards, ratio, last)
    tied = lax.optimization_barrier((*received, *early))
    received, early = tied[:parts], tied[parts:]
    if last:
        first = background.add("B", permuted_task(*early, layer, background, "B", column))
    else:
        first = background.add("C", offloaded_task(*early, layer, background, "C", column))
    sent = attention_backward(received, attn_saved, order, size)
    received = background.slot("BC" if last else "", exchange(sent))
    results = qkv_backward(ids, x, ginner, vec, table, weight, received, shards, last)
    grad_x, *late = lax.optimization_barrier(tuple(results))
    if last:
        (grad_x,) = background.slot("BC", [grad_x])
        second = background.add("A", permuted_task(*late, layer, background, "A", None))
    else:
        second = background.add("D", offloaded_task(*late, layer, background, "D", None))
    return grad_x, first, second


def blocks_to_columns(value, parts):
    depth = value.shape[0] // parts
    return [value[i * depth : (i + 1) * depth] for i in range(parts)]


def split_layers(pack, core):
    rows = pack.shape[0] // 2
    first, second = pack[:rows], pack[rows:]
    other = lax.ppermute(jnp.where(core == 0, second, first), "section", [(0, 1), (1, 0)])
    return jnp.where(core == 0, first, other), jnp.where(core == 0, other, second)


def gather(part):
    return lax.all_gather(part, SHARDS, axis=0, tiled=True)


def across(value, bit):
    count = lax.axis_size("fsdp")
    return lax.ppermute(value, "fsdp", [(i, i ^ bit) for i in range(count)])


def swap_cores(value):
    return lax.ppermute(value, "section", [(0, 1), (1, 0)])


def gather_pieces(part):
    rows = part.shape[0] // 2
    by_x, by_y = across(part, 1), across(part, 2)
    pieces = [part, by_x, by_y, across(by_x[:rows], 2), across(by_y[rows:], 1)]
    return pieces + [swap_cores(piece) for piece in pieces]


class Background:
    def __init__(self):
        self.tasks = []

    def add(self, lane, task):
        entry = {"lane": lane, "task": task, "result": None}
        entry["flight"] = next(task)
        self.tasks.append(entry)
        return entry

    def slot(self, lanes, values=()):
        waiting = [e for e in self.tasks if e["flight"] is not None and e["lane"] in lanes]
        flat = list(values)
        for entry in waiting:
            flat += entry["flight"]
        if len(flat) > 0:
            flat = list(lax.optimization_barrier(tuple(flat)))
        values, flat = flat[: len(values)], flat[len(values) :]
        for entry in waiting:
            count = len(entry["flight"])
            held, flat = flat[:count], flat[count:]
            try:
                entry["flight"] = entry["task"].send(held)
            except StopIteration as stop:
                entry["flight"], entry["result"] = None, stop.value
        return values

    def finish(self, lanes):
        while any(entry["flight"] is not None for entry in self.tasks):
            for lane in lanes:
                self.slot(lane)


def permuted_task(keep, send, layer, background, lane, column):
    (received,) = yield [swap_cores(send)]
    rows = keep.shape[1] // 2

    def summed(slots, side):
        return sum_pair(keep[slots, side], received[slots, side])

    top, low = slice(0, rows), slice(rows, 2 * rows)
    by_x, by_y = yield [
        across(summed(slice(1, 4, 2), top), 1),
        across(summed(slice(2, 4), low), 2),
    ]
    first = sum_pair(summed(slice(0, 4, 2), top), by_x)
    second = sum_pair(summed(slice(0, 2), low), by_y)
    by_y, by_x = yield [across(first[1], 2), across(second[1], 1)]
    value = jnp.concatenate([sum_pair(first[0], by_y), sum_pair(second[0], by_x)])
    return (yield from split_task(value, layer, background, lane, column))


def offloaded_task(pack, layer, background, lane, column):
    (value,) = yield [lax.psum_scatter(pack, SHARDS, scatter_dimension=0, tiled=True)]
    return (yield from split_task(value, layer, background, lane, column))


def split_task(value, layer, background, lane, column):
    if column is None:
        return (yield from ctx_task(value, layer))
    other = background.add(lane, ctx_task(value[:, column:], layer))
    mine = yield from ctx_task(value[:, :column], layer)
    return mine, other


def ctx_task(value, layer):
    if lax.axis_size("ctx") == 4:
        index = lax.axis_index("ctx")
        (received,) = yield [lax.ppermute(value, "ctx", [(0, 1), (3, 2)])]
        value = sum_pair(value, received)
        (received,) = yield [lax.ppermute(value, "ctx", [(1, 2), (2, 1)])]
        value = sum_pair(value, received)
        (received,) = yield [lax.ppermute(value, "ctx", [(1, 0), (2, 3)])]
        value = jnp.where((index == 0) | (index == 3), received, value)
    else:
        value = lax.psum(value, "ctx")
    (other,) = yield [lax.ppermute(value, "section", [(1 - layer, layer)])]
    return value, other


def return_task(value, layer, pause):
    for _ in range(pause):
        yield []
    flight = yield return_rows(value, layer)
    return flight


def sum_pair(a, b):
    return (a.astype(F32) + b.astype(F32)).astype(BF)


def body(
    tokens, cotangent, span_order, w_qkv, w_out, w_up, w_down, norm_gains, bias_rows, bias_hidden
):
    core = lax.axis_index("section")
    ctx = lax.axis_size("ctx")
    cores = lax.axis_size("section")
    shards = lax.axis_size("fsdp")
    half = ctx // cores
    base = lax.axis_index("ctx") // half
    member = core * half + lax.axis_index("ctx") % half
    depth = w_qkv.shape[1]
    width = depth * shards
    ratio = bias_hidden.shape[1] // depth
    size = width // HEADS
    gain_count, shift_count = norm_gains.shape[1], bias_rows.shape[1]

    steps = jnp.arange(ctx, dtype=jnp.int32)
    came, goes = (member - steps) % ctx, (member + steps) % ctx
    shard = lax.axis_index("fsdp")
    slots = [shard ^ k for k in range(shards)] + [core, 1 - core]
    ids = jnp.concatenate([goes, came, jnp.stack(slots)]).astype(jnp.int32)
    order = jnp.concatenate([span_order[came], span_order[goes]])

    small = jnp.concatenate([norm_gains[0], bias_rows[0], bias_hidden[0].reshape(ratio, depth)]).T
    small = jnp.pad(small, ((0, 0), (0, LANES - small.shape[1])))
    first = jnp.concatenate([w_qkv[0], small], axis=1)
    rest = jnp.concatenate([w_out[0], w_up[0]] + blocks_to_columns(w_down[0], ratio), axis=1)
    first0, first1 = split_layers(first, core)
    x = bring_rows(tokens[:, 0], core, base)
    rest0, rest1 = split_layers(rest, core)
    first0, first1 = gather_pieces(first0), gather_pieces(first1)
    rest0, rest1 = gather(rest0), gather(rest1)
    sizes = (ids, order, ctx, size, shards, ratio)
    out0, saved0, _ = layer_forward(x, first0, rest0, *sizes)
    late_cot, out0 = lax.optimization_barrier((cotangent[:, 0], out0))
    out1, saved1, back_out0 = layer_forward(out0, first1, rest1, *sizes, out0)
    cot = bring_rows(late_cot, core, base)
    background = Background()
    grad1, early1, late1 = layer_backward(saved1, cot, rest1, *sizes, 1, background)
    back1 = background.add("A", return_task(jnp.concatenate([out1, grad1], axis=1), 1, 0))
    grad0, early0, late0 = layer_backward(saved0, grad1, rest0, *sizes, 0, background)
    back0 = background.add("A", return_task(grad0, 0, 2))
    background.finish(("A", "BD", "C"))

    def chosen(values0, values1):
        return jnp.stack([jnp.where(core == 0, a, b) for a, b in zip(values0, values1)])

    layer_outputs = chosen(back_out0, [value[:, :width] for value in back1["result"]])
    input_grads = chosen(
        back0["result"], [value[:, width:] for value in back1["result"]]
    ).astype(F32)

    def joined(pair0, pair1):
        return jnp.where(
            core == 0,
            jnp.concatenate([pair0[0], pair0[1]]),
            jnp.concatenate([pair1[1], pair1[0]]),
        ).astype(F32)

    (up0, down0), (up1, down1) = early0["result"], early1["result"]
    early = joined(up0, up1)
    late = joined(late0["result"], late1["result"])
    down = joined(down0["result"], down1["result"])
    table = late[:, 3 * width :].T
    return (
        layer_outputs[None, :, None],
        input_grads[None, :, None],
        late[None, :, : 3 * width],
        early[None, :, :width],
        early[None, :, width:],
        jnp.concatenate([down[:, j * width : (j + 1) * width] for j in range(ratio)])[None],
        table[None, :gain_count],
        table[None, gain_count : gain_count + shift_count],
        table[gain_count + shift_count : gain_count + shift_count + ratio].reshape(1, -1),
    )


def solution(mesh):
    return jax.shard_map(
        body,
        mesh=mesh,
        in_specs=(
            P(None, "fsdp", "ctx", None),
            P(None, "fsdp", "ctx", None),
            P(),
            P("section", "fsdp", None),
            P("section", "fsdp", None),
            P("section", "fsdp", None),
            P("section", "fsdp", None),
            P("section", None, "fsdp"),
            P("section", None, "fsdp"),
            P("section", "fsdp"),
        ),
        out_specs=(
            P("section", None, "fsdp", "ctx", None),
            P("section", None, "fsdp", "ctx", None),
            P("section", "fsdp", None),
            P("section", "fsdp", None),
            P("section", "fsdp", None),
            P("section", "fsdp", None),
            P("section", None, "fsdp"),
            P("section", None, "fsdp"),
            P("section", "fsdp"),
        ),
        check_vma=False,
    )
```

```python
import functools

import jax
import jax.numpy as jnp
from jax import lax
from jax.experimental import pallas as pl
from jax.experimental.pallas import tpu as pltpu
from jax.sharding import PartitionSpec as P

HEADS = 12
EPS = 1e-05
GELU_C = 0.7978845608
GELU_A = 0.044715
LANES = 128
BF = jnp.bfloat16
F32 = jnp.float32
VMEM = pl.BlockSpec(memory_space=pltpu.VMEM)
SMEM = pl.BlockSpec(memory_space=pltpu.SMEM)
HBM = pl.BlockSpec(memory_space=pl.ANY)
PARAMS = pltpu.CompilerParams(vmem_limit_bytes=56 * 1024 * 1024)
GROUP = ("section", "ctx")
SHARDS = ("fsdp", "section")


def dot(a, b, ca, cb):
    return lax.dot_general(a, b, (((ca,), (cb,)), ((), ())), preferred_element_type=F32)


def shape(dims, dtype):
    return jax.ShapeDtypeStruct(dims, dtype)


def place_of(core, ctx_index):
    return core * lax.axis_size("ctx") + ctx_index


def exchange(pieces):
    ctx, cores = lax.axis_size("ctx"), lax.axis_size("section")
    half = ctx // cores
    moved = [pieces[0]]
    for d in range(1, ctx):
        pairs = []
        for base in range(cores):
            for g in range(ctx):
                t = (g + d) % ctx
                pairs.append(
                    (
                        place_of(g // half, base * half + g % half),
                        place_of(t // half, base * half + t % half),
                    )
                )
        moved.append(lax.ppermute(pieces[d], GROUP, pairs))
    return moved


def bring_rows(both, core, base):
    ctx, cores = lax.axis_size("ctx"), lax.axis_size("section")
    half = ctx // cores
    pairs = [
        (place_of(c, c * half + i), place_of(c, (1 - c) * half + i))
        for c in range(cores)
        for i in range(half)
    ]
    received = lax.ppermute(jnp.where(core == 0, both[1], both[0]), GROUP, pairs)
    own = jnp.where(core == 0, both[0], both[1])
    return jnp.where(core == base, own, received)


def return_rows(value, layer):
    ctx, cores = lax.axis_size("ctx"), lax.axis_size("section")
    half = ctx // cores
    return [
        lax.ppermute(
            value,
            GROUP,
            [(place_of(z // half, m * half + z % half), place_of(layer, z)) for z in range(ctx)],
        )
        for m in range(cores)
    ]


def normalised(values):
    centred = values - jnp.mean(values, axis=-1, keepdims=True)
    scale = lax.rsqrt(jnp.mean(centred * centred, axis=-1, keepdims=True) + EPS)
    return centred * scale, scale


def norm_back(unit, scale, upstream, gain):
    w = upstream * gain
    return (
        w - jnp.mean(w, axis=-1, keepdims=True) - unit * jnp.mean(w * unit, axis=-1, keepdims=True)
    ) * scale


def piece_places(ids_ref, parts, depth, slots):
    first = 2 * parts
    rows = depth // 2
    places = []
    for side in range(2):
        core = ids_ref[first + slots + side]
        for slot, start, count in (
            (0, 0, rows),
            (1, 0, rows),
            (2, 0, rows),
            (3, 0, rows // 2),
            (3, rows // 2, rows // 2),
        ):
            place = ids_ref[first + slot] * depth + core * rows + start
            places.append((pl.multiple_of(place, 16), count))
    return places


def qkv_kernel(ids_ref, x_ref, *refs, parts, size, shards):
    packs, refs = refs[:10], refs[10:]
    outs, (weight_ref, vec_ref), refs = refs[:parts], refs[parts : parts + 2], refs[parts + 2 :]
    weight, small, whole, sems = refs
    width = x_ref.shape[1]
    copies = []
    for i, (place, count) in enumerate(piece_places(ids_ref, parts, width // shards, shards)):
        for j, target, cols in (
            (0, small, slice(3 * width, 3 * width + LANES)),
            (1, weight, slice(0, 3 * width)),
        ):
            copies.append(
                pltpu.make_async_copy(
                    packs[i].at[:, cols], target.at[pl.ds(place, count)], sems.at[2 * i + j]
                )
            )
    for copy in copies:
        copy.start()
    unit, _ = normalised(x_ref[...].astype(F32))
    for copy in copies:
        copy.wait()
    keep = pltpu.make_async_copy(weight, weight_ref, sems.at[20])
    keep.start()
    vec = small[...].astype(F32).T
    vec_ref[...] = vec[:16]
    normed = (unit * vec[0:1] + vec[2:3]).astype(BF)
    held = outs[0].shape[0] // 3
    if parts * held != width:
        whole[...] = jnp.zeros_like(whole)
    for b in range(3):
        block = dot(normed, weight[:, b * width : (b + 1) * width], 1, 0)
        if b == 0:
            block = block + vec[3:4]
        if b == 2:
            block = block + vec[4:5]
        whole[b * parts * held : b * parts * held + width] = block.T.astype(BF)
    for d in range(parts):
        for b in range(3):
            first = pl.multiple_of(b * parts * held + ids_ref[d] * held, size)
            outs[d][b * held : (b + 1) * held] = whole[pl.ds(first, held)]
    keep.wait()


def qkv_project(ids, x, packs, parts, size, shards):
    rows, width = x.shape
    held = pl.cdiv(HEADS, parts) * size
    results = pl.pallas_call(
        functools.partial(qkv_kernel, parts=parts, size=size, shards=shards),
        in_specs=[SMEM, VMEM] + [HBM] * 10,
        out_specs=[VMEM] * parts + [HBM, VMEM],
        out_shape=[shape((3 * held, rows), BF)] * parts
        + [shape((width, 3 * width), BF), shape((16, width), F32)],
        scratch_shapes=[
            pltpu.VMEM((width, 3 * width), BF),
            pltpu.VMEM((width, LANES), BF),
            pltpu.VMEM((3 * parts * held, rows), BF),
            pltpu.SemaphoreType.DMA((21,)),
        ],
        compiler_params=PARAMS,
        name="qkv_project",
    )(ids, x, *packs)
    return results[:parts], results[parts], results[parts + 1]


def spans_of(order_ref, which, count, span):
    first = order_ref[which]
    return (
        (0, pl.multiple_of(first * span, span)),
        (1, pl.multiple_of((2 * count - 1 - first) * span, span)),
    )


def causal(scores, width, fill):
    depth = scores.shape[0]
    keys = lax.broadcasted_iota(jnp.int32, (width, width), 0)
    rows = lax.broadcasted_iota(jnp.int32, (width, width), 1)
    last = jnp.where(keys <= rows, scores[depth - width :], fill)
    if depth == width:
        return last
    return jnp.concatenate([scores[: depth - width], last], axis=0)


def sort_in(order_ref, pieces, target):
    count = len(pieces)
    span = pieces[0].shape[1] // 2
    for d in range(count):
        for side, place in spans_of(order_ref, d, count, span):
            target[:, pl.ds(place, span)] = pieces[d][:, side * span : (side + 1) * span]


def sort_out(order_ref, source, pieces):
    count = len(pieces)
    span = pieces[0].shape[1] // 2
    for d in range(count):
        for side, place in spans_of(order_ref, count + d, count, span):
            pieces[d][:, side * span : (side + 1) * span] = source[:, pl.ds(place, span)]


def attn_fwd_kernel(order_ref, *refs, parts, heads, size, block):
    pieces, mixed, (sorted_ref, out_ref, lse_ref) = refs[:parts], refs[parts : 2 * parts], refs[2 * parts :]
    feats = heads * size
    seq = sorted_ref.shape[1]
    sort_in(order_ref, pieces, sorted_ref)
    lse_ref[...] = jnp.zeros_like(lse_ref)
    for h in range(heads):
        for start in range(0, seq, block):
            end = start + block
            q = sorted_ref[h * size : (h + 1) * size, start:end]
            k = sorted_ref[feats + h * size : feats + (h + 1) * size, :end]
            v = sorted_ref[2 * feats + h * size : 2 * feats + (h + 1) * size, :end]
            scores = causal(dot(k, q, 0, 0) * 0.125, block, -1e30)
            top = jnp.max(scores, axis=0, keepdims=True)
            weights = jnp.exp(scores - top)
            total = jnp.sum(weights, axis=0, keepdims=True)
            mixed_part = dot(v, weights.astype(BF), 1, 0) / total
            out_ref[h * size : (h + 1) * size, start:end] = mixed_part.astype(BF)
            lse_ref[h : h + 1, start:end] = top + jnp.log(total)
    sort_out(order_ref, out_ref, mixed)


def attn_bwd_kernel(order_ref, *refs, parts, heads, size, block):
    pieces, (sorted_ref, out_ref, lse_ref) = refs[:parts], refs[parts : parts + 3]
    grads, (dsort, gsort, gk, gv) = refs[parts + 3 : 2 * parts + 3], refs[2 * parts + 3 :]
    feats = heads * size
    seq = sorted_ref.shape[1]
    sort_in(order_ref, pieces, dsort)
    for h in range(heads):
        own = slice(h * size, (h + 1) * size)
        gk[...] = jnp.zeros_like(gk)
        gv[...] = jnp.zeros_like(gv)
        for start in range(0, seq, block):
            end = start + block
            q = sorted_ref[own, start:end]
            k = sorted_ref[feats + h * size : feats + (h + 1) * size, :end]
            v = sorted_ref[2 * feats + h * size : 2 * feats + (h + 1) * size, :end]
            dout = dsort[own, start:end]
            delta = jnp.sum(
                dout.astype(F32) * out_ref[own, start:end].astype(F32), axis=0, keepdims=True
            )
            scores = dot(k, q, 0, 0) * 0.125 - lse_ref[h : h + 1, start:end]
            probs = jnp.exp(causal(scores, block, -1e30))
            dprobs = dot(v, dout, 0, 0)
            dscores = (probs * (dprobs - delta)).astype(BF)
            gsort[own, start:end] = (dot(k, dscores, 1, 0) * 0.125).astype(BF)
            gk[:, :end] += dot(q, dscores, 1, 1)
            gv[:, :end] += dot(dout, probs.astype(BF), 1, 1)
        gsort[feats + h * size : feats + (h + 1) * size, :] = (gk[...] * 0.125).astype(BF)
        gsort[2 * feats + h * size : 2 * feats + (h + 1) * size, :] = gv[...].astype(BF)
    sort_out(order_ref, gsort, grads)


def widen(pieces, order):
    count = len(pieces)
    span = pieces[0].shape[1] // 2
    came = order[:count]
    holder = jnp.stack([came, 2 * count - 1 - came], axis=1).reshape(-1)
    place = jnp.argsort(holder)
    flat = jnp.concatenate(pieces, axis=1).reshape(-1, 2 * count, span)
    return [jnp.take(flat, place, axis=1).reshape(flat.shape[0], -1)]


def narrow(wide, order, count):
    feats, seq = wide.shape
    span = seq // (2 * count)
    goes = order[count:]
    holder = jnp.stack([goes, 2 * count - 1 - goes], axis=1).reshape(-1)
    flat = jnp.take(wide.reshape(feats, 2 * count, span), holder, axis=1)
    flat = flat.reshape(feats, count, 2 * span)
    return [flat[:, d] for d in range(count)]


def attention_forward(pieces, order, size):
    parts, rows = len(pieces), pieces[0].shape[1]
    seq = parts * rows
    heads = pieces[0].shape[0] // (3 * size)
    narrow_spans = (rows // 2) % LANES != 0
    ids, given = order, parts
    if narrow_spans:
        pieces, ids, given = widen(pieces, order), jnp.zeros((2,), jnp.int32), 1
    results = pl.pallas_call(
        functools.partial(
            attn_fwd_kernel, parts=given, heads=heads, size=size, block=min(256, seq // 2)
        ),
        in_specs=[SMEM] + [VMEM] * given,
        out_specs=[VMEM] * (given + 3),
        out_shape=[shape((heads * size, pieces[0].shape[1]), BF)] * given
        + [
            shape((3 * heads * size, seq), BF),
            shape((heads * size, seq), BF),
            shape((8 * pl.cdiv(heads, 8), seq), F32),
        ],
        compiler_params=PARAMS,
        name="attn_fwd",
    )(ids, *pieces)
    mixed = results[:given]
    if narrow_spans:
        mixed = narrow(mixed[0], order, parts)
    return mixed, tuple(results[given:])


def attention_backward(pieces, saved, order, size):
    parts, rows = len(pieces), pieces[0].shape[1]
    seq = parts * rows
    heads = pieces[0].shape[0] // size
    narrow_spans = (rows // 2) % LANES != 0
    ids, given = order, parts
    if narrow_spans:
        pieces, ids, given = widen(pieces, order), jnp.zeros((2,), jnp.int32), 1
    grads = pl.pallas_call(
        functools.partial(
            attn_bwd_kernel, parts=given, heads=heads, size=size, block=min(256, seq // 2)
        ),
        in_specs=[SMEM] + [VMEM] * (given + 3),
        out_specs=[VMEM] * given,
        out_shape=[shape((3 * heads * size, pieces[0].shape[1]), BF)] * given,
        scratch_shapes=[
            pltpu.VMEM((heads * size, seq), BF),
            pltpu.VMEM((3 * heads * size, seq), BF),
            pltpu.VMEM((size, seq), F32),
            pltpu.VMEM((size, seq), F32),
        ],
        compiler_params=PARAMS,
        name="attn_bwd",
    )(ids, *pieces, *saved)
    if narrow_spans:
        grads = narrow(grads[0], order, parts)
    return grads


def down_blocks(shards, ratio, depth):
    width = shards * depth
    for f in range(shards):
        for j in range(ratio):
            first = (f * ratio + j) * depth
            yield slice(first, first + depth), slice(f * depth, (f + 1) * depth), j * width


def rest_copies(pack, w_out, w_up, w_down, sems, shards, ratio):
    width = w_out.shape[0]
    depth = width // shards
    hidden = w_up.shape[1]
    out = [pltpu.make_async_copy(pack.at[:, :width], w_out, sems.at[0])]
    up = [pltpu.make_async_copy(pack.at[:, width : width + hidden], w_up, sems.at[1])]
    down = []
    for i, (rows, packed, column) in enumerate(down_blocks(shards, ratio, depth)):
        start = width + hidden + column
        down.append(
            pltpu.make_async_copy(
                pack.at[packed, start : start + width], w_down.at[rows], sems.at[2 + i]
            )
        )
    return out, up, down


def put_pieces(ids_ref, first, pieces, target):
    held = pieces[0].shape[0]
    for d, piece in enumerate(pieces):
        place = pl.multiple_of(ids_ref[first + d] * held, held)
        target[pl.ds(place, held)] = piece[...]


def mlp_kernel(ids_ref, x_ref, vec_ref, bias_ref, pack_ref, *refs, parts, shards, ratio):
    pieces = refs[:parts]
    result_ref, inner_ref, hidden_ref, mixed_ref = refs[parts : parts + 4]
    w_out, w_up, w_down, whole, sems = refs[parts + 4 :]
    width = x_ref.shape[1]
    out, up, down = rest_copies(pack_ref, w_out, w_up, w_down, sems, shards, ratio)
    for copy in out + up + down:
        copy.start()
    put_pieces(ids_ref, parts, pieces, whole)
    mixed_ref[...] = whole[:width]
    out[0].wait()
    inner = x_ref[...].astype(F32) + dot(whole[:width], w_out[...], 0, 0) + vec_ref[5:6]
    inner_ref[...] = inner
    unit, _ = normalised(inner)
    middle = (unit * vec_ref[1:2] + vec_ref[6:7]).astype(BF)
    up[0].wait()
    for copy in down:
        copy.wait()
    total = inner + vec_ref[7:8]
    for start in range(0, w_up.shape[1], width):
        cols = slice(start, start + width)
        hidden = dot(middle, w_up[:, cols], 1, 0) + bias_ref[:, cols]
        hidden_ref[:, cols] = hidden
        act = 0.5 * hidden * (1.0 + jnp.tanh(GELU_C * (hidden + GELU_A * hidden * hidden * hidden)))
        total = total + dot(act.astype(BF), w_down[cols], 1, 0)
    result_ref[...] = total.astype(BF)


def rest_scratch(width, hidden, shards, ratio):
    return [
        pltpu.VMEM((width, width), BF),
        pltpu.VMEM((width, hidden), BF),
        pltpu.VMEM((hidden, width), BF),
    ]


def mlp_forward(ids, x, vec, bias, pack, pieces, shards, ratio):
    parts = len(pieces)
    rows, width = x.shape
    hidden = ratio * width
    return pl.pallas_call(
        functools.partial(mlp_kernel, parts=parts, shards=shards, ratio=ratio),
        in_specs=[SMEM, VMEM, VMEM, VMEM, HBM] + [VMEM] * parts,
        out_specs=[VMEM] * 4,
        out_shape=[
            shape((rows, width), BF),
            shape((rows, width), F32),
            shape((rows, hidden), F32),
            shape((width, rows), BF),
        ],
        scratch_shapes=rest_scratch(width, hidden, shards, ratio)
        + [
            pltpu.VMEM((parts * pieces[0].shape[0], rows), BF),
            pltpu.SemaphoreType.DMA((2 + shards * ratio,)),
        ],
        compiler_params=PARAMS,
        name="mlp_forward",
    )(ids, x, vec, bias, pack, *pieces)


def mlp_back_kernel(
    ids_ref, grad_ref, inner_ref, hidden_ref, vec_ref, pack_ref, *refs, parts, shards, ratio
):
    outs = refs[:parts]
    ginner_ref, gattn_ref, ghid_ref, act_ref, middle_ref, table_ref = refs[parts : parts + 6]
    w_out, w_up, w_down, whole, sems = refs[parts + 6 :]
    width = grad_ref.shape[1]
    out, up, down = rest_copies(pack_ref, w_out, w_up, w_down, sems, shards, ratio)
    for copy in down + up + out:
        copy.start()
    grad_low = grad_ref[...].astype(BF)
    unit, scale = normalised(inner_ref[...])
    middle_ref[...] = (unit * vec_ref[1:2] + vec_ref[6:7]).astype(BF)
    for copy in down:
        copy.wait()
    up[0].wait()
    up_mid = jnp.zeros(unit.shape, F32)
    depth = width // shards
    table_ref[...] = jnp.zeros_like(table_ref)
    for start in range(0, w_up.shape[1], width):
        cols = slice(start, start + width)
        hidden = hidden_ref[:, cols]
        th = jnp.tanh(GELU_C * (hidden + GELU_A * hidden * hidden * hidden))
        act_ref[:, cols] = (0.5 * hidden * (1.0 + th)).astype(BF)
        slope = 0.5 * (1.0 + th) + 0.5 * hidden * (1.0 - th * th) * GELU_C * (
            1.0 + 3.0 * GELU_A * hidden * hidden
        )
        grad_hid = (dot(grad_low, w_down[cols], 1, 1) * slope).astype(BF)
        ghid_ref[:, cols] = grad_hid
        sums = jnp.sum(grad_hid.astype(F32), axis=0, keepdims=True)
        for i in range(width // depth):
            f, j = divmod(start // depth + i, ratio)
            table_ref[8 + j : 9 + j, f * depth : (f + 1) * depth] = sums[:, i * depth : (i + 1) * depth]
        up_mid = up_mid + dot(grad_hid, w_up[:, cols], 1, 1)
    grad_inner = grad_ref[...].astype(F32) + norm_back(unit, scale, up_mid, vec_ref[1:2])
    ginner_ref[...] = grad_inner
    grad_attn = grad_inner.astype(BF)
    gattn_ref[...] = grad_attn
    out[0].wait()
    held = outs[0].shape[0]
    if parts * held != width:
        whole[...] = jnp.zeros_like(whole)
    whole[:width] = dot(w_out[...], grad_attn, 1, 1).astype(BF)
    for d in range(parts):
        outs[d][...] = whole[pl.ds(pl.multiple_of(ids_ref[d] * held, held), held)]
    table_ref[1:2] = jnp.sum(up_mid * unit, axis=0, keepdims=True)
    table_ref[5:6] = jnp.sum(grad_attn.astype(F32), axis=0, keepdims=True)
    table_ref[6:7] = jnp.sum(up_mid, axis=0, keepdims=True)
    table_ref[7:8] = jnp.sum(grad_low.astype(F32), axis=0, keepdims=True)


def mlp_backward(ids, grad, inner, hidden, vec, pack, parts, size, shards, ratio):
    rows, width = inner.shape
    held = pl.cdiv(HEADS, parts) * size
    wide = ratio * width
    results = pl.pallas_call(
        functools.partial(mlp_back_kernel, parts=parts, shards=shards, ratio=ratio),
        in_specs=[SMEM, VMEM, VMEM, VMEM, VMEM, HBM],
        out_specs=[VMEM] * (parts + 6),
        out_shape=[shape((held, rows), BF)] * parts
        + [
            shape((rows, width), F32),
            shape((rows, width), BF),
            shape((rows, wide), BF),
            shape((rows, wide), BF),
            shape((rows, width), BF),
            shape((LANES, width), F32),
        ],
        scratch_shapes=rest_scratch(width, wide, shards, ratio)
        + [
            pltpu.VMEM((parts * held, rows), BF),
            pltpu.SemaphoreType.DMA((2 + shards * ratio,)),
        ],
        compiler_params=PARAMS,
        name="mlp_backward",
    )(ids, grad, inner, hidden, vec, pack)
    return results[:parts], results[parts:]


def write_down(act_ref, glow_ref, pack, start, shards, ratio):
    width = glow_ref.shape[1]
    depth = width // shards
    glow = glow_ref[...].astype(BF)
    for f in range(shards):
        block = dot(act_ref[:, f * ratio * depth : (f + 1) * ratio * depth], glow, 0, 0).astype(BF)
        for j in range(ratio):
            first = start + j * width
            pack[f * depth : (f + 1) * depth, first : first + width] = block[
                j * depth : (j + 1) * depth
            ]


def send_sides(ids_ref, first, pack, start, count, targets, sems, offset, shards):
    depth = pack.shape[0] // shards
    rows = depth // 2
    copies = []
    for side in range(2):
        core = ids_ref[first + shards + side]
        for k in range(shards):
            place = pl.multiple_of(ids_ref[first + k] * depth + core * rows, 16)
            copies.append(
                pltpu.make_async_copy(
                    pack.at[pl.ds(place, rows), start : start + count],
                    targets[side].at[k],
                    sems.at[offset + side * shards + k],
                )
            )
    for copy in copies:
        copy.start()
    return copies


def early_kernel(
    ids_ref, middle_ref, ghid_ref, mixed_ref, gattn_ref, act_ref, glow_ref, *refs, parts, shards, ratio, apart
):
    if apart:
        outs, (scratch, sems) = refs[:2], refs[2:]
    else:
        pack_ref, scratch, sems = refs
    width = middle_ref.shape[1]
    main = (1 + ratio) * width
    copies = []

    def send(columns, i):
        copy = pltpu.make_async_copy(scratch.at[:, columns], pack_ref.at[:, columns], sems.at[i])
        copy.start()
        copies.append(copy)

    scratch[:, :width] = dot(mixed_ref[...], gattn_ref[...], 1, 0).astype(BF)
    for i in range(ratio):
        cols = slice(i * width, (i + 1) * width)
        block = dot(middle_ref[...], ghid_ref[:, cols], 0, 0).astype(BF)
        scratch[:, (i + 1) * width : (i + 2) * width] = block
    if not apart:
        send(slice(0, main), 0)
    write_down(act_ref, glow_ref, scratch, main, shards, ratio)
    if apart:
        copies += send_sides(
            ids_ref, 2 * parts, scratch, 0, main + ratio * width, outs, sems, 0, shards
        )
    else:
        send(slice(main, main + ratio * width), 1)
    for copy in copies:
        copy.wait()


def early_grads(ids, middle, ghid, mixed, gattn, act, grad, parts, shards, ratio, apart):
    width = middle.shape[1]
    main, hidden = (1 + ratio) * width, ratio * width
    rows = width // shards // 2
    side = shape((shards, rows, main + hidden), BF)
    return pl.pallas_call(
        functools.partial(early_kernel, parts=parts, shards=shards, ratio=ratio, apart=apart),
        in_specs=[SMEM] + [VMEM] * 6,
        out_specs=[HBM] * (2 if apart else 1),
        out_shape=[side, side] if apart else [shape((width, main + hidden), BF)],
        scratch_shapes=[
            pltpu.VMEM((width, main + hidden), BF),
            pltpu.SemaphoreType.DMA((2 + 2 * shards,)),
        ],
        compiler_params=PARAMS,
        name="early_grads",
    )(ids, middle, ghid, mixed, gattn, act, grad)


def qkv_back_kernel(
    ids_ref, x_ref, ginner_ref, vec_ref, table_ref, weight_hbm, *refs, parts, shards
):
    pieces, refs = refs[:parts], refs[parts:]
    gx_ref, *outs, weight, whole, pack, sem = refs
    width = x_ref.shape[1]
    main = 3 * width + LANES
    copies = []
    copy = pltpu.make_async_copy(weight_hbm, weight, sem.at[0])
    copy.start()
    held = pieces[0].shape[0] // 3
    padded = parts * held
    for d, piece in enumerate(pieces):
        for b in range(3):
            place = pl.multiple_of(b * padded + ids_ref[parts + d] * held, held)
            whole[pl.ds(place, held)] = piece[b * held : (b + 1) * held]
    unit, scale = normalised(x_ref[...].astype(F32))
    normed = (unit * vec_ref[0:1] + vec_ref[2:3]).T.astype(BF)
    copy.wait()
    up_norm = jnp.zeros((width, x_ref.shape[0]), F32)
    sums = []
    for b in range(3):
        grads = whole[b * padded : b * padded + width]
        cols = slice(b * width, (b + 1) * width)
        up_norm = up_norm + dot(weight[:, cols], grads, 1, 0)
        pack[:, cols] = dot(normed, grads, 1, 1).astype(BF)
        sums.append(jnp.sum(grads.astype(F32), axis=1, keepdims=True))
    up_norm = up_norm.T
    gx_ref[...] = (ginner_ref[...] + norm_back(unit, scale, up_norm, vec_ref[0:1])).astype(BF)
    line = lax.broadcasted_iota(jnp.int32, table_ref.shape, 0)
    table = jnp.where(
        line == 0,
        jnp.sum(up_norm * unit, axis=0, keepdims=True),
        jnp.where(line == 2, jnp.sum(up_norm, axis=0, keepdims=True), table_ref[...]),
    ).T
    lane = lax.broadcasted_iota(jnp.int32, table.shape, 1)
    table = jnp.where(lane == 3, sums[0], jnp.where(lane == 4, sums[2], table))
    pack[:, 3 * width : main] = table.astype(BF)
    copies += send_sides(ids_ref, 2 * parts, pack, 0, main, outs, sem, 1, shards)
    for copy in copies:
        copy.wait()


def qkv_backward(ids, x, ginner, vec, table, weight, pieces, shards):
    parts = len(pieces)
    rows, width = x.shape
    total = 3 * width + LANES
    part = shape((shards, width // shards // 2, total), BF)
    return pl.pallas_call(
        functools.partial(qkv_back_kernel, parts=parts, shards=shards),
        in_specs=[SMEM, VMEM, VMEM, VMEM, VMEM, HBM] + [VMEM] * parts,
        out_specs=[VMEM, HBM, HBM],
        out_shape=[shape((rows, width), BF), part, part],
        scratch_shapes=[
            pltpu.VMEM((width, 3 * width), BF),
            pltpu.VMEM((parts * pieces[0].shape[0], rows), BF),
            pltpu.VMEM((width, total), BF),
            pltpu.SemaphoreType.DMA((1 + 2 * shards,)),
        ],
        compiler_params=PARAMS,
        name="qkv_backward",
    )(ids, x, ginner, vec, table, weight, *pieces)


def layer_forward(x, packs, rest, ids, order, parts, size, shards, ratio, back=None):
    sent, weight, vec = qkv_project(ids, x, packs, parts, size, shards)
    width = x.shape[1]
    depth = width // shards
    bias = vec[8 : 8 + ratio].reshape(ratio, shards, depth).transpose(1, 0, 2).reshape(1, -1)
    received = exchange(sent)
    returned = None
    if back is not None:
        *received, back = lax.optimization_barrier((*received, back))
        returned = return_rows(back, 0)
    mixed, attn_saved = attention_forward(received, order, size)
    received = exchange(mixed)
    if back is not None:
        tied = lax.optimization_barrier((*received, *returned))
        received, returned = tied[:parts], tied[parts:]
    result, inner, hidden, mixed = mlp_forward(
        ids, x, vec, bias, rest, received, shards, ratio
    )
    return result, (x, weight, vec, attn_saved, inner, hidden, mixed), returned


def layer_backward(saved, grad, rest, ids, order, parts, size, shards, ratio, layer, background):
    x, weight, vec, attn_saved, inner, hidden, mixed = saved
    last = layer == 0
    column = (1 + ratio) * x.shape[1]
    sent, (ginner, gattn, ghid, act, middle, table) = mlp_backward(
        ids, grad, inner, hidden, vec, rest, parts, size, shards, ratio
    )
    received = exchange(background.slot("AD", sent))
    early = early_grads(ids, middle, ghid, mixed, gattn, act, grad, parts, shards, ratio, last)
    tied = lax.optimization_barrier((*received, *early))
    received, early = tied[:parts], tied[parts:]
    if last:
        first = background.add("B", permuted_task(*early, layer, background, column))
    else:
        first = background.add("C", offloaded_task(*early, layer, background, column, 1))
    sent = attention_backward(received, attn_saved, order, size)
    if last:
        sent = background.slot("BCD", sent)
    received = exchange(sent)
    if last:
        received = background.slot("CD", received)
    results = qkv_backward(ids, x, ginner, vec, table, weight, received, shards)
    grad_x, *late = lax.optimization_barrier(tuple(results))
    if last:
        (grad_x,) = background.slot("ABCD", [grad_x])
        second = background.add("A", permuted_task(*late, layer, background, None))
    else:
        second = background.add("D", permuted_task(*late, layer, background, None, 1, 4))
    return grad_x, first, second


def blocks_to_columns(value, parts):
    depth = value.shape[0] // parts
    return [value[i * depth : (i + 1) * depth] for i in range(parts)]


def split_layers(pack, core):
    rows = pack.shape[0] // 2
    first, second = pack[:rows], pack[rows:]
    other = lax.ppermute(jnp.where(core == 0, second, first), "section", [(0, 1), (1, 0)])
    return jnp.where(core == 0, first, other), jnp.where(core == 0, other, second)


def gather(part):
    return lax.all_gather(part, SHARDS, axis=0, tiled=True)


def across(value, bit):
    count = lax.axis_size("fsdp")
    return lax.ppermute(value, "fsdp", [(i, i ^ bit) for i in range(count)])


def swap_cores(value):
    return lax.ppermute(value, "section", [(0, 1), (1, 0)])


def gather_pieces(part):
    rows = part.shape[0] // 2
    by_x, by_y = across(part, 1), across(part, 2)
    pieces = [part, by_x, by_y, across(by_x[:rows], 2), across(by_y[rows:], 1)]
    return pieces + [swap_cores(piece) for piece in pieces]


class Background:
    def __init__(self):
        self.tasks = []

    def add(self, lane, task):
        entry = {"lane": lane, "task": task, "result": None}
        entry["flight"] = next(task)
        self.tasks.append(entry)
        return entry

    def slot(self, lanes, values=()):
        waiting = [e for e in self.tasks if e["flight"] is not None and e["lane"] in lanes]
        flat = list(values)
        for entry in waiting:
            flat += entry["flight"]
        if len(flat) > 0:
            flat = list(lax.optimization_barrier(tuple(flat)))
        values, flat = flat[: len(values)], flat[len(values) :]
        for entry in waiting:
            count = len(entry["flight"])
            held, flat = flat[:count], flat[count:]
            try:
                entry["flight"] = entry["task"].send(held)
            except StopIteration as stop:
                entry["flight"], entry["result"] = None, stop.value
        return values

    def finish(self):
        while any(entry["flight"] is not None for entry in self.tasks):
            self.slot("ABCD")


def idle(values, slots):
    for _ in range(slots):
        values = yield list(values)
    return values


def permuted_task(keep, send, layer, background, column, hold=0, before=0):
    (received,) = yield [swap_cores(send)]
    rows = keep.shape[1] // 2

    def summed(slots, side):
        return sum_pair(keep[slots, side], received[slots, side])

    top, low = slice(0, rows), slice(rows, 2 * rows)
    by_x, by_y = yield [
        across(summed(slice(1, 4, 2), top), 1),
        across(summed(slice(2, 4), low), 2),
    ]
    by_x, by_y = yield from idle([by_x, by_y], hold)
    first = sum_pair(summed(slice(0, 4, 2), top), by_x)
    second = sum_pair(summed(slice(0, 2), low), by_y)
    by_y, by_x = yield [across(first[1], 2), across(second[1], 1)]
    value = jnp.concatenate([sum_pair(first[0], by_y), sum_pair(second[0], by_x)])
    (value,) = yield from idle([value], before)
    return (yield from split_task(value, layer, background, column))


def offloaded_task(pack, layer, background, column, after):
    value = lax.psum_scatter(pack, SHARDS, scatter_dimension=0, tiled=True)
    (value,) = yield [value]
    (value,) = yield from idle([value], after)
    return (yield from split_task(value, layer, background, column))


def split_task(value, layer, background, column):
    if column is None:
        return (yield from ctx_task(value, layer))
    other = background.add("D", ctx_task(value[:, column:], layer, 1))
    mine = yield from ctx_task(value[:, :column], layer)
    return mine, other


def ctx_task(value, layer, before=0):
    (value,) = yield from idle([value], before)
    if lax.axis_size("ctx") == 4:
        index = lax.axis_index("ctx")
        (received,) = yield [lax.ppermute(value, "ctx", [(0, 1), (3, 2)])]
        value = sum_pair(value, received)
        (received,) = yield [lax.ppermute(value, "ctx", [(1, 2), (2, 1)])]
        value = sum_pair(value, received)
        (received,) = yield [lax.ppermute(value, "ctx", [(1, 0), (2, 3)])]
        value = jnp.where((index == 0) | (index == 3), received, value)
    else:
        value = lax.psum(value, "ctx")
    (other,) = yield [lax.ppermute(value, "section", [(1 - layer, layer)])]
    return value, other


def return_task(value, layer, pause):
    (value,) = yield from idle([value], pause)
    flight = yield return_rows(value, layer)
    return flight


def sum_pair(a, b):
    return (a.astype(F32) + b.astype(F32)).astype(BF)


def body(
    tokens, cotangent, span_order, w_qkv, w_out, w_up, w_down, norm_gains, bias_rows, bias_hidden
):
    core = lax.axis_index("section")
    ctx = lax.axis_size("ctx")
    cores = lax.axis_size("section")
    shards = lax.axis_size("fsdp")
    half = ctx // cores
    base = lax.axis_index("ctx") // half
    member = core * half + lax.axis_index("ctx") % half
    depth = w_qkv.shape[1]
    width = depth * shards
    ratio = bias_hidden.shape[1] // depth
    size = width // HEADS
    gain_count, shift_count = norm_gains.shape[1], bias_rows.shape[1]

    steps = jnp.arange(ctx, dtype=jnp.int32)
    came, goes = (member - steps) % ctx, (member + steps) % ctx
    shard = lax.axis_index("fsdp")
    slots = [shard ^ k for k in range(shards)] + [core, 1 - core]
    ids = jnp.concatenate([goes, came, jnp.stack(slots)]).astype(jnp.int32)
    order = jnp.concatenate([span_order[came], span_order[goes]])

    small = jnp.concatenate([norm_gains[0], bias_rows[0], bias_hidden[0].reshape(ratio, depth)]).T
    small = jnp.pad(small, ((0, 0), (0, LANES - small.shape[1])))
    first = jnp.concatenate([w_qkv[0], small], axis=1)
    rest = jnp.concatenate([w_out[0], w_up[0]] + blocks_to_columns(w_down[0], ratio), axis=1)
    first0, first1 = split_layers(first, core)
    x = bring_rows(tokens[:, 0], core, base)
    rest0, rest1 = split_layers(rest, core)
    first0, first1 = gather_pieces(first0), gather_pieces(first1)
    rest0, rest1 = gather(rest0), gather(rest1)
    sizes = (ids, order, ctx, size, shards, ratio)
    out0, saved0, _ = layer_forward(x, first0, rest0, *sizes)
    late_cot, out0 = lax.optimization_barrier((cotangent[:, 0], out0))
    out1, saved1, back_out0 = layer_forward(out0, first1, rest1, *sizes, out0)
    cot = bring_rows(late_cot, core, base)
    background = Background()
    grad1, early1, late1 = layer_backward(saved1, cot, rest1, *sizes, 1, background)
    back1 = background.add("A", return_task(jnp.concatenate([out1, grad1], axis=1), 1, 0))
    grad0, early0, late0 = layer_backward(saved0, grad1, rest0, *sizes, 0, background)
    back0 = background.add("A", return_task(grad0, 0, 5))
    background.finish()

    def chosen(values0, values1):
        return jnp.stack([jnp.where(core == 0, a, b) for a, b in zip(values0, values1)])

    layer_outputs = chosen(back_out0, [value[:, :width] for value in back1["result"]])
    input_grads = chosen(
        back0["result"], [value[:, width:] for value in back1["result"]]
    ).astype(F32)

    def joined(pair0, pair1):
        return jnp.where(
            core == 0,
            jnp.concatenate([pair0[0], pair0[1]]),
            jnp.concatenate([pair1[1], pair1[0]]),
        ).astype(F32)

    (up0, down0), (up1, down1) = early0["result"], early1["result"]
    early = joined(up0, up1)
    late = joined(late0["result"], late1["result"])
    down = joined(down0["result"], down1["result"])
    table = late[:, 3 * width :].T
    return (
        layer_outputs[None, :, None],
        input_grads[None, :, None],
        late[None, :, : 3 * width],
        early[None, :, :width],
        early[None, :, width:],
        jnp.concatenate([down[:, j * width : (j + 1) * width] for j in range(ratio)])[None],
        table[None, :gain_count],
        table[None, gain_count : gain_count + shift_count],
        table[gain_count + shift_count : gain_count + shift_count + ratio].reshape(1, -1),
    )


def solution(mesh):
    return jax.shard_map(
        body,
        mesh=mesh,
        in_specs=(
            P(None, "fsdp", "ctx", None),
            P(None, "fsdp", "ctx", None),
            P(),
            P("section", "fsdp", None),
            P("section", "fsdp", None),
            P("section", "fsdp", None),
            P("section", "fsdp", None),
            P("section", None, "fsdp"),
            P("section", None, "fsdp"),
            P("section", "fsdp"),
        ),
        out_specs=(
            P("section", None, "fsdp", "ctx", None),
            P("section", None, "fsdp", "ctx", None),
            P("section", "fsdp", None),
            P("section", "fsdp", None),
            P("section", "fsdp", None),
            P("section", "fsdp", None),
            P("section", None, "fsdp"),
            P("section", None, "fsdp"),
            P("section", "fsdp"),
        ),
        check_vma=False,
    )
```

```python
import functools

import jax
import jax.numpy as jnp
from jax import lax
from jax.experimental import pallas as pl
from jax.experimental.pallas import tpu as pltpu
from jax.sharding import PartitionSpec as P

HEADS = 12
EPS = 1e-05
GELU_C = 0.7978845608
GELU_A = 0.044715
LANES = 128
BF = jnp.bfloat16
F32 = jnp.float32
VMEM = pl.BlockSpec(memory_space=pltpu.VMEM)
SMEM = pl.BlockSpec(memory_space=pltpu.SMEM)
HBM = pl.BlockSpec(memory_space=pl.ANY)
PARAMS = pltpu.CompilerParams(vmem_limit_bytes=56 * 1024 * 1024)
GROUP = ("section", "ctx")
SHARDS = ("fsdp", "section")


def dot(a, b, ca, cb):
    return lax.dot_general(a, b, (((ca,), (cb,)), ((), ())), preferred_element_type=F32)


def shape(dims, dtype):
    return jax.ShapeDtypeStruct(dims, dtype)


def place_of(core, ctx_index):
    return core * lax.axis_size("ctx") + ctx_index


def exchange(pieces):
    ctx, cores = lax.axis_size("ctx"), lax.axis_size("section")
    half = ctx // cores
    moved = [pieces[0]]
    for d in range(1, ctx):
        pairs = []
        for base in range(cores):
            for g in range(ctx):
                t = (g + d) % ctx
                pairs.append(
                    (
                        place_of(g // half, base * half + g % half),
                        place_of(t // half, base * half + t % half),
                    )
                )
        moved.append(lax.ppermute(pieces[d], GROUP, pairs))
    return moved


def bring_rows(both, core, base):
    ctx, cores = lax.axis_size("ctx"), lax.axis_size("section")
    half = ctx // cores
    pairs = [
        (place_of(c, c * half + i), place_of(c, (1 - c) * half + i))
        for c in range(cores)
        for i in range(half)
    ]
    received = lax.ppermute(jnp.where(core == 0, both[1], both[0]), GROUP, pairs)
    own = jnp.where(core == 0, both[0], both[1])
    return jnp.where(core == base, own, received)


def return_rows(value, layer):
    ctx, cores = lax.axis_size("ctx"), lax.axis_size("section")
    half = ctx // cores
    return [
        lax.ppermute(
            value,
            GROUP,
            [(place_of(z // half, m * half + z % half), place_of(layer, z)) for z in range(ctx)],
        )
        for m in range(cores)
    ]


def normalised(values):
    centred = values - jnp.mean(values, axis=-1, keepdims=True)
    scale = lax.rsqrt(jnp.mean(centred * centred, axis=-1, keepdims=True) + EPS)
    return centred * scale, scale


def norm_back(unit, scale, upstream, gain):
    w = upstream * gain
    return (
        w - jnp.mean(w, axis=-1, keepdims=True) - unit * jnp.mean(w * unit, axis=-1, keepdims=True)
    ) * scale


def piece_places(ids_ref, parts, depth, slots):
    first = 2 * parts
    rows = depth // 2
    places = []
    for side in range(2):
        core = ids_ref[first + slots + side]
        for slot, start, count in (
            (0, 0, rows),
            (1, 0, rows),
            (2, 0, rows),
            (3, 0, rows // 2),
            (3, rows // 2, rows // 2),
        ):
            place = ids_ref[first + slot] * depth + core * rows + start
            places.append((pl.multiple_of(place, 16), count))
    return places


def qkv_kernel(ids_ref, x_ref, *refs, parts, size, shards):
    packs, refs = refs[:10], refs[10:]
    outs, (weight_ref, vec_ref), refs = refs[:parts], refs[parts : parts + 2], refs[parts + 2 :]
    weight, small, whole, sems = refs
    width = x_ref.shape[1]
    copies = []
    for i, (place, count) in enumerate(piece_places(ids_ref, parts, width // shards, shards)):
        for j, target, cols in (
            (0, small, slice(3 * width, 3 * width + LANES)),
            (1, weight, slice(0, 3 * width)),
        ):
            copies.append(
                pltpu.make_async_copy(
                    packs[i].at[:, cols], target.at[pl.ds(place, count)], sems.at[2 * i + j]
                )
            )
    for copy in copies:
        copy.start()
    unit, _ = normalised(x_ref[...].astype(F32))
    for copy in copies:
        copy.wait()
    keep = pltpu.make_async_copy(weight, weight_ref, sems.at[20])
    keep.start()
    vec = small[...].astype(F32).T
    vec_ref[...] = vec[:16]
    normed = (unit * vec[0:1] + vec[2:3]).astype(BF)
    held = outs[0].shape[0] // 3
    if parts * held != width:
        whole[...] = jnp.zeros_like(whole)
    for b in range(3):
        block = dot(normed, weight[:, b * width : (b + 1) * width], 1, 0)
        if b == 0:
            block = block + vec[3:4]
        if b == 2:
            block = block + vec[4:5]
        whole[b * parts * held : b * parts * held + width] = block.T.astype(BF)
    for d in range(parts):
        for b in range(3):
            first = pl.multiple_of(b * parts * held + ids_ref[d] * held, size)
            outs[d][b * held : (b + 1) * held] = whole[pl.ds(first, held)]
    keep.wait()


def qkv_project(ids, x, packs, parts, size, shards):
    rows, width = x.shape
    held = pl.cdiv(HEADS, parts) * size
    results = pl.pallas_call(
        functools.partial(qkv_kernel, parts=parts, size=size, shards=shards),
        in_specs=[SMEM, VMEM] + [HBM] * 10,
        out_specs=[VMEM] * parts + [HBM, VMEM],
        out_shape=[shape((3 * held, rows), BF)] * parts
        + [shape((width, 3 * width), BF), shape((16, width), F32)],
        scratch_shapes=[
            pltpu.VMEM((width, 3 * width), BF),
            pltpu.VMEM((width, LANES), BF),
            pltpu.VMEM((3 * parts * held, rows), BF),
            pltpu.SemaphoreType.DMA((21,)),
        ],
        compiler_params=PARAMS,
        name="qkv_project",
    )(ids, x, *packs)
    return results[:parts], results[parts], results[parts + 1]


def spans_of(order_ref, which, count, span):
    first = order_ref[which]
    return (
        (0, pl.multiple_of(first * span, span)),
        (1, pl.multiple_of((2 * count - 1 - first) * span, span)),
    )


def causal(scores, width, fill):
    depth = scores.shape[0]
    keys = lax.broadcasted_iota(jnp.int32, (width, width), 0)
    rows = lax.broadcasted_iota(jnp.int32, (width, width), 1)
    last = jnp.where(keys <= rows, scores[depth - width :], fill)
    if depth == width:
        return last
    return jnp.concatenate([scores[: depth - width], last], axis=0)


def sort_in(order_ref, pieces, target):
    count = len(pieces)
    span = pieces[0].shape[1] // 2
    for d in range(count):
        for side, place in spans_of(order_ref, d, count, span):
            target[:, pl.ds(place, span)] = pieces[d][:, side * span : (side + 1) * span]


def sort_out(order_ref, source, pieces):
    count = len(pieces)
    span = pieces[0].shape[1] // 2
    for d in range(count):
        for side, place in spans_of(order_ref, count + d, count, span):
            pieces[d][:, side * span : (side + 1) * span] = source[:, pl.ds(place, span)]


def attn_fwd_kernel(order_ref, *refs, parts, heads, size, block):
    pieces, mixed, (sorted_ref, out_ref, lse_ref) = refs[:parts], refs[parts : 2 * parts], refs[2 * parts :]
    feats = heads * size
    seq = sorted_ref.shape[1]
    sort_in(order_ref, pieces, sorted_ref)
    lse_ref[...] = jnp.zeros_like(lse_ref)
    for h in range(heads):
        for start in range(0, seq, block):
            end = start + block
            q = sorted_ref[h * size : (h + 1) * size, start:end]
            k = sorted_ref[feats + h * size : feats + (h + 1) * size, :end]
            v = sorted_ref[2 * feats + h * size : 2 * feats + (h + 1) * size, :end]
            scores = causal(dot(k, q, 0, 0) * 0.125, block, -1e30)
            top = jnp.max(scores, axis=0, keepdims=True)
            weights = jnp.exp(scores - top)
            total = jnp.sum(weights, axis=0, keepdims=True)
            mixed_part = dot(v, weights.astype(BF), 1, 0) / total
            out_ref[h * size : (h + 1) * size, start:end] = mixed_part.astype(BF)
            lse_ref[h : h + 1, start:end] = top + jnp.log(total)
    sort_out(order_ref, out_ref, mixed)


def attn_bwd_kernel(order_ref, *refs, parts, heads, size, block):
    pieces, (sorted_ref, out_ref, lse_ref) = refs[:parts], refs[parts : parts + 3]
    grads, (dsort, gsort, gk, gv) = refs[parts + 3 : 2 * parts + 3], refs[2 * parts + 3 :]
    feats = heads * size
    seq = sorted_ref.shape[1]
    sort_in(order_ref, pieces, dsort)
    for h in range(heads):
        own = slice(h * size, (h + 1) * size)
        gk[...] = jnp.zeros_like(gk)
        gv[...] = jnp.zeros_like(gv)
        for start in range(0, seq, block):
            end = start + block
            q = sorted_ref[own, start:end]
            k = sorted_ref[feats + h * size : feats + (h + 1) * size, :end]
            v = sorted_ref[2 * feats + h * size : 2 * feats + (h + 1) * size, :end]
            dout = dsort[own, start:end]
            delta = jnp.sum(
                dout.astype(F32) * out_ref[own, start:end].astype(F32), axis=0, keepdims=True
            )
            scores = dot(k, q, 0, 0) * 0.125 - lse_ref[h : h + 1, start:end]
            probs = jnp.exp(causal(scores, block, -1e30))
            dprobs = dot(v, dout, 0, 0)
            dscores = (probs * (dprobs - delta)).astype(BF)
            gsort[own, start:end] = (dot(k, dscores, 1, 0) * 0.125).astype(BF)
            gk[:, :end] += dot(q, dscores, 1, 1)
            gv[:, :end] += dot(dout, probs.astype(BF), 1, 1)
        gsort[feats + h * size : feats + (h + 1) * size, :] = (gk[...] * 0.125).astype(BF)
        gsort[2 * feats + h * size : 2 * feats + (h + 1) * size, :] = gv[...].astype(BF)
    sort_out(order_ref, gsort, grads)


def widen(pieces, order):
    count = len(pieces)
    span = pieces[0].shape[1] // 2
    came = order[:count]
    holder = jnp.stack([came, 2 * count - 1 - came], axis=1).reshape(-1)
    place = jnp.argsort(holder)
    flat = jnp.concatenate(pieces, axis=1).reshape(-1, 2 * count, span)
    return [jnp.take(flat, place, axis=1).reshape(flat.shape[0], -1)]


def narrow(wide, order, count):
    feats, seq = wide.shape
    span = seq // (2 * count)
    goes = order[count:]
    holder = jnp.stack([goes, 2 * count - 1 - goes], axis=1).reshape(-1)
    flat = jnp.take(wide.reshape(feats, 2 * count, span), holder, axis=1)
    flat = flat.reshape(feats, count, 2 * span)
    return [flat[:, d] for d in range(count)]


def attention_forward(pieces, order, size):
    parts, rows = len(pieces), pieces[0].shape[1]
    seq = parts * rows
    heads = pieces[0].shape[0] // (3 * size)
    narrow_spans = (rows // 2) % LANES != 0
    ids, given = order, parts
    if narrow_spans:
        pieces, ids, given = widen(pieces, order), jnp.zeros((2,), jnp.int32), 1
    results = pl.pallas_call(
        functools.partial(
            attn_fwd_kernel, parts=given, heads=heads, size=size, block=min(256, seq // 2)
        ),
        in_specs=[SMEM] + [VMEM] * given,
        out_specs=[VMEM] * (given + 3),
        out_shape=[shape((heads * size, pieces[0].shape[1]), BF)] * given
        + [
            shape((3 * heads * size, seq), BF),
            shape((heads * size, seq), BF),
            shape((8 * pl.cdiv(heads, 8), seq), F32),
        ],
        compiler_params=PARAMS,
        name="attn_fwd",
    )(ids, *pieces)
    mixed = results[:given]
    if narrow_spans:
        mixed = narrow(mixed[0], order, parts)
    return mixed, tuple(results[given:])


def attention_backward(pieces, saved, order, size):
    parts, rows = len(pieces), pieces[0].shape[1]
    seq = parts * rows
    heads = pieces[0].shape[0] // size
    narrow_spans = (rows // 2) % LANES != 0
    ids, given = order, parts
    if narrow_spans:
        pieces, ids, given = widen(pieces, order), jnp.zeros((2,), jnp.int32), 1
    grads = pl.pallas_call(
        functools.partial(
            attn_bwd_kernel, parts=given, heads=heads, size=size, block=min(256, seq // 2)
        ),
        in_specs=[SMEM] + [VMEM] * (given + 3),
        out_specs=[VMEM] * given,
        out_shape=[shape((3 * heads * size, pieces[0].shape[1]), BF)] * given,
        scratch_shapes=[
            pltpu.VMEM((heads * size, seq), BF),
            pltpu.VMEM((3 * heads * size, seq), BF),
            pltpu.VMEM((size, seq), F32),
            pltpu.VMEM((size, seq), F32),
        ],
        compiler_params=PARAMS,
        name="attn_bwd",
    )(ids, *pieces, *saved)
    if narrow_spans:
        grads = narrow(grads[0], order, parts)
    return grads


def down_blocks(shards, ratio, depth):
    width = shards * depth
    for f in range(shards):
        for j in range(ratio):
            first = (f * ratio + j) * depth
            yield slice(first, first + depth), slice(f * depth, (f + 1) * depth), j * width


def rest_copies(pack, w_out, w_up, w_down, sems, shards, ratio):
    width = w_out.shape[0]
    depth = width // shards
    hidden = w_up.shape[1]
    out = [pltpu.make_async_copy(pack.at[:, :width], w_out, sems.at[0])]
    up = [pltpu.make_async_copy(pack.at[:, width : width + hidden], w_up, sems.at[1])]
    down = []
    for i, (rows, packed, column) in enumerate(down_blocks(shards, ratio, depth)):
        start = width + hidden + column
        down.append(
            pltpu.make_async_copy(
                pack.at[packed, start : start + width], w_down.at[rows], sems.at[2 + i]
            )
        )
    return out, up, down


def put_pieces(ids_ref, first, pieces, target):
    held = pieces[0].shape[0]
    for d, piece in enumerate(pieces):
        place = pl.multiple_of(ids_ref[first + d] * held, held)
        target[pl.ds(place, held)] = piece[...]


def mlp_kernel(ids_ref, x_ref, vec_ref, bias_ref, pack_ref, *refs, parts, shards, ratio):
    pieces = refs[:parts]
    result_ref, inner_ref, hidden_ref, mixed_ref = refs[parts : parts + 4]
    w_out, w_up, w_down, whole, sems = refs[parts + 4 :]
    width = x_ref.shape[1]
    out, up, down = rest_copies(pack_ref, w_out, w_up, w_down, sems, shards, ratio)
    for copy in out + up + down:
        copy.start()
    put_pieces(ids_ref, parts, pieces, whole)
    mixed_ref[...] = whole[:width]
    out[0].wait()
    inner = x_ref[...].astype(F32) + dot(whole[:width], w_out[...], 0, 0) + vec_ref[5:6]
    inner_ref[...] = inner
    unit, _ = normalised(inner)
    middle = (unit * vec_ref[1:2] + vec_ref[6:7]).astype(BF)
    up[0].wait()
    for copy in down:
        copy.wait()
    total = inner + vec_ref[7:8]
    for start in range(0, w_up.shape[1], width):
        cols = slice(start, start + width)
        hidden = dot(middle, w_up[:, cols], 1, 0) + bias_ref[:, cols]
        hidden_ref[:, cols] = hidden
        act = 0.5 * hidden * (1.0 + jnp.tanh(GELU_C * (hidden + GELU_A * hidden * hidden * hidden)))
        total = total + dot(act.astype(BF), w_down[cols], 1, 0)
    result_ref[...] = total.astype(BF)


def rest_scratch(width, hidden, shards, ratio):
    return [
        pltpu.VMEM((width, width), BF),
        pltpu.VMEM((width, hidden), BF),
        pltpu.VMEM((hidden, width), BF),
    ]


def mlp_forward(ids, x, vec, bias, pack, pieces, shards, ratio):
    parts = len(pieces)
    rows, width = x.shape
    hidden = ratio * width
    return pl.pallas_call(
        functools.partial(mlp_kernel, parts=parts, shards=shards, ratio=ratio),
        in_specs=[SMEM, VMEM, VMEM, VMEM, HBM] + [VMEM] * parts,
        out_specs=[VMEM] * 4,
        out_shape=[
            shape((rows, width), BF),
            shape((rows, width), F32),
            shape((rows, hidden), F32),
            shape((width, rows), BF),
        ],
        scratch_shapes=rest_scratch(width, hidden, shards, ratio)
        + [
            pltpu.VMEM((parts * pieces[0].shape[0], rows), BF),
            pltpu.SemaphoreType.DMA((2 + shards * ratio,)),
        ],
        compiler_params=PARAMS,
        name="mlp_forward",
    )(ids, x, vec, bias, pack, *pieces)


def mlp_back_kernel(
    ids_ref, grad_ref, inner_ref, hidden_ref, vec_ref, pack_ref, *refs, parts, shards, ratio
):
    outs = refs[:parts]
    ginner_ref, gattn_ref, ghid_ref, act_ref, middle_ref, table_ref = refs[parts : parts + 6]
    w_out, w_up, w_down, whole, sems = refs[parts + 6 :]
    width = grad_ref.shape[1]
    out, up, down = rest_copies(pack_ref, w_out, w_up, w_down, sems, shards, ratio)
    for copy in down + up + out:
        copy.start()
    grad_low = grad_ref[...].astype(BF)
    unit, scale = normalised(inner_ref[...])
    middle_ref[...] = (unit * vec_ref[1:2] + vec_ref[6:7]).astype(BF)
    for copy in down:
        copy.wait()
    up[0].wait()
    up_mid = jnp.zeros(unit.shape, F32)
    depth = width // shards
    table_ref[...] = jnp.zeros_like(table_ref)
    for start in range(0, w_up.shape[1], width):
        cols = slice(start, start + width)
        hidden = hidden_ref[:, cols]
        th = jnp.tanh(GELU_C * (hidden + GELU_A * hidden * hidden * hidden))
        act_ref[:, cols] = (0.5 * hidden * (1.0 + th)).astype(BF)
        slope = 0.5 * (1.0 + th) + 0.5 * hidden * (1.0 - th * th) * GELU_C * (
            1.0 + 3.0 * GELU_A * hidden * hidden
        )
        grad_hid = (dot(grad_low, w_down[cols], 1, 1) * slope).astype(BF)
        ghid_ref[:, cols] = grad_hid
        sums = jnp.sum(grad_hid.astype(F32), axis=0, keepdims=True)
        for i in range(width // depth):
            f, j = divmod(start // depth + i, ratio)
            table_ref[8 + j : 9 + j, f * depth : (f + 1) * depth] = sums[:, i * depth : (i + 1) * depth]
        up_mid = up_mid + dot(grad_hid, w_up[:, cols], 1, 1)
    grad_inner = grad_ref[...].astype(F32) + norm_back(unit, scale, up_mid, vec_ref[1:2])
    ginner_ref[...] = grad_inner
    grad_attn = grad_inner.astype(BF)
    gattn_ref[...] = grad_attn
    out[0].wait()
    held = outs[0].shape[0]
    if parts * held != width:
        whole[...] = jnp.zeros_like(whole)
    whole[:width] = dot(w_out[...], grad_attn, 1, 1).astype(BF)
    for d in range(parts):
        outs[d][...] = whole[pl.ds(pl.multiple_of(ids_ref[d] * held, held), held)]
    table_ref[1:2] = jnp.sum(up_mid * unit, axis=0, keepdims=True)
    table_ref[5:6] = jnp.sum(grad_attn.astype(F32), axis=0, keepdims=True)
    table_ref[6:7] = jnp.sum(up_mid, axis=0, keepdims=True)
    table_ref[7:8] = jnp.sum(grad_low.astype(F32), axis=0, keepdims=True)


def mlp_backward(ids, grad, inner, hidden, vec, pack, parts, size, shards, ratio):
    rows, width = inner.shape
    held = pl.cdiv(HEADS, parts) * size
    wide = ratio * width
    results = pl.pallas_call(
        functools.partial(mlp_back_kernel, parts=parts, shards=shards, ratio=ratio),
        in_specs=[SMEM, VMEM, VMEM, VMEM, VMEM, HBM],
        out_specs=[VMEM] * (parts + 6),
        out_shape=[shape((held, rows), BF)] * parts
        + [
            shape((rows, width), F32),
            shape((rows, width), BF),
            shape((rows, wide), BF),
            shape((rows, wide), BF),
            shape((rows, width), BF),
            shape((LANES, width), F32),
        ],
        scratch_shapes=rest_scratch(width, wide, shards, ratio)
        + [
            pltpu.VMEM((parts * held, rows), BF),
            pltpu.SemaphoreType.DMA((2 + shards * ratio,)),
        ],
        compiler_params=PARAMS,
        name="mlp_backward",
    )(ids, grad, inner, hidden, vec, pack)
    return results[:parts], results[parts:]


def write_down(act_ref, glow_ref, pack, start, shards, ratio):
    width = glow_ref.shape[1]
    depth = width // shards
    glow = glow_ref[...].astype(BF)
    for f in range(shards):
        block = dot(act_ref[:, f * ratio * depth : (f + 1) * ratio * depth], glow, 0, 0).astype(BF)
        for j in range(ratio):
            first = start + j * width
            pack[f * depth : (f + 1) * depth, first : first + width] = block[
                j * depth : (j + 1) * depth
            ]


def send_sides(ids_ref, first, pack, start, count, targets, sems, offset, shards):
    depth = pack.shape[0] // shards
    rows = depth // 2
    copies = []
    for side in range(2):
        core = ids_ref[first + shards + side]
        for k in range(shards):
            place = pl.multiple_of(ids_ref[first + k] * depth + core * rows, 16)
            copies.append(
                pltpu.make_async_copy(
                    pack.at[pl.ds(place, rows), start : start + count],
                    targets[side].at[k],
                    sems.at[offset + side * shards + k],
                )
            )
    for copy in copies:
        copy.start()
    return copies


def early_kernel(
    ids_ref, middle_ref, ghid_ref, mixed_ref, gattn_ref, act_ref, glow_ref, *refs, parts, shards, ratio, apart
):
    if apart:
        outs, (scratch, sems) = refs[:2], refs[2:]
    else:
        pack_ref, scratch, sems = refs
    width = middle_ref.shape[1]
    main = (1 + ratio) * width
    copies = []

    def send(columns, i):
        copy = pltpu.make_async_copy(scratch.at[:, columns], pack_ref.at[:, columns], sems.at[i])
        copy.start()
        copies.append(copy)

    scratch[:, :width] = dot(mixed_ref[...], gattn_ref[...], 1, 0).astype(BF)
    for i in range(ratio):
        cols = slice(i * width, (i + 1) * width)
        block = dot(middle_ref[...], ghid_ref[:, cols], 0, 0).astype(BF)
        scratch[:, (i + 1) * width : (i + 2) * width] = block
    if not apart:
        send(slice(0, main), 0)
    write_down(act_ref, glow_ref, scratch, main, shards, ratio)
    if apart:
        copies += send_sides(
            ids_ref, 2 * parts, scratch, 0, main + ratio * width, outs, sems, 0, shards
        )
    else:
        send(slice(main, main + ratio * width), 1)
    for copy in copies:
        copy.wait()


def early_grads(ids, middle, ghid, mixed, gattn, act, grad, parts, shards, ratio, apart):
    width = middle.shape[1]
    main, hidden = (1 + ratio) * width, ratio * width
    rows = width // shards // 2
    side = shape((shards, rows, main + hidden), BF)
    return pl.pallas_call(
        functools.partial(early_kernel, parts=parts, shards=shards, ratio=ratio, apart=apart),
        in_specs=[SMEM] + [VMEM] * 6,
        out_specs=[HBM] * (2 if apart else 1),
        out_shape=[side, side] if apart else [shape((width, main + hidden), BF)],
        scratch_shapes=[
            pltpu.VMEM((width, main + hidden), BF),
            pltpu.SemaphoreType.DMA((2 + 2 * shards,)),
        ],
        compiler_params=PARAMS,
        name="early_grads",
    )(ids, middle, ghid, mixed, gattn, act, grad)


def qkv_back_kernel(
    ids_ref, x_ref, ginner_ref, vec_ref, table_ref, weight_hbm, *refs, parts, shards
):
    pieces, refs = refs[:parts], refs[parts:]
    gx_ref, *outs, weight, whole, pack, sem = refs
    width = x_ref.shape[1]
    main = 3 * width + LANES
    copies = []
    copy = pltpu.make_async_copy(weight_hbm, weight, sem.at[0])
    copy.start()
    held = pieces[0].shape[0] // 3
    padded = parts * held
    for d, piece in enumerate(pieces):
        for b in range(3):
            place = pl.multiple_of(b * padded + ids_ref[parts + d] * held, held)
            whole[pl.ds(place, held)] = piece[b * held : (b + 1) * held]
    unit, scale = normalised(x_ref[...].astype(F32))
    normed = (unit * vec_ref[0:1] + vec_ref[2:3]).T.astype(BF)
    copy.wait()
    up_norm = jnp.zeros((width, x_ref.shape[0]), F32)
    sums = []
    for b in range(3):
        grads = whole[b * padded : b * padded + width]
        cols = slice(b * width, (b + 1) * width)
        up_norm = up_norm + dot(weight[:, cols], grads, 1, 0)
        pack[:, cols] = dot(normed, grads, 1, 1).astype(BF)
        sums.append(jnp.sum(grads.astype(F32), axis=1, keepdims=True))
    up_norm = up_norm.T
    gx_ref[...] = (ginner_ref[...] + norm_back(unit, scale, up_norm, vec_ref[0:1])).astype(BF)
    line = lax.broadcasted_iota(jnp.int32, table_ref.shape, 0)
    table = jnp.where(
        line == 0,
        jnp.sum(up_norm * unit, axis=0, keepdims=True),
        jnp.where(line == 2, jnp.sum(up_norm, axis=0, keepdims=True), table_ref[...]),
    ).T
    lane = lax.broadcasted_iota(jnp.int32, table.shape, 1)
    table = jnp.where(lane == 3, sums[0], jnp.where(lane == 4, sums[2], table))
    pack[:, 3 * width : main] = table.astype(BF)
    copies += send_sides(ids_ref, 2 * parts, pack, 0, main, outs, sem, 1, shards)
    for copy in copies:
        copy.wait()


def qkv_backward(ids, x, ginner, vec, table, weight, pieces, shards):
    parts = len(pieces)
    rows, width = x.shape
    total = 3 * width + LANES
    part = shape((shards, width // shards // 2, total), BF)
    return pl.pallas_call(
        functools.partial(qkv_back_kernel, parts=parts, shards=shards),
        in_specs=[SMEM, VMEM, VMEM, VMEM, VMEM, HBM] + [VMEM] * parts,
        out_specs=[VMEM, HBM, HBM],
        out_shape=[shape((rows, width), BF), part, part],
        scratch_shapes=[
            pltpu.VMEM((width, 3 * width), BF),
            pltpu.VMEM((parts * pieces[0].shape[0], rows), BF),
            pltpu.VMEM((width, total), BF),
            pltpu.SemaphoreType.DMA((1 + 2 * shards,)),
        ],
        compiler_params=PARAMS,
        name="qkv_backward",
    )(ids, x, ginner, vec, table, weight, *pieces)


def layer_forward(x, packs, rest, ids, order, parts, size, shards, ratio, back=None):
    sent, weight, vec = qkv_project(ids, x, packs, parts, size, shards)
    width = x.shape[1]
    depth = width // shards
    bias = vec[8 : 8 + ratio].reshape(ratio, shards, depth).transpose(1, 0, 2).reshape(1, -1)
    received = exchange(sent)
    returned = None
    if back is not None:
        *received, back = lax.optimization_barrier((*received, back))
        returned = return_rows(back, 0)
    mixed, attn_saved = attention_forward(received, order, size)
    received = exchange(mixed)
    if back is not None:
        tied = lax.optimization_barrier((*received, *returned))
        received, returned = tied[:parts], tied[parts:]
    result, inner, hidden, mixed = mlp_forward(
        ids, x, vec, bias, rest, received, shards, ratio
    )
    return result, (x, weight, vec, attn_saved, inner, hidden, mixed), returned


def layer_backward(saved, grad, rest, ids, order, parts, size, shards, ratio, layer, background):
    x, weight, vec, attn_saved, inner, hidden, mixed = saved
    last = layer == 0
    column = (1 + ratio) * x.shape[1]
    sent, (ginner, gattn, ghid, act, middle, table) = mlp_backward(
        ids, grad, inner, hidden, vec, rest, parts, size, shards, ratio
    )
    received = exchange(background.slot("AD", sent))
    early = early_grads(ids, middle, ghid, mixed, gattn, act, grad, parts, shards, ratio, last)
    tied = lax.optimization_barrier((*received, *early))
    received, early = tied[:parts], tied[parts:]
    if last:
        first = background.add("B", early_task0(*early, background, column))
    else:
        first = background.add("C", early_task1(*early, background, column))
    sent = attention_backward(received, attn_saved, order, size)
    if last:
        sent = background.slot("BCD", sent)
    received = exchange(sent)
    if last:
        received = background.slot("CD", received)
    results = qkv_backward(ids, x, ginner, vec, table, weight, received, shards)
    grad_x, *late = lax.optimization_barrier(tuple(results))
    if last:
        for lane in "DCB":
            background.slot(lane, [grad_x])
        second = background.add("A", late_task0(*late, background))
    else:
        second = background.add("D", late_task1(*late, background))
    return grad_x, first, second


def blocks_to_columns(value, parts):
    depth = value.shape[0] // parts
    return [value[i * depth : (i + 1) * depth] for i in range(parts)]


def split_layers(pack, core):
    rows = pack.shape[0] // 2
    first, second = pack[:rows], pack[rows:]
    other = lax.ppermute(jnp.where(core == 0, second, first), "section", [(0, 1), (1, 0)])
    return jnp.where(core == 0, first, other), jnp.where(core == 0, other, second)


def gather(part):
    return lax.all_gather(part, SHARDS, axis=0, tiled=True)


def across(value, bit):
    count = lax.axis_size("fsdp")
    return lax.ppermute(value, "fsdp", [(i, i ^ bit) for i in range(count)])


def swap_cores(value):
    return lax.ppermute(value, "section", [(0, 1), (1, 0)])


def gather_pieces(part):
    rows = part.shape[0] // 2
    by_x, by_y = across(part, 1), across(part, 2)
    pieces = [part, by_x, by_y, across(by_x[:rows], 2), across(by_y[rows:], 1)]
    return pieces + [swap_cores(piece) for piece in pieces]


class Background:
    def __init__(self):
        self.tasks = []
        self.links = {}
        self.shared = {}

    def send(self, link, value, axis, pairs):
        if link in self.links:
            value, _ = lax.optimization_barrier((value, self.links[link]))
        moved = lax.ppermute(value, axis, pairs)
        self.links[link] = moved
        return moved

    def across(self, value, bit):
        count = lax.axis_size("fsdp")
        return self.send(bit, value, "fsdp", [(i, i ^ bit) for i in range(count)])

    def add(self, lane, task):
        entry = {"lane": lane, "task": task, "result": None}
        entry["flight"] = next(task)
        self.tasks.append(entry)
        return entry

    def resume(self, entry, flight):
        try:
            entry["flight"] = entry["task"].send(flight)
        except StopIteration as stop:
            entry["flight"], entry["result"] = None, stop.value

    def slot(self, lanes, values=()):
        waiting = [e for e in self.tasks if e["flight"] is not None and e["lane"] in lanes]
        flat = list(values)
        for entry in waiting:
            flat += entry["flight"]
        if len(flat) > 0:
            flat = list(lax.optimization_barrier(tuple(flat)))
        values, flat = flat[: len(values)], flat[len(values) :]
        for entry in waiting:
            count = len(entry["flight"])
            self.resume(entry, flat[:count])
            flat = flat[count:]
        return values

    def finish(self):
        while any(entry["flight"] is not None for entry in self.tasks):
            for entry in list(self.tasks):
                if entry["flight"] is not None:
                    self.resume(entry, entry["flight"])


def idle(values, slots):
    for _ in range(slots):
        values = yield list(values)
    return values


def permuted_value(keep, send, background, hold):
    (received,) = yield [swap_cores(send)]
    rows = keep.shape[1] // 2

    def summed(slots, side):
        return sum_pair(keep[slots, side], received[slots, side])

    top, low = slice(0, rows), slice(rows, 2 * rows)
    by_x, by_y = yield [
        background.across(summed(slice(1, 4, 2), top), 1),
        background.across(summed(slice(2, 4), low), 2),
    ]
    by_x, by_y = yield from idle([by_x, by_y], hold)
    first = sum_pair(summed(slice(0, 4, 2), top), by_x)
    second = sum_pair(summed(slice(0, 2), low), by_y)
    by_y, by_x = yield [background.across(first[1], 2), background.across(second[1], 1)]
    return jnp.concatenate([sum_pair(first[0], by_y), sum_pair(second[0], by_x)])


def early_task0(keep, send, background, column):
    value = yield from permuted_value(keep, send, background, 0)
    other = background.add("D", ctx_task(value[:, column:], 0, background, 1))
    mine = yield from ctx_task(value[:, :column], 0, background)
    return mine, other


def late_task0(keep, send, background):
    value = yield from permuted_value(keep, send, background, 0)
    return (yield from ctx_task(value, 0, background))


def early_task1(pack, background, column):
    value = lax.psum_scatter(pack, SHARDS, scatter_dimension=0, tiled=True)
    (value,) = yield [value]
    (value,) = yield [value]
    background.shared["down"] = value[:, column:]
    return (yield from ctx_task(value[:, :column], 1, background))


def late_task1(keep, send, background):
    value = yield from permuted_value(keep, send, background, 1)
    value = jnp.concatenate([background.shared["down"], value], axis=1)
    return (yield from ctx_task(value, 1, background))


def ctx_task(value, layer, background, before=0):
    (value,) = yield from idle([value], before)
    if lax.axis_size("ctx") == 4:
        index = lax.axis_index("ctx")
        (received,) = yield [background.send("in", value, "ctx", [(0, 1), (3, 2)])]
        value = sum_pair(value, received)
        (received,) = yield [background.send("mid", value, "ctx", [(1, 2), (2, 1)])]
        value = sum_pair(value, received)
        (received,) = yield [background.send("out", value, "ctx", [(1, 0), (2, 3)])]
        value = jnp.where((index == 0) | (index == 3), received, value)
    else:
        value = lax.psum(value, "ctx")
    (other,) = yield [lax.ppermute(value, "section", [(1 - layer, layer)])]
    return value, other


def return_task(value, layer, pause):
    (value,) = yield from idle([value], pause)
    flight = yield return_rows(value, layer)
    return flight


def sum_pair(a, b):
    return (a.astype(F32) + b.astype(F32)).astype(BF)


def body(
    tokens, cotangent, span_order, w_qkv, w_out, w_up, w_down, norm_gains, bias_rows, bias_hidden
):
    core = lax.axis_index("section")
    ctx = lax.axis_size("ctx")
    cores = lax.axis_size("section")
    shards = lax.axis_size("fsdp")
    half = ctx // cores
    base = lax.axis_index("ctx") // half
    member = core * half + lax.axis_index("ctx") % half
    depth = w_qkv.shape[1]
    width = depth * shards
    ratio = bias_hidden.shape[1] // depth
    size = width // HEADS
    gain_count, shift_count = norm_gains.shape[1], bias_rows.shape[1]

    steps = jnp.arange(ctx, dtype=jnp.int32)
    came, goes = (member - steps) % ctx, (member + steps) % ctx
    shard = lax.axis_index("fsdp")
    slots = [shard ^ k for k in range(shards)] + [core, 1 - core]
    ids = jnp.concatenate([goes, came, jnp.stack(slots)]).astype(jnp.int32)
    order = jnp.concatenate([span_order[came], span_order[goes]])

    small = jnp.concatenate([norm_gains[0], bias_rows[0], bias_hidden[0].reshape(ratio, depth)]).T
    small = jnp.pad(small, ((0, 0), (0, LANES - small.shape[1])))
    first = jnp.concatenate([w_qkv[0], small], axis=1)
    rest = jnp.concatenate([w_out[0], w_up[0]] + blocks_to_columns(w_down[0], ratio), axis=1)
    first0, first1 = split_layers(first, core)
    x = bring_rows(tokens[:, 0], core, base)
    rest0, rest1 = split_layers(rest, core)
    first0, first1 = gather_pieces(first0), gather_pieces(first1)
    rest0, rest1 = gather(rest0), gather(rest1)
    sizes = (ids, order, ctx, size, shards, ratio)
    out0, saved0, _ = layer_forward(x, first0, rest0, *sizes)
    late_cot, out0 = lax.optimization_barrier((cotangent[:, 0], out0))
    out1, saved1, back_out0 = layer_forward(out0, first1, rest1, *sizes, out0)
    cot = bring_rows(late_cot, core, base)
    background = Background()
    grad1, early1, late1 = layer_backward(saved1, cot, rest1, *sizes, 1, background)
    back1 = background.add("A", return_task(jnp.concatenate([out1, grad1], axis=1), 1, 0))
    grad0, early0, late0 = layer_backward(saved0, grad1, rest0, *sizes, 0, background)
    back0 = background.add("A", return_task(grad0, 0, 5))
    background.finish()

    def chosen(values0, values1):
        return jnp.stack([jnp.where(core == 0, a, b) for a, b in zip(values0, values1)])

    layer_outputs = chosen(back_out0, [value[:, :width] for value in back1["result"]])
    input_grads = chosen(
        back0["result"], [value[:, width:] for value in back1["result"]]
    ).astype(F32)

    def joined(pair0, pair1):
        return jnp.where(
            core == 0,
            jnp.concatenate([pair0[0], pair0[1]]),
            jnp.concatenate([pair1[1], pair1[0]]),
        ).astype(F32)

    (up0, down0), up1, rest1 = early0["result"], early1["result"], late1["result"]
    hidden = ratio * width
    early = joined(up0, up1)
    late = joined(late0["result"], [value[:, hidden:] for value in rest1])
    down = joined(down0["result"], [value[:, :hidden] for value in rest1])
    table = late[:, 3 * width :].T
    return (
        layer_outputs[None, :, None],
        input_grads[None, :, None],
        late[None, :, : 3 * width],
        early[None, :, :width],
        early[None, :, width:],
        jnp.concatenate([down[:, j * width : (j + 1) * width] for j in range(ratio)])[None],
        table[None, :gain_count],
        table[None, gain_count : gain_count + shift_count],
        table[gain_count + shift_count : gain_count + shift_count + ratio].reshape(1, -1),
    )


def solution(mesh):
    return jax.shard_map(
        body,
        mesh=mesh,
        in_specs=(
            P(None, "fsdp", "ctx", None),
            P(None, "fsdp", "ctx", None),
            P(),
            P("section", "fsdp", None),
            P("section", "fsdp", None),
            P("section", "fsdp", None),
            P("section", "fsdp", None),
            P("section", None, "fsdp"),
            P("section", None, "fsdp"),
            P("section", "fsdp"),
        ),
        out_specs=(
            P("section", None, "fsdp", "ctx", None),
            P("section", None, "fsdp", "ctx", None),
            P("section", "fsdp", None),
            P("section", "fsdp", None),
            P("section", "fsdp", None),
            P("section", "fsdp", None),
            P("section", None, "fsdp"),
            P("section", None, "fsdp"),
            P("section", "fsdp"),
        ),
        check_vma=False,
    )
```

```python
import functools

import jax
import jax.numpy as jnp
from jax import lax
from jax.experimental import pallas as pl
from jax.experimental.pallas import tpu as pltpu
from jax.sharding import PartitionSpec as P

HEADS = 12
EPS = 1e-05
GELU_C = 0.7978845608
GELU_A = 0.044715
LANES = 128
BF = jnp.bfloat16
F32 = jnp.float32
VMEM = pl.BlockSpec(memory_space=pltpu.VMEM)
SMEM = pl.BlockSpec(memory_space=pltpu.SMEM)
HBM = pl.BlockSpec(memory_space=pl.ANY)
PARAMS = pltpu.CompilerParams(vmem_limit_bytes=56 * 1024 * 1024)
GROUP = ("section", "ctx")
SHARDS = ("fsdp", "section")


def dot(a, b, ca, cb):
    return lax.dot_general(a, b, (((ca,), (cb,)), ((), ())), preferred_element_type=F32)


def shape(dims, dtype):
    return jax.ShapeDtypeStruct(dims, dtype)


def place_of(core, ctx_index):
    return core * lax.axis_size("ctx") + ctx_index


def exchange(pieces):
    ctx, cores = lax.axis_size("ctx"), lax.axis_size("section")
    half = ctx // cores
    moved = [pieces[0]]
    for d in range(1, ctx):
        pairs = []
        for base in range(cores):
            for g in range(ctx):
                t = (g + d) % ctx
                pairs.append(
                    (
                        place_of(g // half, base * half + g % half),
                        place_of(t // half, base * half + t % half),
                    )
                )
        moved.append(lax.ppermute(pieces[d], GROUP, pairs))
    return moved


def bring_rows(both, core, base):
    ctx, cores = lax.axis_size("ctx"), lax.axis_size("section")
    half = ctx // cores
    pairs = [
        (place_of(c, c * half + i), place_of(c, (1 - c) * half + i))
        for c in range(cores)
        for i in range(half)
    ]
    received = lax.ppermute(jnp.where(core == 0, both[1], both[0]), GROUP, pairs)
    own = jnp.where(core == 0, both[0], both[1])
    return jnp.where(core == base, own, received)


def return_rows(value, layer, background=None):
    ctx, cores = lax.axis_size("ctx"), lax.axis_size("section")
    half = ctx // cores
    if background is not None and "mid" in background.links:
        value, _ = lax.optimization_barrier((value, background.links["mid"]))
    return [
        lax.ppermute(
            value,
            GROUP,
            [(place_of(z // half, m * half + z % half), place_of(layer, z)) for z in range(ctx)],
        )
        for m in range(cores)
    ]


def normalised(values):
    centred = values - jnp.mean(values, axis=-1, keepdims=True)
    scale = lax.rsqrt(jnp.mean(centred * centred, axis=-1, keepdims=True) + EPS)
    return centred * scale, scale


def norm_back(unit, scale, upstream, gain):
    w = upstream * gain
    return (
        w - jnp.mean(w, axis=-1, keepdims=True) - unit * jnp.mean(w * unit, axis=-1, keepdims=True)
    ) * scale


def piece_places(ids_ref, parts, depth, slots):
    first = 2 * parts
    rows = depth // 2
    places = []
    for side in range(2):
        core = ids_ref[first + slots + side]
        for slot, start, count in (
            (0, 0, rows),
            (1, 0, rows),
            (2, 0, rows),
            (3, 0, rows // 2),
            (3, rows // 2, rows // 2),
        ):
            place = ids_ref[first + slot] * depth + core * rows + start
            places.append((pl.multiple_of(place, 16), count))
    return places


def qkv_kernel(ids_ref, x_ref, *refs, parts, size, shards):
    packs, refs = refs[:10], refs[10:]
    outs, (weight_ref, vec_ref), refs = refs[:parts], refs[parts : parts + 2], refs[parts + 2 :]
    weight, small, whole, sems = refs
    width = x_ref.shape[1]
    copies = []
    for i, (place, count) in enumerate(piece_places(ids_ref, parts, width // shards, shards)):
        for j, target, cols in (
            (0, small, slice(3 * width, 3 * width + LANES)),
            (1, weight, slice(0, 3 * width)),
        ):
            copies.append(
                pltpu.make_async_copy(
                    packs[i].at[:, cols], target.at[pl.ds(place, count)], sems.at[2 * i + j]
                )
            )
    for copy in copies:
        copy.start()
    unit, _ = normalised(x_ref[...].astype(F32))
    for copy in copies:
        copy.wait()
    keep = pltpu.make_async_copy(weight, weight_ref, sems.at[20])
    keep.start()
    vec = small[...].astype(F32).T
    vec_ref[...] = vec[:16]
    normed = (unit * vec[0:1] + vec[2:3]).astype(BF)
    held = outs[0].shape[0] // 3
    if parts * held != width:
        whole[...] = jnp.zeros_like(whole)
    for b in range(3):
        block = dot(normed, weight[:, b * width : (b + 1) * width], 1, 0)
        if b == 0:
            block = block + vec[3:4]
        if b == 2:
            block = block + vec[4:5]
        whole[b * parts * held : b * parts * held + width] = block.T.astype(BF)
    for d in range(parts):
        for b in range(3):
            first = pl.multiple_of(b * parts * held + ids_ref[d] * held, size)
            outs[d][b * held : (b + 1) * held] = whole[pl.ds(first, held)]
    keep.wait()


def qkv_project(ids, x, packs, parts, size, shards):
    rows, width = x.shape
    held = pl.cdiv(HEADS, parts) * size
    results = pl.pallas_call(
        functools.partial(qkv_kernel, parts=parts, size=size, shards=shards),
        in_specs=[SMEM, VMEM] + [HBM] * 10,
        out_specs=[VMEM] * parts + [HBM, VMEM],
        out_shape=[shape((3 * held, rows), BF)] * parts
        + [shape((width, 3 * width), BF), shape((16, width), F32)],
        scratch_shapes=[
            pltpu.VMEM((width, 3 * width), BF),
            pltpu.VMEM((width, LANES), BF),
            pltpu.VMEM((3 * parts * held, rows), BF),
            pltpu.SemaphoreType.DMA((21,)),
        ],
        compiler_params=PARAMS,
        name="qkv_project",
    )(ids, x, *packs)
    return results[:parts], results[parts], results[parts + 1]


def spans_of(order_ref, which, count, span):
    first = order_ref[which]
    return (
        (0, pl.multiple_of(first * span, span)),
        (1, pl.multiple_of((2 * count - 1 - first) * span, span)),
    )


def causal(scores, width, fill):
    depth = scores.shape[0]
    keys = lax.broadcasted_iota(jnp.int32, (width, width), 0)
    rows = lax.broadcasted_iota(jnp.int32, (width, width), 1)
    last = jnp.where(keys <= rows, scores[depth - width :], fill)
    if depth == width:
        return last
    return jnp.concatenate([scores[: depth - width], last], axis=0)


def sort_in(order_ref, pieces, target):
    count = len(pieces)
    span = pieces[0].shape[1] // 2
    for d in range(count):
        for side, place in spans_of(order_ref, d, count, span):
            target[:, pl.ds(place, span)] = pieces[d][:, side * span : (side + 1) * span]


def sort_out(order_ref, source, pieces):
    count = len(pieces)
    span = pieces[0].shape[1] // 2
    for d in range(count):
        for side, place in spans_of(order_ref, count + d, count, span):
            pieces[d][:, side * span : (side + 1) * span] = source[:, pl.ds(place, span)]


def attn_fwd_kernel(order_ref, *refs, parts, heads, size, block):
    pieces, mixed, (sorted_ref, out_ref, lse_ref) = refs[:parts], refs[parts : 2 * parts], refs[2 * parts :]
    feats = heads * size
    seq = sorted_ref.shape[1]
    sort_in(order_ref, pieces, sorted_ref)
    lse_ref[...] = jnp.zeros_like(lse_ref)
    for h in range(heads):
        for start in range(0, seq, block):
            end = start + block
            q = sorted_ref[h * size : (h + 1) * size, start:end]
            k = sorted_ref[feats + h * size : feats + (h + 1) * size, :end]
            v = sorted_ref[2 * feats + h * size : 2 * feats + (h + 1) * size, :end]
            scores = causal(dot(k, q, 0, 0) * 0.125, block, -1e30)
            top = jnp.max(scores, axis=0, keepdims=True)
            weights = jnp.exp(scores - top)
            total = jnp.sum(weights, axis=0, keepdims=True)
            mixed_part = dot(v, weights.astype(BF), 1, 0) / total
            out_ref[h * size : (h + 1) * size, start:end] = mixed_part.astype(BF)
            lse_ref[h : h + 1, start:end] = top + jnp.log(total)
    sort_out(order_ref, out_ref, mixed)


def attn_bwd_kernel(order_ref, *refs, parts, heads, size, block):
    pieces, (sorted_ref, out_ref, lse_ref) = refs[:parts], refs[parts : parts + 3]
    grads, (dsort, gsort, gk, gv) = refs[parts + 3 : 2 * parts + 3], refs[2 * parts + 3 :]
    feats = heads * size
    seq = sorted_ref.shape[1]
    sort_in(order_ref, pieces, dsort)
    for h in range(heads):
        own = slice(h * size, (h + 1) * size)
        gk[...] = jnp.zeros_like(gk)
        gv[...] = jnp.zeros_like(gv)
        for start in range(0, seq, block):
            end = start + block
            q = sorted_ref[own, start:end]
            k = sorted_ref[feats + h * size : feats + (h + 1) * size, :end]
            v = sorted_ref[2 * feats + h * size : 2 * feats + (h + 1) * size, :end]
            dout = dsort[own, start:end]
            delta = jnp.sum(
                dout.astype(F32) * out_ref[own, start:end].astype(F32), axis=0, keepdims=True
            )
            scores = dot(k, q, 0, 0) * 0.125 - lse_ref[h : h + 1, start:end]
            probs = jnp.exp(causal(scores, block, -1e30))
            dprobs = dot(v, dout, 0, 0)
            dscores = (probs * (dprobs - delta)).astype(BF)
            gsort[own, start:end] = (dot(k, dscores, 1, 0) * 0.125).astype(BF)
            gk[:, :end] += dot(q, dscores, 1, 1)
            gv[:, :end] += dot(dout, probs.astype(BF), 1, 1)
        gsort[feats + h * size : feats + (h + 1) * size, :] = (gk[...] * 0.125).astype(BF)
        gsort[2 * feats + h * size : 2 * feats + (h + 1) * size, :] = gv[...].astype(BF)
    sort_out(order_ref, gsort, grads)


def widen(pieces, order):
    count = len(pieces)
    span = pieces[0].shape[1] // 2
    came = order[:count]
    holder = jnp.stack([came, 2 * count - 1 - came], axis=1).reshape(-1)
    place = jnp.argsort(holder)
    flat = jnp.concatenate(pieces, axis=1).reshape(-1, 2 * count, span)
    return [jnp.take(flat, place, axis=1).reshape(flat.shape[0], -1)]


def narrow(wide, order, count):
    feats, seq = wide.shape
    span = seq // (2 * count)
    goes = order[count:]
    holder = jnp.stack([goes, 2 * count - 1 - goes], axis=1).reshape(-1)
    flat = jnp.take(wide.reshape(feats, 2 * count, span), holder, axis=1)
    flat = flat.reshape(feats, count, 2 * span)
    return [flat[:, d] for d in range(count)]


def attention_forward(pieces, order, size):
    parts, rows = len(pieces), pieces[0].shape[1]
    seq = parts * rows
    heads = pieces[0].shape[0] // (3 * size)
    narrow_spans = (rows // 2) % LANES != 0
    ids, given = order, parts
    if narrow_spans:
        pieces, ids, given = widen(pieces, order), jnp.zeros((2,), jnp.int32), 1
    results = pl.pallas_call(
        functools.partial(
            attn_fwd_kernel, parts=given, heads=heads, size=size, block=min(256, seq // 2)
        ),
        in_specs=[SMEM] + [VMEM] * given,
        out_specs=[VMEM] * (given + 3),
        out_shape=[shape((heads * size, pieces[0].shape[1]), BF)] * given
        + [
            shape((3 * heads * size, seq), BF),
            shape((heads * size, seq), BF),
            shape((8 * pl.cdiv(heads, 8), seq), F32),
        ],
        compiler_params=PARAMS,
        name="attn_fwd",
    )(ids, *pieces)
    mixed = results[:given]
    if narrow_spans:
        mixed = narrow(mixed[0], order, parts)
    return mixed, tuple(results[given:])


def attention_backward(pieces, saved, order, size):
    parts, rows = len(pieces), pieces[0].shape[1]
    seq = parts * rows
    heads = pieces[0].shape[0] // size
    narrow_spans = (rows // 2) % LANES != 0
    ids, given = order, parts
    if narrow_spans:
        pieces, ids, given = widen(pieces, order), jnp.zeros((2,), jnp.int32), 1
    grads = pl.pallas_call(
        functools.partial(
            attn_bwd_kernel, parts=given, heads=heads, size=size, block=min(256, seq // 2)
        ),
        in_specs=[SMEM] + [VMEM] * (given + 3),
        out_specs=[VMEM] * given,
        out_shape=[shape((3 * heads * size, pieces[0].shape[1]), BF)] * given,
        scratch_shapes=[
            pltpu.VMEM((heads * size, seq), BF),
            pltpu.VMEM((3 * heads * size, seq), BF),
            pltpu.VMEM((size, seq), F32),
            pltpu.VMEM((size, seq), F32),
        ],
        compiler_params=PARAMS,
        name="attn_bwd",
    )(ids, *pieces, *saved)
    if narrow_spans:
        grads = narrow(grads[0], order, parts)
    return grads


def down_blocks(shards, ratio, depth):
    width = shards * depth
    for f in range(shards):
        for j in range(ratio):
            first = (f * ratio + j) * depth
            yield slice(first, first + depth), slice(f * depth, (f + 1) * depth), j * width


def rest_copies(pack, w_out, w_up, w_down, sems, shards, ratio):
    width = w_out.shape[0]
    depth = width // shards
    hidden = w_up.shape[1]
    out = [pltpu.make_async_copy(pack.at[:, :width], w_out, sems.at[0])]
    up = [pltpu.make_async_copy(pack.at[:, width : width + hidden], w_up, sems.at[1])]
    down = []
    for i, (rows, packed, column) in enumerate(down_blocks(shards, ratio, depth)):
        start = width + hidden + column
        down.append(
            pltpu.make_async_copy(
                pack.at[packed, start : start + width], w_down.at[rows], sems.at[2 + i]
            )
        )
    return out, up, down


def put_pieces(ids_ref, first, pieces, target):
    held = pieces[0].shape[0]
    for d, piece in enumerate(pieces):
        place = pl.multiple_of(ids_ref[first + d] * held, held)
        target[pl.ds(place, held)] = piece[...]


def mlp_kernel(ids_ref, x_ref, vec_ref, bias_ref, pack_ref, *refs, parts, shards, ratio):
    pieces = refs[:parts]
    result_ref, inner_ref, hidden_ref, mixed_ref = refs[parts : parts + 4]
    w_out, w_up, w_down, whole, sems = refs[parts + 4 :]
    width = x_ref.shape[1]
    out, up, down = rest_copies(pack_ref, w_out, w_up, w_down, sems, shards, ratio)
    for copy in out + up + down:
        copy.start()
    put_pieces(ids_ref, parts, pieces, whole)
    mixed_ref[...] = whole[:width]
    out[0].wait()
    inner = x_ref[...].astype(F32) + dot(whole[:width], w_out[...], 0, 0) + vec_ref[5:6]
    inner_ref[...] = inner
    unit, _ = normalised(inner)
    middle = (unit * vec_ref[1:2] + vec_ref[6:7]).astype(BF)
    up[0].wait()
    for copy in down:
        copy.wait()
    total = inner + vec_ref[7:8]
    for start in range(0, w_up.shape[1], width):
        cols = slice(start, start + width)
        hidden = dot(middle, w_up[:, cols], 1, 0) + bias_ref[:, cols]
        hidden_ref[:, cols] = hidden
        act = 0.5 * hidden * (1.0 + jnp.tanh(GELU_C * (hidden + GELU_A * hidden * hidden * hidden)))
        total = total + dot(act.astype(BF), w_down[cols], 1, 0)
    result_ref[...] = total.astype(BF)


def rest_scratch(width, hidden, shards, ratio):
    return [
        pltpu.VMEM((width, width), BF),
        pltpu.VMEM((width, hidden), BF),
        pltpu.VMEM((hidden, width), BF),
    ]


def mlp_forward(ids, x, vec, bias, pack, pieces, shards, ratio):
    parts = len(pieces)
    rows, width = x.shape
    hidden = ratio * width
    return pl.pallas_call(
        functools.partial(mlp_kernel, parts=parts, shards=shards, ratio=ratio),
        in_specs=[SMEM, VMEM, VMEM, VMEM, HBM] + [VMEM] * parts,
        out_specs=[VMEM] * 4,
        out_shape=[
            shape((rows, width), BF),
            shape((rows, width), F32),
            shape((rows, hidden), F32),
            shape((width, rows), BF),
        ],
        scratch_shapes=rest_scratch(width, hidden, shards, ratio)
        + [
            pltpu.VMEM((parts * pieces[0].shape[0], rows), BF),
            pltpu.SemaphoreType.DMA((2 + shards * ratio,)),
        ],
        compiler_params=PARAMS,
        name="mlp_forward",
    )(ids, x, vec, bias, pack, *pieces)


def mlp_back_kernel(
    ids_ref, grad_ref, inner_ref, hidden_ref, vec_ref, pack_ref, *refs, parts, shards, ratio
):
    outs = refs[:parts]
    ginner_ref, gattn_ref, ghid_ref, act_ref, middle_ref, table_ref = refs[parts : parts + 6]
    w_out, w_up, w_down, whole, sems = refs[parts + 6 :]
    width = grad_ref.shape[1]
    out, up, down = rest_copies(pack_ref, w_out, w_up, w_down, sems, shards, ratio)
    for copy in down + up + out:
        copy.start()
    grad_low = grad_ref[...].astype(BF)
    unit, scale = normalised(inner_ref[...])
    middle_ref[...] = (unit * vec_ref[1:2] + vec_ref[6:7]).astype(BF)
    for copy in down:
        copy.wait()
    up[0].wait()
    up_mid = jnp.zeros(unit.shape, F32)
    depth = width // shards
    table_ref[...] = jnp.zeros_like(table_ref)
    for start in range(0, w_up.shape[1], width):
        cols = slice(start, start + width)
        hidden = hidden_ref[:, cols]
        th = jnp.tanh(GELU_C * (hidden + GELU_A * hidden * hidden * hidden))
        act_ref[:, cols] = (0.5 * hidden * (1.0 + th)).astype(BF)
        slope = 0.5 * (1.0 + th) + 0.5 * hidden * (1.0 - th * th) * GELU_C * (
            1.0 + 3.0 * GELU_A * hidden * hidden
        )
        grad_hid = (dot(grad_low, w_down[cols], 1, 1) * slope).astype(BF)
        ghid_ref[:, cols] = grad_hid
        sums = jnp.sum(grad_hid.astype(F32), axis=0, keepdims=True)
        for i in range(width // depth):
            f, j = divmod(start // depth + i, ratio)
            table_ref[8 + j : 9 + j, f * depth : (f + 1) * depth] = sums[:, i * depth : (i + 1) * depth]
        up_mid = up_mid + dot(grad_hid, w_up[:, cols], 1, 1)
    grad_inner = grad_ref[...].astype(F32) + norm_back(unit, scale, up_mid, vec_ref[1:2])
    ginner_ref[...] = grad_inner
    grad_attn = grad_inner.astype(BF)
    gattn_ref[...] = grad_attn
    out[0].wait()
    held = outs[0].shape[0]
    if parts * held != width:
        whole[...] = jnp.zeros_like(whole)
    whole[:width] = dot(w_out[...], grad_attn, 1, 1).astype(BF)
    for d in range(parts):
        outs[d][...] = whole[pl.ds(pl.multiple_of(ids_ref[d] * held, held), held)]
    table_ref[1:2] = jnp.sum(up_mid * unit, axis=0, keepdims=True)
    table_ref[5:6] = jnp.sum(grad_attn.astype(F32), axis=0, keepdims=True)
    table_ref[6:7] = jnp.sum(up_mid, axis=0, keepdims=True)
    table_ref[7:8] = jnp.sum(grad_low.astype(F32), axis=0, keepdims=True)


def mlp_backward(ids, grad, inner, hidden, vec, pack, parts, size, shards, ratio):
    rows, width = inner.shape
    held = pl.cdiv(HEADS, parts) * size
    wide = ratio * width
    results = pl.pallas_call(
        functools.partial(mlp_back_kernel, parts=parts, shards=shards, ratio=ratio),
        in_specs=[SMEM, VMEM, VMEM, VMEM, VMEM, HBM],
        out_specs=[VMEM] * (parts + 6),
        out_shape=[shape((held, rows), BF)] * parts
        + [
            shape((rows, width), F32),
            shape((rows, width), BF),
            shape((rows, wide), BF),
            shape((rows, wide), BF),
            shape((rows, width), BF),
            shape((LANES, width), F32),
        ],
        scratch_shapes=rest_scratch(width, wide, shards, ratio)
        + [
            pltpu.VMEM((parts * held, rows), BF),
            pltpu.SemaphoreType.DMA((2 + shards * ratio,)),
        ],
        compiler_params=PARAMS,
        name="mlp_backward",
    )(ids, grad, inner, hidden, vec, pack)
    return results[:parts], results[parts:]


def write_down(act_ref, glow_ref, pack, start, shards, ratio):
    width = glow_ref.shape[1]
    depth = width // shards
    glow = glow_ref[...].astype(BF)
    for f in range(shards):
        block = dot(act_ref[:, f * ratio * depth : (f + 1) * ratio * depth], glow, 0, 0).astype(BF)
        for j in range(ratio):
            first = start + j * width
            pack[f * depth : (f + 1) * depth, first : first + width] = block[
                j * depth : (j + 1) * depth
            ]


def send_sides(ids_ref, first, pack, start, count, targets, sems, offset, shards):
    depth = pack.shape[0] // shards
    rows = depth // 2
    copies = []
    for side in range(2):
        core = ids_ref[first + shards + side]
        for k in range(shards):
            place = pl.multiple_of(ids_ref[first + k] * depth + core * rows, 16)
            copies.append(
                pltpu.make_async_copy(
                    pack.at[pl.ds(place, rows), start : start + count],
                    targets[side].at[k],
                    sems.at[offset + side * shards + k],
                )
            )
    for copy in copies:
        copy.start()
    return copies


def early_kernel(
    ids_ref, middle_ref, ghid_ref, mixed_ref, gattn_ref, act_ref, glow_ref, *refs, parts, shards, ratio, apart
):
    if apart:
        outs, (scratch, sems) = refs[:2], refs[2:]
    else:
        pack_ref, scratch, sems = refs
    width = middle_ref.shape[1]
    main = (1 + ratio) * width
    copies = []

    def send(columns, i):
        copy = pltpu.make_async_copy(scratch.at[:, columns], pack_ref.at[:, columns], sems.at[i])
        copy.start()
        copies.append(copy)

    scratch[:, :width] = dot(mixed_ref[...], gattn_ref[...], 1, 0).astype(BF)
    for i in range(ratio):
        cols = slice(i * width, (i + 1) * width)
        block = dot(middle_ref[...], ghid_ref[:, cols], 0, 0).astype(BF)
        scratch[:, (i + 1) * width : (i + 2) * width] = block
    if not apart:
        send(slice(0, main), 0)
    write_down(act_ref, glow_ref, scratch, main, shards, ratio)
    if apart:
        copies += send_sides(
            ids_ref, 2 * parts, scratch, 0, main + ratio * width, outs, sems, 0, shards
        )
    else:
        send(slice(main, main + ratio * width), 1)
    for copy in copies:
        copy.wait()


def early_grads(ids, middle, ghid, mixed, gattn, act, grad, parts, shards, ratio, apart):
    width = middle.shape[1]
    main, hidden = (1 + ratio) * width, ratio * width
    rows = width // shards // 2
    side = shape((shards, rows, main + hidden), BF)
    return pl.pallas_call(
        functools.partial(early_kernel, parts=parts, shards=shards, ratio=ratio, apart=apart),
        in_specs=[SMEM] + [VMEM] * 6,
        out_specs=[HBM] * (2 if apart else 1),
        out_shape=[side, side] if apart else [shape((width, main + hidden), BF)],
        scratch_shapes=[
            pltpu.VMEM((width, main + hidden), BF),
            pltpu.SemaphoreType.DMA((2 + 2 * shards,)),
        ],
        compiler_params=PARAMS,
        name="early_grads",
    )(ids, middle, ghid, mixed, gattn, act, grad)


def qkv_back_kernel(
    ids_ref, x_ref, ginner_ref, vec_ref, table_ref, weight_hbm, *refs, parts, shards
):
    pieces, refs = refs[:parts], refs[parts:]
    gx_ref, *outs, weight, whole, pack, sem = refs
    width = x_ref.shape[1]
    main = 3 * width + LANES
    copies = []
    copy = pltpu.make_async_copy(weight_hbm, weight, sem.at[0])
    copy.start()
    held = pieces[0].shape[0] // 3
    padded = parts * held
    for d, piece in enumerate(pieces):
        for b in range(3):
            place = pl.multiple_of(b * padded + ids_ref[parts + d] * held, held)
            whole[pl.ds(place, held)] = piece[b * held : (b + 1) * held]
    unit, scale = normalised(x_ref[...].astype(F32))
    normed = (unit * vec_ref[0:1] + vec_ref[2:3]).T.astype(BF)
    copy.wait()
    up_norm = jnp.zeros((width, x_ref.shape[0]), F32)
    sums = []
    for b in range(3):
        grads = whole[b * padded : b * padded + width]
        cols = slice(b * width, (b + 1) * width)
        up_norm = up_norm + dot(weight[:, cols], grads, 1, 0)
        pack[:, cols] = dot(normed, grads, 1, 1).astype(BF)
        sums.append(jnp.sum(grads.astype(F32), axis=1, keepdims=True))
    up_norm = up_norm.T
    gx_ref[...] = (ginner_ref[...] + norm_back(unit, scale, up_norm, vec_ref[0:1])).astype(BF)
    line = lax.broadcasted_iota(jnp.int32, table_ref.shape, 0)
    table = jnp.where(
        line == 0,
        jnp.sum(up_norm * unit, axis=0, keepdims=True),
        jnp.where(line == 2, jnp.sum(up_norm, axis=0, keepdims=True), table_ref[...]),
    ).T
    lane = lax.broadcasted_iota(jnp.int32, table.shape, 1)
    table = jnp.where(lane == 3, sums[0], jnp.where(lane == 4, sums[2], table))
    pack[:, 3 * width : main] = table.astype(BF)
    copies += send_sides(ids_ref, 2 * parts, pack, 0, main, outs, sem, 1, shards)
    for copy in copies:
        copy.wait()


def qkv_backward(ids, x, ginner, vec, table, weight, pieces, shards):
    parts = len(pieces)
    rows, width = x.shape
    total = 3 * width + LANES
    part = shape((shards, width // shards // 2, total), BF)
    return pl.pallas_call(
        functools.partial(qkv_back_kernel, parts=parts, shards=shards),
        in_specs=[SMEM, VMEM, VMEM, VMEM, VMEM, HBM] + [VMEM] * parts,
        out_specs=[VMEM, HBM, HBM],
        out_shape=[shape((rows, width), BF), part, part],
        scratch_shapes=[
            pltpu.VMEM((width, 3 * width), BF),
            pltpu.VMEM((parts * pieces[0].shape[0], rows), BF),
            pltpu.VMEM((width, total), BF),
            pltpu.SemaphoreType.DMA((1 + 2 * shards,)),
        ],
        compiler_params=PARAMS,
        name="qkv_backward",
    )(ids, x, ginner, vec, table, weight, *pieces)


def layer_forward(x, packs, rest, ids, order, parts, size, shards, ratio, back=None):
    sent, weight, vec = qkv_project(ids, x, packs, parts, size, shards)
    width = x.shape[1]
    depth = width // shards
    bias = vec[8 : 8 + ratio].reshape(ratio, shards, depth).transpose(1, 0, 2).reshape(1, -1)
    received = exchange(sent)
    returned = None
    if back is not None:
        *received, back = lax.optimization_barrier((*received, back))
        returned = return_rows(back, 0)
    mixed, attn_saved = attention_forward(received, order, size)
    received = exchange(mixed)
    if back is not None:
        tied = lax.optimization_barrier((*received, *returned))
        received, returned = tied[:parts], tied[parts:]
    result, inner, hidden, mixed = mlp_forward(
        ids, x, vec, bias, rest, received, shards, ratio
    )
    return result, (x, weight, vec, attn_saved, inner, hidden, mixed), returned


def layer_backward(
    saved, grad, rest, ids, order, parts, size, shards, ratio, layer, background, result=None
):
    x, weight, vec, attn_saved, inner, hidden, mixed = saved
    last = layer == 0
    column = (1 + ratio) * x.shape[1]
    sent, (ginner, gattn, ghid, act, middle, table) = mlp_backward(
        ids, grad, inner, hidden, vec, rest, parts, size, shards, ratio
    )
    received = exchange(background.slot("AD", sent))
    early = early_grads(ids, middle, ghid, mixed, gattn, act, grad, parts, shards, ratio, last)
    tied = lax.optimization_barrier((*received, *early, result if result is not None else grad))
    received, early = tied[:parts], tied[parts:-1]
    returned = None
    if last:
        first = background.add("B", early_task0(*early, background, column))
    else:
        first = background.add("C", early_task1(*early, background, column))
        returned = background.add("A", return_task(tied[-1], layer, 0))
    sent = attention_backward(received, attn_saved, order, size)
    sent = background.slot("BC" if last else "A", sent)
    received = exchange(sent)
    if last:
        received = background.slot("CD", received)
    grad_x, *late = lax.optimization_barrier(
        tuple(qkv_backward(ids, x, ginner, vec, table, weight, received, shards))
    )
    if last:
        for lane in "EB":
            background.slot(lane, [grad_x])
        second = background.add("A", late_task0(*late, background))
    else:
        second = background.add("D", late_task1(*late, background))
    return grad_x, first, second, returned


def blocks_to_columns(value, parts):
    depth = value.shape[0] // parts
    return [value[i * depth : (i + 1) * depth] for i in range(parts)]


def split_layers(pack, core):
    rows = pack.shape[0] // 2
    first, second = pack[:rows], pack[rows:]
    other = lax.ppermute(jnp.where(core == 0, second, first), "section", [(0, 1), (1, 0)])
    return jnp.where(core == 0, first, other), jnp.where(core == 0, other, second)


def gather(part):
    return lax.all_gather(part, SHARDS, axis=0, tiled=True)


def across(value, bit):
    count = lax.axis_size("fsdp")
    return lax.ppermute(value, "fsdp", [(i, i ^ bit) for i in range(count)])


def swap_cores(value):
    return lax.ppermute(value, "section", [(0, 1), (1, 0)])


def gather_pieces(part):
    rows = part.shape[0] // 2
    by_x, by_y = across(part, 1), across(part, 2)
    pieces = [part, by_x, by_y, across(by_x[:rows], 2), across(by_y[rows:], 1)]
    return pieces + [swap_cores(piece) for piece in pieces]


class Background:
    def __init__(self):
        self.tasks = []
        self.links = {}

    def send(self, link, value, axis, pairs):
        if link in self.links:
            value, _ = lax.optimization_barrier((value, self.links[link]))
        moved = lax.ppermute(value, axis, pairs)
        self.links[link] = moved
        return moved

    def across(self, value, bit):
        count = lax.axis_size("fsdp")
        return self.send(bit, value, "fsdp", [(i, i ^ bit) for i in range(count)])

    def add(self, lane, task):
        entry = {"lane": lane, "task": task, "result": None}
        entry["flight"] = next(task)
        self.tasks.append(entry)
        return entry

    def resume(self, entry, flight):
        try:
            entry["flight"] = entry["task"].send(flight)
        except StopIteration as stop:
            entry["flight"], entry["result"] = None, stop.value

    def slot(self, lanes, values=()):
        waiting = [e for e in self.tasks if e["flight"] is not None and e["lane"] in lanes]
        flat = list(values)
        for entry in waiting:
            flat += entry["flight"]
        if len(flat) > 0:
            flat = list(lax.optimization_barrier(tuple(flat)))
        values, flat = flat[: len(values)], flat[len(values) :]
        for entry in waiting:
            count = len(entry["flight"])
            self.resume(entry, flat[:count])
            flat = flat[count:]
        return values

    def finish(self):
        while any(entry["flight"] is not None for entry in self.tasks):
            for entry in list(self.tasks):
                if entry["flight"] is not None:
                    self.resume(entry, entry["flight"])


def idle(values, slots):
    for _ in range(slots):
        values = yield list(values)
    return values


def permuted_value(keep, send, background, hold):
    (received,) = yield [swap_cores(send)]
    (received,) = yield from idle([received], hold)
    rows = keep.shape[1] // 2

    def summed(slots, side):
        return sum_pair(keep[slots, side], received[slots, side])

    top, low = slice(0, rows), slice(rows, 2 * rows)
    by_x, by_y = yield [
        background.across(summed(slice(1, 4, 2), top), 1),
        background.across(summed(slice(2, 4), low), 2),
    ]
    first = sum_pair(summed(slice(0, 4, 2), top), by_x)
    second = sum_pair(summed(slice(0, 2), low), by_y)
    by_y, by_x = yield [background.across(first[1], 2), background.across(second[1], 1)]
    return jnp.concatenate([sum_pair(first[0], by_y), sum_pair(second[0], by_x)])


def early_task0(keep, send, background, column):
    value = yield from permuted_value(keep, send, background, 0)
    other = background.add("D", ctx_task(value[:, column:], 0, background, 1))
    mine = yield from ctx_task(value[:, :column], 0, background)
    return mine, other


def late_task0(keep, send, background):
    value = yield from permuted_value(keep, send, background, 0)
    return (yield from ctx_task(value, 0, background))


def early_task1(pack, background, column):
    value = lax.psum_scatter(pack, SHARDS, scatter_dimension=0, tiled=True)
    (value,) = yield [value]
    (value,) = yield [value]
    other = background.add("E", ctx_task(value[:, column:], 1, background))
    mine = yield from ctx_task(value[:, :column], 1, background)
    return mine, other


def late_task1(keep, send, background):
    value = yield from permuted_value(keep, send, background, 2)
    return (yield from ctx_task(value, 1, background))


def ctx_task(value, layer, background, before=0):
    (value,) = yield from idle([value], before)
    if lax.axis_size("ctx") == 4:
        index = lax.axis_index("ctx")
        (received,) = yield [background.send("in", value, "ctx", [(0, 1), (3, 2)])]
        value = sum_pair(value, received)
        (received,) = yield [background.send("mid", value, "ctx", [(1, 2), (2, 1)])]
        value = sum_pair(value, received)
        (received,) = yield [background.send("out", value, "ctx", [(1, 0), (2, 3)])]
        value = jnp.where((index == 0) | (index == 3), received, value)
    else:
        value = lax.psum(value, "ctx")
    (other,) = yield [lax.ppermute(value, "section", [(1 - layer, layer)])]
    return value, other


def return_task(value, layer, pause, background=None):
    (value,) = yield from idle([value], pause)
    flight = yield return_rows(value, layer, background)
    return flight


def sum_pair(a, b):
    return (a.astype(F32) + b.astype(F32)).astype(BF)


def body(
    tokens, cotangent, span_order, w_qkv, w_out, w_up, w_down, norm_gains, bias_rows, bias_hidden
):
    core = lax.axis_index("section")
    ctx = lax.axis_size("ctx")
    cores = lax.axis_size("section")
    shards = lax.axis_size("fsdp")
    half = ctx // cores
    base = lax.axis_index("ctx") // half
    member = core * half + lax.axis_index("ctx") % half
    depth = w_qkv.shape[1]
    width = depth * shards
    ratio = bias_hidden.shape[1] // depth
    size = width // HEADS
    gain_count, shift_count = norm_gains.shape[1], bias_rows.shape[1]

    steps = jnp.arange(ctx, dtype=jnp.int32)
    came, goes = (member - steps) % ctx, (member + steps) % ctx
    shard = lax.axis_index("fsdp")
    slots = [shard ^ k for k in range(shards)] + [core, 1 - core]
    ids = jnp.concatenate([goes, came, jnp.stack(slots)]).astype(jnp.int32)
    order = jnp.concatenate([span_order[came], span_order[goes]])

    small = jnp.concatenate([norm_gains[0], bias_rows[0], bias_hidden[0].reshape(ratio, depth)]).T
    small = jnp.pad(small, ((0, 0), (0, LANES - small.shape[1])))
    first = jnp.concatenate([w_qkv[0], small], axis=1)
    rest = jnp.concatenate([w_out[0], w_up[0]] + blocks_to_columns(w_down[0], ratio), axis=1)
    first0, first1 = split_layers(first, core)
    x = bring_rows(tokens[:, 0], core, base)
    rest0, rest1 = split_layers(rest, core)
    first0, first1 = gather_pieces(first0), gather_pieces(first1)
    rest0, rest1 = gather(rest0), gather(rest1)
    sizes = (ids, order, ctx, size, shards, ratio)
    out0, saved0, _ = layer_forward(x, first0, rest0, *sizes)
    late_cot, out0 = lax.optimization_barrier((cotangent[:, 0], out0))
    out1, saved1, back_out0 = layer_forward(out0, first1, rest1, *sizes, out0)
    cot = bring_rows(late_cot, core, base)
    background = Background()
    grad1, early1, late1, back_out1 = layer_backward(
        saved1, cot, rest1, *sizes, 1, background, out1
    )
    back1 = background.add("A", return_task(grad1, 1, 0))
    grad0, early0, late0, _ = layer_backward(saved0, grad1, rest0, *sizes, 0, background)
    back0 = background.add("A", return_task(grad0, 0, 5, background))
    background.finish()

    def chosen(values0, values1):
        return jnp.stack([jnp.where(core == 0, a, b) for a, b in zip(values0, values1)])

    layer_outputs = chosen(back_out0, back_out1["result"])
    input_grads = chosen(back0["result"], back1["result"]).astype(F32)

    def joined(pair0, pair1):
        return jnp.where(
            core == 0,
            jnp.concatenate([pair0[0], pair0[1]]),
            jnp.concatenate([pair1[1], pair1[0]]),
        ).astype(F32)

    (up0, down0), (up1, down1) = early0["result"], early1["result"]
    early = joined(up0, up1)
    late = joined(late0["result"], late1["result"])
    down = joined(down0["result"], down1["result"])
    table = late[:, 3 * width :].T
    return (
        layer_outputs[None, :, None],
        input_grads[None, :, None],
        late[None, :, : 3 * width],
        early[None, :, :width],
        early[None, :, width:],
        jnp.concatenate([down[:, j * width : (j + 1) * width] for j in range(ratio)])[None],
        table[None, :gain_count],
        table[None, gain_count : gain_count + shift_count],
        table[gain_count + shift_count : gain_count + shift_count + ratio].reshape(1, -1),
    )


def solution(mesh):
    return jax.shard_map(
        body,
        mesh=mesh,
        in_specs=(
            P(None, "fsdp", "ctx", None),
            P(None, "fsdp", "ctx", None),
            P(),
            P("section", "fsdp", None),
            P("section", "fsdp", None),
            P("section", "fsdp", None),
            P("section", "fsdp", None),
            P("section", None, "fsdp"),
            P("section", None, "fsdp"),
            P("section", "fsdp"),
        ),
        out_specs=(
            P("section", None, "fsdp", "ctx", None),
            P("section", None, "fsdp", "ctx", None),
            P("section", "fsdp", None),
            P("section", "fsdp", None),
            P("section", "fsdp", None),
            P("section", "fsdp", None),
            P("section", None, "fsdp"),
            P("section", None, "fsdp"),
            P("section", "fsdp"),
        ),
        check_vma=False,
    )
```

```python
import functools

import jax
import jax.numpy as jnp
from jax import lax
from jax.experimental import pallas as pl
from jax.experimental.pallas import tpu as pltpu
from jax.sharding import PartitionSpec as P

HEADS = 12
EPS = 1e-05
GELU_C = 0.7978845608
GELU_A = 0.044715
LANES = 128
BF = jnp.bfloat16
F32 = jnp.float32
VMEM = pl.BlockSpec(memory_space=pltpu.VMEM)
SMEM = pl.BlockSpec(memory_space=pltpu.SMEM)
HBM = pl.BlockSpec(memory_space=pl.ANY)
PARAMS = pltpu.CompilerParams(vmem_limit_bytes=56 * 1024 * 1024)
GROUP = ("section", "ctx")
SHARDS = ("fsdp", "section")


def dot(a, b, ca, cb):
    return lax.dot_general(a, b, (((ca,), (cb,)), ((), ())), preferred_element_type=F32)


def shape(dims, dtype):
    return jax.ShapeDtypeStruct(dims, dtype)


def place_of(core, ctx_index):
    return core * lax.axis_size("ctx") + ctx_index


def exchange(pieces):
    ctx, cores = lax.axis_size("ctx"), lax.axis_size("section")
    half = ctx // cores
    moved = [pieces[0]]
    for d in range(1, ctx):
        pairs = []
        for base in range(cores):
            for g in range(ctx):
                t = (g + d) % ctx
                pairs.append(
                    (
                        place_of(g // half, base * half + g % half),
                        place_of(t // half, base * half + t % half),
                    )
                )
        moved.append(lax.ppermute(pieces[d], GROUP, pairs))
    return moved


def bring_rows(both, core, base):
    ctx, cores = lax.axis_size("ctx"), lax.axis_size("section")
    half = ctx // cores
    pairs = [
        (place_of(c, c * half + i), place_of(c, (1 - c) * half + i))
        for c in range(cores)
        for i in range(half)
    ]
    received = lax.ppermute(jnp.where(core == 0, both[1], both[0]), GROUP, pairs)
    own = jnp.where(core == 0, both[0], both[1])
    return jnp.where(core == base, own, received)


def return_rows(value, layer, background=None):
    ctx, cores = lax.axis_size("ctx"), lax.axis_size("section")
    half = ctx // cores
    if background is not None and "mid" in background.links:
        value, _ = lax.optimization_barrier((value, background.links["mid"]))
    return [
        lax.ppermute(
            value,
            GROUP,
            [(place_of(z // half, m * half + z % half), place_of(layer, z)) for z in range(ctx)],
        )
        for m in range(cores)
    ]


def normalised(values):
    centred = values - jnp.mean(values, axis=-1, keepdims=True)
    scale = lax.rsqrt(jnp.mean(centred * centred, axis=-1, keepdims=True) + EPS)
    return centred * scale, scale


def norm_back(unit, scale, upstream, gain):
    w = upstream * gain
    return (
        w - jnp.mean(w, axis=-1, keepdims=True) - unit * jnp.mean(w * unit, axis=-1, keepdims=True)
    ) * scale


def piece_places(ids_ref, parts, depth, slots):
    first = 2 * parts
    rows = depth // 2
    places = []
    for side in range(2):
        core = ids_ref[first + slots + side]
        for slot, start, count in (
            (0, 0, rows),
            (1, 0, rows),
            (2, 0, rows),
            (3, 0, rows // 2),
            (3, rows // 2, rows // 2),
        ):
            place = ids_ref[first + slot] * depth + core * rows + start
            places.append((pl.multiple_of(place, 16), count))
    return places


def qkv_kernel(ids_ref, x_ref, *refs, parts, size, shards):
    packs, refs = refs[:10], refs[10:]
    outs, (weight_ref, vec_ref), refs = refs[:parts], refs[parts : parts + 2], refs[parts + 2 :]
    weight, small, whole, sems = refs
    width = x_ref.shape[1]
    copies = []
    for i, (place, count) in enumerate(piece_places(ids_ref, parts, width // shards, shards)):
        for j, target, cols in (
            (0, small, slice(3 * width, 3 * width + LANES)),
            (1, weight, slice(0, 3 * width)),
        ):
            copies.append(
                pltpu.make_async_copy(
                    packs[i].at[:, cols], target.at[pl.ds(place, count)], sems.at[2 * i + j]
                )
            )
    for copy in copies:
        copy.start()
    unit, _ = normalised(x_ref[...].astype(F32))
    for copy in copies:
        copy.wait()
    keep = pltpu.make_async_copy(weight, weight_ref, sems.at[20])
    keep.start()
    vec = small[...].astype(F32).T
    vec_ref[...] = vec[:16]
    normed = (unit * vec[0:1] + vec[2:3]).astype(BF)
    held = outs[0].shape[0] // 3
    if parts * held != width:
        whole[...] = jnp.zeros_like(whole)
    for b in range(3):
        block = dot(normed, weight[:, b * width : (b + 1) * width], 1, 0)
        if b == 0:
            block = block + vec[3:4]
        if b == 2:
            block = block + vec[4:5]
        whole[b * parts * held : b * parts * held + width] = block.T.astype(BF)
    for d in range(parts):
        for b in range(3):
            first = pl.multiple_of(b * parts * held + ids_ref[d] * held, size)
            outs[d][b * held : (b + 1) * held] = whole[pl.ds(first, held)]
    keep.wait()


def qkv_project(ids, x, packs, parts, size, shards):
    rows, width = x.shape
    held = pl.cdiv(HEADS, parts) * size
    results = pl.pallas_call(
        functools.partial(qkv_kernel, parts=parts, size=size, shards=shards),
        in_specs=[SMEM, VMEM] + [HBM] * 10,
        out_specs=[VMEM] * parts + [HBM, VMEM],
        out_shape=[shape((3 * held, rows), BF)] * parts
        + [shape((width, 3 * width), BF), shape((16, width), F32)],
        scratch_shapes=[
            pltpu.VMEM((width, 3 * width), BF),
            pltpu.VMEM((width, LANES), BF),
            pltpu.VMEM((3 * parts * held, rows), BF),
            pltpu.SemaphoreType.DMA((21,)),
        ],
        compiler_params=PARAMS,
        name="qkv_project",
    )(ids, x, *packs)
    return results[:parts], results[parts], results[parts + 1]


def spans_of(order_ref, which, count, span):
    first = order_ref[which]
    return (
        (0, pl.multiple_of(first * span, span)),
        (1, pl.multiple_of((2 * count - 1 - first) * span, span)),
    )


def causal(scores, width, fill):
    depth = scores.shape[0]
    keys = lax.broadcasted_iota(jnp.int32, (width, width), 0)
    rows = lax.broadcasted_iota(jnp.int32, (width, width), 1)
    last = jnp.where(keys <= rows, scores[depth - width :], fill)
    if depth == width:
        return last
    return jnp.concatenate([scores[: depth - width], last], axis=0)


def sort_in(order_ref, pieces, target):
    count = len(pieces)
    span = pieces[0].shape[1] // 2
    for d in range(count):
        for side, place in spans_of(order_ref, d, count, span):
            target[:, pl.ds(place, span)] = pieces[d][:, side * span : (side + 1) * span]


def sort_out(order_ref, source, pieces):
    count = len(pieces)
    span = pieces[0].shape[1] // 2
    for d in range(count):
        for side, place in spans_of(order_ref, count + d, count, span):
            pieces[d][:, side * span : (side + 1) * span] = source[:, pl.ds(place, span)]


def attn_fwd_kernel(order_ref, *refs, parts, heads, size, block):
    pieces, mixed, (sorted_ref, out_ref, lse_ref) = refs[:parts], refs[parts : 2 * parts], refs[2 * parts :]
    feats = heads * size
    seq = sorted_ref.shape[1]
    sort_in(order_ref, pieces, sorted_ref)
    lse_ref[...] = jnp.zeros_like(lse_ref)
    for h in range(heads):
        for start in range(0, seq, block):
            end = start + block
            q = sorted_ref[h * size : (h + 1) * size, start:end]
            k = sorted_ref[feats + h * size : feats + (h + 1) * size, :end]
            v = sorted_ref[2 * feats + h * size : 2 * feats + (h + 1) * size, :end]
            scores = causal(dot(k, q, 0, 0) * 0.125, block, -1e30)
            top = jnp.max(scores, axis=0, keepdims=True)
            weights = jnp.exp(scores - top)
            total = jnp.sum(weights, axis=0, keepdims=True)
            mixed_part = dot(v, weights.astype(BF), 1, 0) / total
            out_ref[h * size : (h + 1) * size, start:end] = mixed_part.astype(BF)
            lse_ref[h : h + 1, start:end] = top + jnp.log(total)
    sort_out(order_ref, out_ref, mixed)


def attn_bwd_kernel(order_ref, *refs, parts, heads, size, block):
    pieces, (sorted_ref, out_ref, lse_ref) = refs[:parts], refs[parts : parts + 3]
    grads, (dsort, gsort, gk, gv) = refs[parts + 3 : 2 * parts + 3], refs[2 * parts + 3 :]
    feats = heads * size
    seq = sorted_ref.shape[1]
    sort_in(order_ref, pieces, dsort)
    for h in range(heads):
        own = slice(h * size, (h + 1) * size)
        gk[...] = jnp.zeros_like(gk)
        gv[...] = jnp.zeros_like(gv)
        for start in range(0, seq, block):
            end = start + block
            q = sorted_ref[own, start:end]
            k = sorted_ref[feats + h * size : feats + (h + 1) * size, :end]
            v = sorted_ref[2 * feats + h * size : 2 * feats + (h + 1) * size, :end]
            dout = dsort[own, start:end]
            delta = jnp.sum(
                dout.astype(F32) * out_ref[own, start:end].astype(F32), axis=0, keepdims=True
            )
            scores = dot(k, q, 0, 0) * 0.125 - lse_ref[h : h + 1, start:end]
            probs = jnp.exp(causal(scores, block, -1e30))
            dprobs = dot(v, dout, 0, 0)
            dscores = (probs * (dprobs - delta)).astype(BF)
            gsort[own, start:end] = (dot(k, dscores, 1, 0) * 0.125).astype(BF)
            gk[:, :end] += dot(q, dscores, 1, 1)
            gv[:, :end] += dot(dout, probs.astype(BF), 1, 1)
        gsort[feats + h * size : feats + (h + 1) * size, :] = (gk[...] * 0.125).astype(BF)
        gsort[2 * feats + h * size : 2 * feats + (h + 1) * size, :] = gv[...].astype(BF)
    sort_out(order_ref, gsort, grads)


def widen(pieces, order):
    count = len(pieces)
    span = pieces[0].shape[1] // 2
    came = order[:count]
    holder = jnp.stack([came, 2 * count - 1 - came], axis=1).reshape(-1)
    place = jnp.argsort(holder)
    flat = jnp.concatenate(pieces, axis=1).reshape(-1, 2 * count, span)
    return [jnp.take(flat, place, axis=1).reshape(flat.shape[0], -1)]


def narrow(wide, order, count):
    feats, seq = wide.shape
    span = seq // (2 * count)
    goes = order[count:]
    holder = jnp.stack([goes, 2 * count - 1 - goes], axis=1).reshape(-1)
    flat = jnp.take(wide.reshape(feats, 2 * count, span), holder, axis=1)
    flat = flat.reshape(feats, count, 2 * span)
    return [flat[:, d] for d in range(count)]


def attention_forward(pieces, order, size):
    parts, rows = len(pieces), pieces[0].shape[1]
    seq = parts * rows
    heads = pieces[0].shape[0] // (3 * size)
    narrow_spans = (rows // 2) % LANES != 0
    ids, given = order, parts
    if narrow_spans:
        pieces, ids, given = widen(pieces, order), jnp.zeros((2,), jnp.int32), 1
    results = pl.pallas_call(
        functools.partial(
            attn_fwd_kernel, parts=given, heads=heads, size=size, block=min(256, seq // 2)
        ),
        in_specs=[SMEM] + [VMEM] * given,
        out_specs=[VMEM] * (given + 3),
        out_shape=[shape((heads * size, pieces[0].shape[1]), BF)] * given
        + [
            shape((3 * heads * size, seq), BF),
            shape((heads * size, seq), BF),
            shape((8 * pl.cdiv(heads, 8), seq), F32),
        ],
        compiler_params=PARAMS,
        name="attn_fwd",
    )(ids, *pieces)
    mixed = results[:given]
    if narrow_spans:
        mixed = narrow(mixed[0], order, parts)
    return mixed, tuple(results[given:])


def attention_backward(pieces, saved, order, size):
    parts, rows = len(pieces), pieces[0].shape[1]
    seq = parts * rows
    heads = pieces[0].shape[0] // size
    narrow_spans = (rows // 2) % LANES != 0
    ids, given = order, parts
    if narrow_spans:
        pieces, ids, given = widen(pieces, order), jnp.zeros((2,), jnp.int32), 1
    grads = pl.pallas_call(
        functools.partial(
            attn_bwd_kernel, parts=given, heads=heads, size=size, block=min(256, seq // 2)
        ),
        in_specs=[SMEM] + [VMEM] * (given + 3),
        out_specs=[VMEM] * given,
        out_shape=[shape((3 * heads * size, pieces[0].shape[1]), BF)] * given,
        scratch_shapes=[
            pltpu.VMEM((heads * size, seq), BF),
            pltpu.VMEM((3 * heads * size, seq), BF),
            pltpu.VMEM((size, seq), F32),
            pltpu.VMEM((size, seq), F32),
        ],
        compiler_params=PARAMS,
        name="attn_bwd",
    )(ids, *pieces, *saved)
    if narrow_spans:
        grads = narrow(grads[0], order, parts)
    return grads


def down_blocks(shards, ratio, depth):
    width = shards * depth
    for f in range(shards):
        for j in range(ratio):
            first = (f * ratio + j) * depth
            yield slice(first, first + depth), slice(f * depth, (f + 1) * depth), j * width


def rest_copies(pack, w_out, w_up, w_down, sems, shards, ratio):
    width = w_out.shape[0]
    depth = width // shards
    hidden = w_up.shape[1]
    out = [pltpu.make_async_copy(pack.at[:, :width], w_out, sems.at[0])]
    up = [pltpu.make_async_copy(pack.at[:, width : width + hidden], w_up, sems.at[1])]
    down = []
    for i, (rows, packed, column) in enumerate(down_blocks(shards, ratio, depth)):
        start = width + hidden + column
        down.append(
            pltpu.make_async_copy(
                pack.at[packed, start : start + width], w_down.at[rows], sems.at[2 + i]
            )
        )
    return out, up, down


def put_pieces(ids_ref, first, pieces, target):
    held = pieces[0].shape[0]
    for d, piece in enumerate(pieces):
        place = pl.multiple_of(ids_ref[first + d] * held, held)
        target[pl.ds(place, held)] = piece[...]


def mlp_kernel(ids_ref, x_ref, vec_ref, bias_ref, pack_ref, *refs, parts, shards, ratio):
    pieces = refs[:parts]
    result_ref, inner_ref, hidden_ref, mixed_ref = refs[parts : parts + 4]
    w_out, w_up, w_down, whole, sems = refs[parts + 4 :]
    width = x_ref.shape[1]
    out, up, down = rest_copies(pack_ref, w_out, w_up, w_down, sems, shards, ratio)
    for copy in out + up + down:
        copy.start()
    put_pieces(ids_ref, parts, pieces, whole)
    mixed_ref[...] = whole[:width]
    out[0].wait()
    inner = x_ref[...].astype(F32) + dot(whole[:width], w_out[...], 0, 0) + vec_ref[5:6]
    inner_ref[...] = inner
    unit, _ = normalised(inner)
    middle = (unit * vec_ref[1:2] + vec_ref[6:7]).astype(BF)
    up[0].wait()
    for copy in down:
        copy.wait()
    total = inner + vec_ref[7:8]
    for start in range(0, w_up.shape[1], width):
        cols = slice(start, start + width)
        hidden = dot(middle, w_up[:, cols], 1, 0) + bias_ref[:, cols]
        hidden_ref[:, cols] = hidden
        act = 0.5 * hidden * (1.0 + jnp.tanh(GELU_C * (hidden + GELU_A * hidden * hidden * hidden)))
        total = total + dot(act.astype(BF), w_down[cols], 1, 0)
    result_ref[...] = total.astype(BF)


def rest_scratch(width, hidden, shards, ratio):
    return [
        pltpu.VMEM((width, width), BF),
        pltpu.VMEM((width, hidden), BF),
        pltpu.VMEM((hidden, width), BF),
    ]


def mlp_forward(ids, x, vec, bias, pack, pieces, shards, ratio):
    parts = len(pieces)
    rows, width = x.shape
    hidden = ratio * width
    return pl.pallas_call(
        functools.partial(mlp_kernel, parts=parts, shards=shards, ratio=ratio),
        in_specs=[SMEM, VMEM, VMEM, VMEM, HBM] + [VMEM] * parts,
        out_specs=[VMEM] * 4,
        out_shape=[
            shape((rows, width), BF),
            shape((rows, width), F32),
            shape((rows, hidden), F32),
            shape((width, rows), BF),
        ],
        scratch_shapes=rest_scratch(width, hidden, shards, ratio)
        + [
            pltpu.VMEM((parts * pieces[0].shape[0], rows), BF),
            pltpu.SemaphoreType.DMA((2 + shards * ratio,)),
        ],
        compiler_params=PARAMS,
        name="mlp_forward",
    )(ids, x, vec, bias, pack, *pieces)


def mlp_back_kernel(
    ids_ref, grad_ref, inner_ref, hidden_ref, vec_ref, pack_ref, *refs, parts, shards, ratio
):
    outs = refs[:parts]
    ginner_ref, gattn_ref, ghid_ref, act_ref, middle_ref, table_ref = refs[parts : parts + 6]
    w_out, w_up, w_down, whole, sems = refs[parts + 6 :]
    width = grad_ref.shape[1]
    out, up, down = rest_copies(pack_ref, w_out, w_up, w_down, sems, shards, ratio)
    for copy in down + up + out:
        copy.start()
    grad_low = grad_ref[...].astype(BF)
    unit, scale = normalised(inner_ref[...])
    middle_ref[...] = (unit * vec_ref[1:2] + vec_ref[6:7]).astype(BF)
    for copy in down:
        copy.wait()
    up[0].wait()
    up_mid = jnp.zeros(unit.shape, F32)
    depth = width // shards
    table_ref[...] = jnp.zeros_like(table_ref)
    for start in range(0, w_up.shape[1], width):
        cols = slice(start, start + width)
        hidden = hidden_ref[:, cols]
        th = jnp.tanh(GELU_C * (hidden + GELU_A * hidden * hidden * hidden))
        act_ref[:, cols] = (0.5 * hidden * (1.0 + th)).astype(BF)
        slope = 0.5 * (1.0 + th) + 0.5 * hidden * (1.0 - th * th) * GELU_C * (
            1.0 + 3.0 * GELU_A * hidden * hidden
        )
        grad_hid = (dot(grad_low, w_down[cols], 1, 1) * slope).astype(BF)
        ghid_ref[:, cols] = grad_hid
        sums = jnp.sum(grad_hid.astype(F32), axis=0, keepdims=True)
        for i in range(width // depth):
            f, j = divmod(start // depth + i, ratio)
            table_ref[8 + j : 9 + j, f * depth : (f + 1) * depth] = sums[:, i * depth : (i + 1) * depth]
        up_mid = up_mid + dot(grad_hid, w_up[:, cols], 1, 1)
    grad_inner = grad_ref[...].astype(F32) + norm_back(unit, scale, up_mid, vec_ref[1:2])
    ginner_ref[...] = grad_inner
    grad_attn = grad_inner.astype(BF)
    gattn_ref[...] = grad_attn
    out[0].wait()
    held = outs[0].shape[0]
    if parts * held != width:
        whole[...] = jnp.zeros_like(whole)
    whole[:width] = dot(w_out[...], grad_attn, 1, 1).astype(BF)
    for d in range(parts):
        outs[d][...] = whole[pl.ds(pl.multiple_of(ids_ref[d] * held, held), held)]
    table_ref[1:2] = jnp.sum(up_mid * unit, axis=0, keepdims=True)
    table_ref[5:6] = jnp.sum(grad_attn.astype(F32), axis=0, keepdims=True)
    table_ref[6:7] = jnp.sum(up_mid, axis=0, keepdims=True)
    table_ref[7:8] = jnp.sum(grad_low.astype(F32), axis=0, keepdims=True)


def mlp_backward(ids, grad, inner, hidden, vec, pack, parts, size, shards, ratio):
    rows, width = inner.shape
    held = pl.cdiv(HEADS, parts) * size
    wide = ratio * width
    results = pl.pallas_call(
        functools.partial(mlp_back_kernel, parts=parts, shards=shards, ratio=ratio),
        in_specs=[SMEM, VMEM, VMEM, VMEM, VMEM, HBM],
        out_specs=[VMEM] * (parts + 6),
        out_shape=[shape((held, rows), BF)] * parts
        + [
            shape((rows, width), F32),
            shape((rows, width), BF),
            shape((rows, wide), BF),
            shape((rows, wide), BF),
            shape((rows, width), BF),
            shape((LANES, width), F32),
        ],
        scratch_shapes=rest_scratch(width, wide, shards, ratio)
        + [
            pltpu.VMEM((parts * held, rows), BF),
            pltpu.SemaphoreType.DMA((2 + shards * ratio,)),
        ],
        compiler_params=PARAMS,
        name="mlp_backward",
    )(ids, grad, inner, hidden, vec, pack)
    return results[:parts], results[parts:]


def write_down(act_ref, glow_ref, pack, start, shards, ratio):
    width = glow_ref.shape[1]
    depth = width // shards
    glow = glow_ref[...].astype(BF)
    for f in range(shards):
        block = dot(act_ref[:, f * ratio * depth : (f + 1) * ratio * depth], glow, 0, 0).astype(BF)
        for j in range(ratio):
            first = start + j * width
            pack[f * depth : (f + 1) * depth, first : first + width] = block[
                j * depth : (j + 1) * depth
            ]


def send_sides(ids_ref, first, pack, start, count, targets, sems, offset, shards):
    depth = pack.shape[0] // shards
    rows = depth // 2
    copies = []
    for side in range(2):
        core = ids_ref[first + shards + side]
        for k in range(shards):
            place = pl.multiple_of(ids_ref[first + k] * depth + core * rows, 16)
            copies.append(
                pltpu.make_async_copy(
                    pack.at[pl.ds(place, rows), start : start + count],
                    targets[side].at[k],
                    sems.at[offset + side * shards + k],
                )
            )
    for copy in copies:
        copy.start()
    return copies


def early_kernel(
    ids_ref, middle_ref, ghid_ref, mixed_ref, gattn_ref, act_ref, glow_ref, *refs, parts, shards, ratio, apart
):
    if apart:
        outs, (scratch, sems) = refs[:2], refs[2:]
    else:
        pack_ref, scratch, sems = refs
    width = middle_ref.shape[1]
    main = (1 + ratio) * width
    copies = []

    def send(columns, i):
        copy = pltpu.make_async_copy(scratch.at[:, columns], pack_ref.at[:, columns], sems.at[i])
        copy.start()
        copies.append(copy)

    scratch[:, :width] = dot(mixed_ref[...], gattn_ref[...], 1, 0).astype(BF)
    for i in range(ratio):
        cols = slice(i * width, (i + 1) * width)
        block = dot(middle_ref[...], ghid_ref[:, cols], 0, 0).astype(BF)
        scratch[:, (i + 1) * width : (i + 2) * width] = block
    if not apart:
        send(slice(0, main), 0)
    write_down(act_ref, glow_ref, scratch, main, shards, ratio)
    if apart:
        copies += send_sides(
            ids_ref, 2 * parts, scratch, 0, main + ratio * width, outs, sems, 0, shards
        )
    else:
        send(slice(main, main + ratio * width), 1)
    for copy in copies:
        copy.wait()


def early_grads(ids, middle, ghid, mixed, gattn, act, grad, parts, shards, ratio, apart):
    width = middle.shape[1]
    main, hidden = (1 + ratio) * width, ratio * width
    rows = width // shards // 2
    side = shape((shards, rows, main + hidden), BF)
    return pl.pallas_call(
        functools.partial(early_kernel, parts=parts, shards=shards, ratio=ratio, apart=apart),
        in_specs=[SMEM] + [VMEM] * 6,
        out_specs=[HBM] * (2 if apart else 1),
        out_shape=[side, side] if apart else [shape((width, main + hidden), BF)],
        scratch_shapes=[
            pltpu.VMEM((width, main + hidden), BF),
            pltpu.SemaphoreType.DMA((2 + 2 * shards,)),
        ],
        compiler_params=PARAMS,
        name="early_grads",
    )(ids, middle, ghid, mixed, gattn, act, grad)


def qkv_back_kernel(
    ids_ref, x_ref, ginner_ref, vec_ref, table_ref, weight_hbm, *refs, parts, shards
):
    pieces, refs = refs[:parts], refs[parts:]
    gx_ref, *outs, weight, whole, pack, sem = refs
    width = x_ref.shape[1]
    main = 3 * width + LANES
    copies = []
    copy = pltpu.make_async_copy(weight_hbm, weight, sem.at[0])
    copy.start()
    held = pieces[0].shape[0] // 3
    padded = parts * held
    for d, piece in enumerate(pieces):
        for b in range(3):
            place = pl.multiple_of(b * padded + ids_ref[parts + d] * held, held)
            whole[pl.ds(place, held)] = piece[b * held : (b + 1) * held]
    unit, scale = normalised(x_ref[...].astype(F32))
    normed = (unit * vec_ref[0:1] + vec_ref[2:3]).T.astype(BF)
    copy.wait()
    up_norm = jnp.zeros((width, x_ref.shape[0]), F32)
    sums = []
    for b in range(3):
        grads = whole[b * padded : b * padded + width]
        cols = slice(b * width, (b + 1) * width)
        up_norm = up_norm + dot(weight[:, cols], grads, 1, 0)
        pack[:, cols] = dot(normed, grads, 1, 1).astype(BF)
        sums.append(jnp.sum(grads.astype(F32), axis=1, keepdims=True))
    up_norm = up_norm.T
    gx_ref[...] = (ginner_ref[...] + norm_back(unit, scale, up_norm, vec_ref[0:1])).astype(BF)
    line = lax.broadcasted_iota(jnp.int32, table_ref.shape, 0)
    table = jnp.where(
        line == 0,
        jnp.sum(up_norm * unit, axis=0, keepdims=True),
        jnp.where(line == 2, jnp.sum(up_norm, axis=0, keepdims=True), table_ref[...]),
    ).T
    lane = lax.broadcasted_iota(jnp.int32, table.shape, 1)
    table = jnp.where(lane == 3, sums[0], jnp.where(lane == 4, sums[2], table))
    pack[:, 3 * width : main] = table.astype(BF)
    copies += send_sides(ids_ref, 2 * parts, pack, 0, main, outs, sem, 1, shards)
    for copy in copies:
        copy.wait()


def qkv_backward(ids, x, ginner, vec, table, weight, pieces, shards):
    parts = len(pieces)
    rows, width = x.shape
    total = 3 * width + LANES
    part = shape((shards, width // shards // 2, total), BF)
    return pl.pallas_call(
        functools.partial(qkv_back_kernel, parts=parts, shards=shards),
        in_specs=[SMEM, VMEM, VMEM, VMEM, VMEM, HBM] + [VMEM] * parts,
        out_specs=[VMEM, HBM, HBM],
        out_shape=[shape((rows, width), BF), part, part],
        scratch_shapes=[
            pltpu.VMEM((width, 3 * width), BF),
            pltpu.VMEM((parts * pieces[0].shape[0], rows), BF),
            pltpu.VMEM((width, total), BF),
            pltpu.SemaphoreType.DMA((1 + 2 * shards,)),
        ],
        compiler_params=PARAMS,
        name="qkv_backward",
    )(ids, x, ginner, vec, table, weight, *pieces)


def layer_forward(x, packs, rest, ids, order, parts, size, shards, ratio, back=None):
    sent, weight, vec = qkv_project(ids, x, packs, parts, size, shards)
    width = x.shape[1]
    depth = width // shards
    bias = vec[8 : 8 + ratio].reshape(ratio, shards, depth).transpose(1, 0, 2).reshape(1, -1)
    received = exchange(sent)
    returned = None
    if back is not None:
        *received, back = lax.optimization_barrier((*received, back))
        returned = return_rows(back, 0)
    mixed, attn_saved = attention_forward(received, order, size)
    received = exchange(mixed)
    if back is not None:
        tied = lax.optimization_barrier((*received, *returned))
        received, returned = tied[:parts], tied[parts:]
    result, inner, hidden, mixed = mlp_forward(
        ids, x, vec, bias, rest, received, shards, ratio
    )
    return result, (x, weight, vec, attn_saved, inner, hidden, mixed), returned


def layer_backward(
    saved, grad, rest, ids, order, parts, size, shards, ratio, layer, background, result=None
):
    x, weight, vec, attn_saved, inner, hidden, mixed = saved
    last = layer == 0
    column = (1 + ratio) * x.shape[1]
    sent, (ginner, gattn, ghid, act, middle, table) = mlp_backward(
        ids, grad, inner, hidden, vec, rest, parts, size, shards, ratio
    )
    received = exchange(background.slot("AD", sent))
    early = early_grads(ids, middle, ghid, mixed, gattn, act, grad, parts, shards, ratio, last)
    tied = lax.optimization_barrier((*received, *early, result if result is not None else grad))
    received, early = tied[:parts], tied[parts:-1]
    returned = None
    if last:
        first = background.add("B", early_task0(*early, background, column))
    else:
        first = background.add("C", early_task1(*early, background, column))
        returned = background.add("A", return_task(tied[-1], layer, 0))
    sent = attention_backward(received, attn_saved, order, size)
    sent = background.slot("BC" if last else "A", sent)
    received = exchange(sent)
    if last:
        received = background.slot("E", background.slot("CD", received))
    grad_x, *late = lax.optimization_barrier(
        tuple(qkv_backward(ids, x, ginner, vec, table, weight, received, shards))
    )
    if last:
        background.slot("B", [grad_x])
        second = background.add("A", late_task0(*late, background))
    else:
        second = background.add("D", late_task1(*late, background))
    return grad_x, first, second, returned


def blocks_to_columns(value, parts):
    depth = value.shape[0] // parts
    return [value[i * depth : (i + 1) * depth] for i in range(parts)]


def split_layers(pack, core):
    rows = pack.shape[0] // 2
    first, second = pack[:rows], pack[rows:]
    other = lax.ppermute(jnp.where(core == 0, second, first), "section", [(0, 1), (1, 0)])
    return jnp.where(core == 0, first, other), jnp.where(core == 0, other, second)


def gather(part):
    return lax.all_gather(part, SHARDS, axis=0, tiled=True)


def across(value, bit):
    count = lax.axis_size("fsdp")
    return lax.ppermute(value, "fsdp", [(i, i ^ bit) for i in range(count)])


def swap_cores(value):
    return lax.ppermute(value, "section", [(0, 1), (1, 0)])


def gather_pieces(part):
    rows = part.shape[0] // 2
    by_x, by_y = across(part, 1), across(part, 2)
    pieces = [part, by_x, by_y, across(by_x[:rows], 2), across(by_y[rows:], 1)]
    return pieces + [swap_cores(piece) for piece in pieces]


class Background:
    def __init__(self):
        self.tasks = []
        self.links = {}

    def send(self, link, value, axis, pairs):
        if link in self.links:
            value, _ = lax.optimization_barrier((value, self.links[link]))
        moved = lax.ppermute(value, axis, pairs)
        self.links[link] = moved
        return moved

    def across(self, value, bit):
        count = lax.axis_size("fsdp")
        return self.send(bit, value, "fsdp", [(i, i ^ bit) for i in range(count)])

    def add(self, lane, task):
        entry = {"lane": lane, "task": task, "result": None}
        entry["flight"] = next(task)
        self.tasks.append(entry)
        return entry

    def resume(self, entry, flight):
        try:
            entry["flight"] = entry["task"].send(flight)
        except StopIteration as stop:
            entry["flight"], entry["result"] = None, stop.value

    def slot(self, lanes, values=()):
        waiting = [e for e in self.tasks if e["flight"] is not None and e["lane"] in lanes]
        flat = list(values)
        for entry in waiting:
            flat += entry["flight"]
        if len(flat) > 0:
            flat = list(lax.optimization_barrier(tuple(flat)))
        values, flat = flat[: len(values)], flat[len(values) :]
        for entry in waiting:
            count = len(entry["flight"])
            self.resume(entry, flat[:count])
            flat = flat[count:]
        return values

    def finish(self):
        while any(entry["flight"] is not None for entry in self.tasks):
            for entry in list(self.tasks):
                if entry["flight"] is not None:
                    self.resume(entry, entry["flight"])


def idle(values, slots):
    for _ in range(slots):
        values = yield list(values)
    return values


def permuted_value(keep, send, background, hold):
    (received,) = yield [swap_cores(send)]
    (received,) = yield from idle([received], hold)
    rows = keep.shape[1] // 2

    def summed(slots, side):
        return sum_pair(keep[slots, side], received[slots, side])

    top, low = slice(0, rows), slice(rows, 2 * rows)
    by_x, by_y = yield [
        background.across(summed(slice(1, 4, 2), top), 1),
        background.across(summed(slice(2, 4), low), 2),
    ]
    first = sum_pair(summed(slice(0, 4, 2), top), by_x)
    second = sum_pair(summed(slice(0, 2), low), by_y)
    by_y, by_x = yield [background.across(first[1], 2), background.across(second[1], 1)]
    return jnp.concatenate([sum_pair(first[0], by_y), sum_pair(second[0], by_x)])


def early_task0(keep, send, background, column):
    value = yield from permuted_value(keep, send, background, 0)
    other = background.add("D", ctx_task(value[:, column:], 0, background, 1))
    mine = yield from ctx_task(value[:, :column], 0, background)
    return mine, other


def late_task0(keep, send, background):
    value = yield from permuted_value(keep, send, background, 0)
    return (yield from ctx_task(value, 0, background))


def early_task1(pack, background, column):
    value = lax.psum_scatter(pack, SHARDS, scatter_dimension=0, tiled=True)
    (value,) = yield [value]
    (value,) = yield [value]
    other = background.add("E", ctx_task(value[:, column:], 1, background))
    mine = yield from ctx_task(value[:, :column], 1, background)
    return mine, other


def late_task1(keep, send, background):
    value = yield from permuted_value(keep, send, background, 2)
    return (yield from ctx_task(value, 1, background))


def ctx_task(value, layer, background, before=0):
    (value,) = yield from idle([value], before)
    if lax.axis_size("ctx") == 4:
        index = lax.axis_index("ctx")
        (received,) = yield [background.send("in", value, "ctx", [(0, 1), (3, 2)])]
        value = sum_pair(value, received)
        (received,) = yield [background.send("mid", value, "ctx", [(1, 2), (2, 1)])]
        value = sum_pair(value, received)
        (received,) = yield [background.send("out", value, "ctx", [(1, 0), (2, 3)])]
        value = jnp.where((index == 0) | (index == 3), received, value)
    else:
        value = lax.psum(value, "ctx")
    (other,) = yield [lax.ppermute(value, "section", [(1 - layer, layer)])]
    return value, other


def return_task(value, layer, pause, background=None):
    (value,) = yield from idle([value], pause)
    flight = yield return_rows(value, layer, background)
    return flight


def sum_pair(a, b):
    return (a.astype(F32) + b.astype(F32)).astype(BF)


def body(
    tokens, cotangent, span_order, w_qkv, w_out, w_up, w_down, norm_gains, bias_rows, bias_hidden
):
    core = lax.axis_index("section")
    ctx = lax.axis_size("ctx")
    cores = lax.axis_size("section")
    shards = lax.axis_size("fsdp")
    half = ctx // cores
    base = lax.axis_index("ctx") // half
    member = core * half + lax.axis_index("ctx") % half
    depth = w_qkv.shape[1]
    width = depth * shards
    ratio = bias_hidden.shape[1] // depth
    size = width // HEADS
    gain_count, shift_count = norm_gains.shape[1], bias_rows.shape[1]

    steps = jnp.arange(ctx, dtype=jnp.int32)
    came, goes = (member - steps) % ctx, (member + steps) % ctx
    shard = lax.axis_index("fsdp")
    slots = [shard ^ k for k in range(shards)] + [core, 1 - core]
    ids = jnp.concatenate([goes, came, jnp.stack(slots)]).astype(jnp.int32)
    order = jnp.concatenate([span_order[came], span_order[goes]])

    small = jnp.concatenate([norm_gains[0], bias_rows[0], bias_hidden[0].reshape(ratio, depth)]).T
    small = jnp.pad(small, ((0, 0), (0, LANES - small.shape[1])))
    first = jnp.concatenate([w_qkv[0], small], axis=1)
    rest = jnp.concatenate([w_out[0], w_up[0]] + blocks_to_columns(w_down[0], ratio), axis=1)
    first0, first1 = split_layers(first, core)
    x = bring_rows(tokens[:, 0], core, base)
    rest0, rest1 = split_layers(rest, core)
    first0, first1 = gather_pieces(first0), gather_pieces(first1)
    rest0, rest1 = gather(rest0), gather(rest1)
    sizes = (ids, order, ctx, size, shards, ratio)
    out0, saved0, _ = layer_forward(x, first0, rest0, *sizes)
    late_cot, out0 = lax.optimization_barrier((cotangent[:, 0], out0))
    out1, saved1, back_out0 = layer_forward(out0, first1, rest1, *sizes, out0)
    cot = bring_rows(late_cot, core, base)
    background = Background()
    grad1, early1, late1, back_out1 = layer_backward(
        saved1, cot, rest1, *sizes, 1, background, out1
    )
    back1 = background.add("A", return_task(grad1, 1, 0))
    grad0, early0, late0, _ = layer_backward(saved0, grad1, rest0, *sizes, 0, background)
    back0 = background.add("A", return_task(grad0, 0, 5, background))
    background.finish()

    def chosen(values0, values1):
        return jnp.stack([jnp.where(core == 0, a, b) for a, b in zip(values0, values1)])

    layer_outputs = chosen(back_out0, back_out1["result"])
    input_grads = chosen(back0["result"], back1["result"]).astype(F32)

    def joined(pair0, pair1):
        return jnp.where(
            core == 0,
            jnp.concatenate([pair0[0], pair0[1]]),
            jnp.concatenate([pair1[1], pair1[0]]),
        ).astype(F32)

    (up0, down0), (up1, down1) = early0["result"], early1["result"]
    early = joined(up0, up1)
    late = joined(late0["result"], late1["result"])
    down = joined(down0["result"], down1["result"])
    table = late[:, 3 * width :].T
    return (
        layer_outputs[None, :, None],
        input_grads[None, :, None],
        late[None, :, : 3 * width],
        early[None, :, :width],
        early[None, :, width:],
        jnp.concatenate([down[:, j * width : (j + 1) * width] for j in range(ratio)])[None],
        table[None, :gain_count],
        table[None, gain_count : gain_count + shift_count],
        table[gain_count + shift_count : gain_count + shift_count + ratio].reshape(1, -1),
    )


def solution(mesh):
    return jax.shard_map(
        body,
        mesh=mesh,
        in_specs=(
            P(None, "fsdp", "ctx", None),
            P(None, "fsdp", "ctx", None),
            P(),
            P("section", "fsdp", None),
            P("section", "fsdp", None),
            P("section", "fsdp", None),
            P("section", "fsdp", None),
            P("section", None, "fsdp"),
            P("section", None, "fsdp"),
            P("section", "fsdp"),
        ),
        out_specs=(
            P("section", None, "fsdp", "ctx", None),
            P("section", None, "fsdp", "ctx", None),
            P("section", "fsdp", None),
            P("section", "fsdp", None),
            P("section", "fsdp", None),
            P("section", "fsdp", None),
            P("section", None, "fsdp"),
            P("section", None, "fsdp"),
            P("section", "fsdp"),
        ),
        check_vma=False,
    )
```

```python
import functools

import jax
import jax.numpy as jnp
from jax import lax
from jax.experimental import pallas as pl
from jax.experimental.pallas import tpu as pltpu
from jax.sharding import PartitionSpec as P

HEADS = 12
EPS = 1e-05
GELU_C = 0.7978845608
GELU_A = 0.044715
LANES = 128
BF = jnp.bfloat16
F32 = jnp.float32
VMEM = pl.BlockSpec(memory_space=pltpu.VMEM)
SMEM = pl.BlockSpec(memory_space=pltpu.SMEM)
HBM = pl.BlockSpec(memory_space=pl.ANY)
PARAMS = pltpu.CompilerParams(vmem_limit_bytes=56 * 1024 * 1024)
GROUP = ("section", "ctx")
SHARDS = ("fsdp", "section")


def dot(a, b, ca, cb):
    return lax.dot_general(a, b, (((ca,), (cb,)), ((), ())), preferred_element_type=F32)


def shape(dims, dtype):
    return jax.ShapeDtypeStruct(dims, dtype)


def place_of(core, ctx_index):
    return core * lax.axis_size("ctx") + ctx_index


def exchange(pieces):
    ctx, cores = lax.axis_size("ctx"), lax.axis_size("section")
    half = ctx // cores
    moved = [pieces[0]]
    for d in range(1, ctx):
        pairs = []
        for base in range(cores):
            for g in range(ctx):
                t = (g + d) % ctx
                pairs.append(
                    (
                        place_of(g // half, base * half + g % half),
                        place_of(t // half, base * half + t % half),
                    )
                )
        moved.append(lax.ppermute(pieces[d], GROUP, pairs))
    return moved


def bring_rows(both, core, base):
    ctx, cores = lax.axis_size("ctx"), lax.axis_size("section")
    half = ctx // cores
    pairs = [
        (place_of(c, c * half + i), place_of(c, (1 - c) * half + i))
        for c in range(cores)
        for i in range(half)
    ]
    received = lax.ppermute(jnp.where(core == 0, both[1], both[0]), GROUP, pairs)
    own = jnp.where(core == 0, both[0], both[1])
    return jnp.where(core == base, own, received)


def return_rows(value, layer, background=None):
    ctx, cores = lax.axis_size("ctx"), lax.axis_size("section")
    half = ctx // cores
    if background is not None and "mid" in background.links:
        value, _ = lax.optimization_barrier((value, background.links["mid"]))
    return [
        lax.ppermute(
            value,
            GROUP,
            [(place_of(z // half, m * half + z % half), place_of(layer, z)) for z in range(ctx)],
        )
        for m in range(cores)
    ]


def normalised(values):
    centred = values - jnp.mean(values, axis=-1, keepdims=True)
    scale = lax.rsqrt(jnp.mean(centred * centred, axis=-1, keepdims=True) + EPS)
    return centred * scale, scale


def norm_back(unit, scale, upstream, gain):
    w = upstream * gain
    return (
        w - jnp.mean(w, axis=-1, keepdims=True) - unit * jnp.mean(w * unit, axis=-1, keepdims=True)
    ) * scale


def piece_places(ids_ref, parts, depth, slots):
    first = 2 * parts
    rows = depth // 2
    places = []
    for side in range(2):
        core = ids_ref[first + slots + side]
        for slot, start, count in (
            (0, 0, rows),
            (1, 0, rows),
            (2, 0, rows),
            (3, 0, rows // 2),
            (3, rows // 2, rows // 2),
        ):
            place = ids_ref[first + slot] * depth + core * rows + start
            places.append((pl.multiple_of(place, 16), count))
    return places


def qkv_kernel(ids_ref, x_ref, *refs, parts, size, shards):
    packs, refs = refs[:10], refs[10:]
    outs, (weight_ref, vec_ref), refs = refs[:parts], refs[parts : parts + 2], refs[parts + 2 :]
    weight, small, whole, sems = refs
    width = x_ref.shape[1]
    copies = []
    for i, (place, count) in enumerate(piece_places(ids_ref, parts, width // shards, shards)):
        for j, target, cols in (
            (0, small, slice(3 * width, 3 * width + LANES)),
            (1, weight, slice(0, 3 * width)),
        ):
            copies.append(
                pltpu.make_async_copy(
                    packs[i].at[:, cols], target.at[pl.ds(place, count)], sems.at[2 * i + j]
                )
            )
    for copy in copies:
        copy.start()
    unit, _ = normalised(x_ref[...].astype(F32))
    for copy in copies:
        copy.wait()
    keep = pltpu.make_async_copy(weight, weight_ref, sems.at[20])
    keep.start()
    vec = small[...].astype(F32).T
    vec_ref[...] = vec[:16]
    normed = (unit * vec[0:1] + vec[2:3]).astype(BF)
    held = outs[0].shape[0] // 3
    if parts * held != width:
        whole[...] = jnp.zeros_like(whole)
    for b in range(3):
        block = dot(normed, weight[:, b * width : (b + 1) * width], 1, 0)
        if b == 0:
            block = block + vec[3:4]
        if b == 2:
            block = block + vec[4:5]
        whole[b * parts * held : b * parts * held + width] = block.T.astype(BF)
    for d in range(parts):
        for b in range(3):
            first = pl.multiple_of(b * parts * held + ids_ref[d] * held, size)
            outs[d][b * held : (b + 1) * held] = whole[pl.ds(first, held)]
    keep.wait()


def qkv_project(ids, x, packs, parts, size, shards):
    rows, width = x.shape
    held = pl.cdiv(HEADS, parts) * size
    results = pl.pallas_call(
        functools.partial(qkv_kernel, parts=parts, size=size, shards=shards),
        in_specs=[SMEM, VMEM] + [HBM] * 10,
        out_specs=[VMEM] * parts + [HBM, VMEM],
        out_shape=[shape((3 * held, rows), BF)] * parts
        + [shape((width, 3 * width), BF), shape((16, width), F32)],
        scratch_shapes=[
            pltpu.VMEM((width, 3 * width), BF),
            pltpu.VMEM((width, LANES), BF),
            pltpu.VMEM((3 * parts * held, rows), BF),
            pltpu.SemaphoreType.DMA((21,)),
        ],
        compiler_params=PARAMS,
        name="qkv_project",
    )(ids, x, *packs)
    return results[:parts], results[parts], results[parts + 1]


def spans_of(order_ref, which, count, span):
    first = order_ref[which]
    return (
        (0, pl.multiple_of(first * span, span)),
        (1, pl.multiple_of((2 * count - 1 - first) * span, span)),
    )


def causal(scores, width, fill):
    depth = scores.shape[0]
    keys = lax.broadcasted_iota(jnp.int32, (width, width), 0)
    rows = lax.broadcasted_iota(jnp.int32, (width, width), 1)
    last = jnp.where(keys <= rows, scores[depth - width :], fill)
    if depth == width:
        return last
    return jnp.concatenate([scores[: depth - width], last], axis=0)


def sort_in(order_ref, pieces, target):
    count = len(pieces)
    span = pieces[0].shape[1] // 2
    for d in range(count):
        for side, place in spans_of(order_ref, d, count, span):
            target[:, pl.ds(place, span)] = pieces[d][:, side * span : (side + 1) * span]


def sort_out(order_ref, source, pieces):
    count = len(pieces)
    span = pieces[0].shape[1] // 2
    for d in range(count):
        for side, place in spans_of(order_ref, count + d, count, span):
            pieces[d][:, side * span : (side + 1) * span] = source[:, pl.ds(place, span)]


def attn_fwd_kernel(order_ref, *refs, parts, heads, size, block):
    pieces, mixed, (sorted_ref, out_ref, lse_ref) = refs[:parts], refs[parts : 2 * parts], refs[2 * parts :]
    feats = heads * size
    seq = sorted_ref.shape[1]
    sort_in(order_ref, pieces, sorted_ref)
    lse_ref[...] = jnp.zeros_like(lse_ref)
    for h in range(heads):
        for start in range(0, seq, block):
            end = start + block
            q = sorted_ref[h * size : (h + 1) * size, start:end]
            k = sorted_ref[feats + h * size : feats + (h + 1) * size, :end]
            v = sorted_ref[2 * feats + h * size : 2 * feats + (h + 1) * size, :end]
            scores = causal(dot(k, q, 0, 0) * 0.125, block, -1e30)
            top = jnp.max(scores, axis=0, keepdims=True)
            weights = jnp.exp(scores - top)
            total = jnp.sum(weights, axis=0, keepdims=True)
            mixed_part = dot(v, weights.astype(BF), 1, 0) / total
            out_ref[h * size : (h + 1) * size, start:end] = mixed_part.astype(BF)
            lse_ref[h : h + 1, start:end] = top + jnp.log(total)
    sort_out(order_ref, out_ref, mixed)


def attn_bwd_kernel(order_ref, *refs, parts, heads, size, block):
    pieces, (sorted_ref, out_ref, lse_ref) = refs[:parts], refs[parts : parts + 3]
    grads, (dsort, gsort, gk, gv) = refs[parts + 3 : 2 * parts + 3], refs[2 * parts + 3 :]
    feats = heads * size
    seq = sorted_ref.shape[1]
    sort_in(order_ref, pieces, dsort)
    for h in range(heads):
        own = slice(h * size, (h + 1) * size)
        gk[...] = jnp.zeros_like(gk)
        gv[...] = jnp.zeros_like(gv)
        for start in range(0, seq, block):
            end = start + block
            q = sorted_ref[own, start:end]
            k = sorted_ref[feats + h * size : feats + (h + 1) * size, :end]
            v = sorted_ref[2 * feats + h * size : 2 * feats + (h + 1) * size, :end]
            dout = dsort[own, start:end]
            delta = jnp.sum(
                dout.astype(F32) * out_ref[own, start:end].astype(F32), axis=0, keepdims=True
            )
            scores = dot(k, q, 0, 0) * 0.125 - lse_ref[h : h + 1, start:end]
            probs = jnp.exp(causal(scores, block, -1e30))
            dprobs = dot(v, dout, 0, 0)
            dscores = (probs * (dprobs - delta)).astype(BF)
            gsort[own, start:end] = (dot(k, dscores, 1, 0) * 0.125).astype(BF)
            gk[:, :end] += dot(q, dscores, 1, 1)
            gv[:, :end] += dot(dout, probs.astype(BF), 1, 1)
        gsort[feats + h * size : feats + (h + 1) * size, :] = (gk[...] * 0.125).astype(BF)
        gsort[2 * feats + h * size : 2 * feats + (h + 1) * size, :] = gv[...].astype(BF)
    sort_out(order_ref, gsort, grads)


def widen(pieces, order):
    count = len(pieces)
    span = pieces[0].shape[1] // 2
    came = order[:count]
    holder = jnp.stack([came, 2 * count - 1 - came], axis=1).reshape(-1)
    place = jnp.argsort(holder)
    flat = jnp.concatenate(pieces, axis=1).reshape(-1, 2 * count, span)
    return [jnp.take(flat, place, axis=1).reshape(flat.shape[0], -1)]


def narrow(wide, order, count):
    feats, seq = wide.shape
    span = seq // (2 * count)
    goes = order[count:]
    holder = jnp.stack([goes, 2 * count - 1 - goes], axis=1).reshape(-1)
    flat = jnp.take(wide.reshape(feats, 2 * count, span), holder, axis=1)
    flat = flat.reshape(feats, count, 2 * span)
    return [flat[:, d] for d in range(count)]


def attention_forward(pieces, order, size):
    parts, rows = len(pieces), pieces[0].shape[1]
    seq = parts * rows
    heads = pieces[0].shape[0] // (3 * size)
    narrow_spans = (rows // 2) % LANES != 0
    ids, given = order, parts
    if narrow_spans:
        pieces, ids, given = widen(pieces, order), jnp.zeros((2,), jnp.int32), 1
    results = pl.pallas_call(
        functools.partial(
            attn_fwd_kernel, parts=given, heads=heads, size=size, block=min(256, seq // 2)
        ),
        in_specs=[SMEM] + [VMEM] * given,
        out_specs=[VMEM] * (given + 3),
        out_shape=[shape((heads * size, pieces[0].shape[1]), BF)] * given
        + [
            shape((3 * heads * size, seq), BF),
            shape((heads * size, seq), BF),
            shape((8 * pl.cdiv(heads, 8), seq), F32),
        ],
        compiler_params=PARAMS,
        name="attn_fwd",
    )(ids, *pieces)
    mixed = results[:given]
    if narrow_spans:
        mixed = narrow(mixed[0], order, parts)
    return mixed, tuple(results[given:])


def attention_backward(pieces, saved, order, size):
    parts, rows = len(pieces), pieces[0].shape[1]
    seq = parts * rows
    heads = pieces[0].shape[0] // size
    narrow_spans = (rows // 2) % LANES != 0
    ids, given = order, parts
    if narrow_spans:
        pieces, ids, given = widen(pieces, order), jnp.zeros((2,), jnp.int32), 1
    grads = pl.pallas_call(
        functools.partial(
            attn_bwd_kernel, parts=given, heads=heads, size=size, block=min(256, seq // 2)
        ),
        in_specs=[SMEM] + [VMEM] * (given + 3),
        out_specs=[VMEM] * given,
        out_shape=[shape((3 * heads * size, pieces[0].shape[1]), BF)] * given,
        scratch_shapes=[
            pltpu.VMEM((heads * size, seq), BF),
            pltpu.VMEM((3 * heads * size, seq), BF),
            pltpu.VMEM((size, seq), F32),
            pltpu.VMEM((size, seq), F32),
        ],
        compiler_params=PARAMS,
        name="attn_bwd",
    )(ids, *pieces, *saved)
    if narrow_spans:
        grads = narrow(grads[0], order, parts)
    return grads


def down_blocks(shards, ratio, depth):
    width = shards * depth
    for f in range(shards):
        for j in range(ratio):
            first = (f * ratio + j) * depth
            yield slice(first, first + depth), slice(f * depth, (f + 1) * depth), j * width


def rest_copies(pack, w_out, w_up, w_down, sems, shards, ratio):
    width = w_out.shape[0]
    depth = width // shards
    hidden = w_up.shape[1]
    out = [pltpu.make_async_copy(pack.at[:, :width], w_out, sems.at[0])]
    up = [pltpu.make_async_copy(pack.at[:, width : width + hidden], w_up, sems.at[1])]
    down = []
    for i, (rows, packed, column) in enumerate(down_blocks(shards, ratio, depth)):
        start = width + hidden + column
        down.append(
            pltpu.make_async_copy(
                pack.at[packed, start : start + width], w_down.at[rows], sems.at[2 + i]
            )
        )
    return out, up, down


def put_pieces(ids_ref, first, pieces, target):
    held = pieces[0].shape[0]
    for d, piece in enumerate(pieces):
        place = pl.multiple_of(ids_ref[first + d] * held, held)
        target[pl.ds(place, held)] = piece[...]


def mlp_kernel(ids_ref, x_ref, vec_ref, bias_ref, pack_ref, *refs, parts, shards, ratio):
    pieces = refs[:parts]
    result_ref, inner_ref, hidden_ref, mixed_ref = refs[parts : parts + 4]
    w_out, w_up, w_down, whole, sems = refs[parts + 4 :]
    width = x_ref.shape[1]
    out, up, down = rest_copies(pack_ref, w_out, w_up, w_down, sems, shards, ratio)
    for copy in out + up + down:
        copy.start()
    put_pieces(ids_ref, parts, pieces, whole)
    mixed_ref[...] = whole[:width]
    out[0].wait()
    inner = x_ref[...].astype(F32) + dot(whole[:width], w_out[...], 0, 0) + vec_ref[5:6]
    inner_ref[...] = inner
    unit, _ = normalised(inner)
    middle = (unit * vec_ref[1:2] + vec_ref[6:7]).astype(BF)
    up[0].wait()
    for copy in down:
        copy.wait()
    total = inner + vec_ref[7:8]
    for start in range(0, w_up.shape[1], width):
        cols = slice(start, start + width)
        hidden = dot(middle, w_up[:, cols], 1, 0) + bias_ref[:, cols]
        hidden_ref[:, cols] = hidden
        act = 0.5 * hidden * (1.0 + jnp.tanh(GELU_C * (hidden + GELU_A * hidden * hidden * hidden)))
        total = total + dot(act.astype(BF), w_down[cols], 1, 0)
    result_ref[...] = total.astype(BF)


def rest_scratch(width, hidden, shards, ratio):
    return [
        pltpu.VMEM((width, width), BF),
        pltpu.VMEM((width, hidden), BF),
        pltpu.VMEM((hidden, width), BF),
    ]


def mlp_forward(ids, x, vec, bias, pack, pieces, shards, ratio):
    parts = len(pieces)
    rows, width = x.shape
    hidden = ratio * width
    return pl.pallas_call(
        functools.partial(mlp_kernel, parts=parts, shards=shards, ratio=ratio),
        in_specs=[SMEM, VMEM, VMEM, VMEM, HBM] + [VMEM] * parts,
        out_specs=[VMEM] * 4,
        out_shape=[
            shape((rows, width), BF),
            shape((rows, width), F32),
            shape((rows, hidden), F32),
            shape((width, rows), BF),
        ],
        scratch_shapes=rest_scratch(width, hidden, shards, ratio)
        + [
            pltpu.VMEM((parts * pieces[0].shape[0], rows), BF),
            pltpu.SemaphoreType.DMA((2 + shards * ratio,)),
        ],
        compiler_params=PARAMS,
        name="mlp_forward",
    )(ids, x, vec, bias, pack, *pieces)


def mlp_back_kernel(
    ids_ref, grad_ref, inner_ref, hidden_ref, vec_ref, pack_ref, *refs, parts, shards, ratio
):
    outs = refs[:parts]
    ginner_ref, gattn_ref, ghid_ref, act_ref, middle_ref, table_ref = refs[parts : parts + 6]
    w_out, w_up, w_down, whole, sems = refs[parts + 6 :]
    width = grad_ref.shape[1]
    out, up, down = rest_copies(pack_ref, w_out, w_up, w_down, sems, shards, ratio)
    for copy in down + up + out:
        copy.start()
    grad_low = grad_ref[...].astype(BF)
    unit, scale = normalised(inner_ref[...])
    middle_ref[...] = (unit * vec_ref[1:2] + vec_ref[6:7]).astype(BF)
    for copy in down:
        copy.wait()
    up[0].wait()
    up_mid = jnp.zeros(unit.shape, F32)
    depth = width // shards
    table_ref[...] = jnp.zeros_like(table_ref)
    for start in range(0, w_up.shape[1], width):
        cols = slice(start, start + width)
        hidden = hidden_ref[:, cols]
        th = jnp.tanh(GELU_C * (hidden + GELU_A * hidden * hidden * hidden))
        act_ref[:, cols] = (0.5 * hidden * (1.0 + th)).astype(BF)
        slope = 0.5 * (1.0 + th) + 0.5 * hidden * (1.0 - th * th) * GELU_C * (
            1.0 + 3.0 * GELU_A * hidden * hidden
        )
        grad_hid = (dot(grad_low, w_down[cols], 1, 1) * slope).astype(BF)
        ghid_ref[:, cols] = grad_hid
        sums = jnp.sum(grad_hid.astype(F32), axis=0, keepdims=True)
        for i in range(width // depth):
            f, j = divmod(start // depth + i, ratio)
            table_ref[8 + j : 9 + j, f * depth : (f + 1) * depth] = sums[:, i * depth : (i + 1) * depth]
        up_mid = up_mid + dot(grad_hid, w_up[:, cols], 1, 1)
    grad_inner = grad_ref[...].astype(F32) + norm_back(unit, scale, up_mid, vec_ref[1:2])
    ginner_ref[...] = grad_inner
    grad_attn = grad_inner.astype(BF)
    gattn_ref[...] = grad_attn
    out[0].wait()
    held = outs[0].shape[0]
    if parts * held != width:
        whole[...] = jnp.zeros_like(whole)
    whole[:width] = dot(w_out[...], grad_attn, 1, 1).astype(BF)
    for d in range(parts):
        outs[d][...] = whole[pl.ds(pl.multiple_of(ids_ref[d] * held, held), held)]
    table_ref[1:2] = jnp.sum(up_mid * unit, axis=0, keepdims=True)
    table_ref[5:6] = jnp.sum(grad_attn.astype(F32), axis=0, keepdims=True)
    table_ref[6:7] = jnp.sum(up_mid, axis=0, keepdims=True)
    table_ref[7:8] = jnp.sum(grad_low.astype(F32), axis=0, keepdims=True)


def mlp_backward(ids, grad, inner, hidden, vec, pack, parts, size, shards, ratio):
    rows, width = inner.shape
    held = pl.cdiv(HEADS, parts) * size
    wide = ratio * width
    results = pl.pallas_call(
        functools.partial(mlp_back_kernel, parts=parts, shards=shards, ratio=ratio),
        in_specs=[SMEM, VMEM, VMEM, VMEM, VMEM, HBM],
        out_specs=[VMEM] * (parts + 6),
        out_shape=[shape((held, rows), BF)] * parts
        + [
            shape((rows, width), F32),
            shape((rows, width), BF),
            shape((rows, wide), BF),
            shape((rows, wide), BF),
            shape((rows, width), BF),
            shape((LANES, width), F32),
        ],
        scratch_shapes=rest_scratch(width, wide, shards, ratio)
        + [
            pltpu.VMEM((parts * held, rows), BF),
            pltpu.SemaphoreType.DMA((2 + shards * ratio,)),
        ],
        compiler_params=PARAMS,
        name="mlp_backward",
    )(ids, grad, inner, hidden, vec, pack)
    return results[:parts], results[parts:]


def write_down(act_ref, glow_ref, pack, start, shards, ratio):
    width = glow_ref.shape[1]
    depth = width // shards
    glow = glow_ref[...].astype(BF)
    for f in range(shards):
        block = dot(act_ref[:, f * ratio * depth : (f + 1) * ratio * depth], glow, 0, 0).astype(BF)
        for j in range(ratio):
            first = start + j * width
            pack[f * depth : (f + 1) * depth, first : first + width] = block[
                j * depth : (j + 1) * depth
            ]


def send_sides(ids_ref, first, pack, start, count, targets, sems, offset, shards):
    depth = pack.shape[0] // shards
    rows = depth // 2
    copies = []
    for side in range(2):
        core = ids_ref[first + shards + side]
        for k in range(shards):
            place = pl.multiple_of(ids_ref[first + k] * depth + core * rows, 16)
            copies.append(
                pltpu.make_async_copy(
                    pack.at[pl.ds(place, rows), start : start + count],
                    targets[side].at[k],
                    sems.at[offset + side * shards + k],
                )
            )
    for copy in copies:
        copy.start()
    return copies


def early_kernel(
    ids_ref, middle_ref, ghid_ref, mixed_ref, gattn_ref, act_ref, glow_ref, *refs, parts, shards, ratio, apart
):
    if apart:
        outs, (scratch, sems) = refs[:2], refs[2:]
    else:
        pack_ref, scratch, sems = refs
    width = middle_ref.shape[1]
    main = (1 + ratio) * width
    copies = []

    def send(columns, i):
        copy = pltpu.make_async_copy(scratch.at[:, columns], pack_ref.at[:, columns], sems.at[i])
        copy.start()
        copies.append(copy)

    scratch[:, :width] = dot(mixed_ref[...], gattn_ref[...], 1, 0).astype(BF)
    for i in range(ratio):
        cols = slice(i * width, (i + 1) * width)
        block = dot(middle_ref[...], ghid_ref[:, cols], 0, 0).astype(BF)
        scratch[:, (i + 1) * width : (i + 2) * width] = block
    if not apart:
        send(slice(0, main), 0)
    write_down(act_ref, glow_ref, scratch, main, shards, ratio)
    if apart:
        copies += send_sides(
            ids_ref, 2 * parts, scratch, 0, main + ratio * width, outs, sems, 0, shards
        )
    else:
        send(slice(main, main + ratio * width), 1)
    for copy in copies:
        copy.wait()


def early_grads(ids, middle, ghid, mixed, gattn, act, grad, parts, shards, ratio, apart):
    width = middle.shape[1]
    main, hidden = (1 + ratio) * width, ratio * width
    rows = width // shards // 2
    side = shape((shards, rows, main + hidden), BF)
    return pl.pallas_call(
        functools.partial(early_kernel, parts=parts, shards=shards, ratio=ratio, apart=apart),
        in_specs=[SMEM] + [VMEM] * 6,
        out_specs=[HBM] * (2 if apart else 1),
        out_shape=[side, side] if apart else [shape((width, main + hidden), BF)],
        scratch_shapes=[
            pltpu.VMEM((width, main + hidden), BF),
            pltpu.SemaphoreType.DMA((2 + 2 * shards,)),
        ],
        compiler_params=PARAMS,
        name="early_grads",
    )(ids, middle, ghid, mixed, gattn, act, grad)


def qkv_back_kernel(
    ids_ref, x_ref, ginner_ref, vec_ref, table_ref, weight_hbm, *refs, parts, shards
):
    pieces, refs = refs[:parts], refs[parts:]
    gx_ref, *outs, weight, whole, pack, sem = refs
    width = x_ref.shape[1]
    main = 3 * width + LANES
    copies = []
    copy = pltpu.make_async_copy(weight_hbm, weight, sem.at[0])
    copy.start()
    held = pieces[0].shape[0] // 3
    padded = parts * held
    for d, piece in enumerate(pieces):
        for b in range(3):
            place = pl.multiple_of(b * padded + ids_ref[parts + d] * held, held)
            whole[pl.ds(place, held)] = piece[b * held : (b + 1) * held]
    unit, scale = normalised(x_ref[...].astype(F32))
    normed = (unit * vec_ref[0:1] + vec_ref[2:3]).T.astype(BF)
    copy.wait()
    up_norm = jnp.zeros((width, x_ref.shape[0]), F32)
    sums = []
    for b in range(3):
        grads = whole[b * padded : b * padded + width]
        cols = slice(b * width, (b + 1) * width)
        up_norm = up_norm + dot(weight[:, cols], grads, 1, 0)
        pack[:, cols] = dot(normed, grads, 1, 1).astype(BF)
        sums.append(jnp.sum(grads.astype(F32), axis=1, keepdims=True))
    up_norm = up_norm.T
    gx_ref[...] = (ginner_ref[...] + norm_back(unit, scale, up_norm, vec_ref[0:1])).astype(BF)
    line = lax.broadcasted_iota(jnp.int32, table_ref.shape, 0)
    table = jnp.where(
        line == 0,
        jnp.sum(up_norm * unit, axis=0, keepdims=True),
        jnp.where(line == 2, jnp.sum(up_norm, axis=0, keepdims=True), table_ref[...]),
    ).T
    lane = lax.broadcasted_iota(jnp.int32, table.shape, 1)
    table = jnp.where(lane == 3, sums[0], jnp.where(lane == 4, sums[2], table))
    pack[:, 3 * width : main] = table.astype(BF)
    copies += send_sides(ids_ref, 2 * parts, pack, 0, main, outs, sem, 1, shards)
    for copy in copies:
        copy.wait()


def qkv_backward(ids, x, ginner, vec, table, weight, pieces, shards):
    parts = len(pieces)
    rows, width = x.shape
    total = 3 * width + LANES
    part = shape((shards, width // shards // 2, total), BF)
    return pl.pallas_call(
        functools.partial(qkv_back_kernel, parts=parts, shards=shards),
        in_specs=[SMEM, VMEM, VMEM, VMEM, VMEM, HBM] + [VMEM] * parts,
        out_specs=[VMEM, HBM, HBM],
        out_shape=[shape((rows, width), BF), part, part],
        scratch_shapes=[
            pltpu.VMEM((width, 3 * width), BF),
            pltpu.VMEM((parts * pieces[0].shape[0], rows), BF),
            pltpu.VMEM((width, total), BF),
            pltpu.SemaphoreType.DMA((1 + 2 * shards,)),
        ],
        compiler_params=PARAMS,
        name="qkv_backward",
    )(ids, x, ginner, vec, table, weight, *pieces)


def layer_forward(x, packs, rest, ids, order, parts, size, shards, ratio, back=None):
    sent, weight, vec = qkv_project(ids, x, packs, parts, size, shards)
    width = x.shape[1]
    depth = width // shards
    bias = vec[8 : 8 + ratio].reshape(ratio, shards, depth).transpose(1, 0, 2).reshape(1, -1)
    received = exchange(sent)
    returned = None
    if back is not None:
        *received, back = lax.optimization_barrier((*received, back))
        returned = return_rows(back, 0)
    mixed, attn_saved = attention_forward(received, order, size)
    received = exchange(mixed)
    if back is not None:
        tied = lax.optimization_barrier((*received, *returned))
        received, returned = tied[:parts], tied[parts:]
    result, inner, hidden, mixed = mlp_forward(
        ids, x, vec, bias, rest, received, shards, ratio
    )
    return result, (x, weight, vec, attn_saved, inner, hidden, mixed), returned


def layer_backward(
    saved, grad, rest, ids, order, parts, size, shards, ratio, layer, background, result=None
):
    x, weight, vec, attn_saved, inner, hidden, mixed = saved
    last = layer == 0
    column = (1 + ratio) * x.shape[1]
    sent, (ginner, gattn, ghid, act, middle, table) = mlp_backward(
        ids, grad, inner, hidden, vec, rest, parts, size, shards, ratio
    )
    received = exchange(background.slot("AD", sent))
    early = early_grads(ids, middle, ghid, mixed, gattn, act, grad, parts, shards, ratio, last)
    tied = lax.optimization_barrier((*received, *early, result if result is not None else grad))
    received, early = tied[:parts], tied[parts:-1]
    returned = None
    if last:
        first = background.add("B", early_task0(*early, background, column))
    else:
        first = background.add("C", early_task1(*early, background, column))
        returned = background.add("A", return_task(tied[-1], layer, 0))
    sent = attention_backward(received, attn_saved, order, size)
    sent = background.slot("BC" if last else "A", sent)
    received = exchange(sent)
    if last:
        received = background.slot("CD", received)
    grad_x, *late = lax.optimization_barrier(
        tuple(qkv_backward(ids, x, ginner, vec, table, weight, received, shards))
    )
    if last:
        background.slot("B", [grad_x])
        second = background.add("A", late_task0(*late, background))
    else:
        second = background.add("D", late_task1(*late, background))
    return grad_x, first, second, returned


def blocks_to_columns(value, parts):
    depth = value.shape[0] // parts
    return [value[i * depth : (i + 1) * depth] for i in range(parts)]


def split_layers(pack, core):
    rows = pack.shape[0] // 2
    first, second = pack[:rows], pack[rows:]
    other = lax.ppermute(jnp.where(core == 0, second, first), "section", [(0, 1), (1, 0)])
    return jnp.where(core == 0, first, other), jnp.where(core == 0, other, second)


def gather(part):
    return lax.all_gather(part, SHARDS, axis=0, tiled=True)


def across(value, bit):
    count = lax.axis_size("fsdp")
    return lax.ppermute(value, "fsdp", [(i, i ^ bit) for i in range(count)])


def swap_cores(value):
    return lax.ppermute(value, "section", [(0, 1), (1, 0)])


def gather_pieces(part):
    rows = part.shape[0] // 2
    by_x, by_y = across(part, 1), across(part, 2)
    pieces = [part, by_x, by_y, across(by_x[:rows], 2), across(by_y[rows:], 1)]
    return pieces + [swap_cores(piece) for piece in pieces]


class Background:
    def __init__(self):
        self.tasks = []
        self.links = {}

    def send(self, link, value, axis, pairs):
        before = [self.links[name] for name in (link, "sums") if name in self.links]
        if len(before) > 0:
            value, *_ = lax.optimization_barrier((value, *before))
        moved = lax.ppermute(value, axis, pairs)
        self.links[link] = moved
        return moved

    def across(self, value, bit):
        count = lax.axis_size("fsdp")
        return self.send(bit, value, "fsdp", [(i, i ^ bit) for i in range(count)])

    def add(self, lane, task):
        entry = {"lane": lane, "task": task, "result": None}
        entry["flight"] = next(task)
        self.tasks.append(entry)
        return entry

    def resume(self, entry, flight):
        try:
            entry["flight"] = entry["task"].send(flight)
        except StopIteration as stop:
            entry["flight"], entry["result"] = None, stop.value

    def slot(self, lanes, values=()):
        waiting = [e for e in self.tasks if e["flight"] is not None and e["lane"] in lanes]
        flat = list(values)
        for entry in waiting:
            flat += entry["flight"]
        if len(flat) > 0:
            flat = list(lax.optimization_barrier(tuple(flat)))
        values, flat = flat[: len(values)], flat[len(values) :]
        for entry in waiting:
            count = len(entry["flight"])
            self.resume(entry, flat[:count])
            flat = flat[count:]
        return values

    def finish(self):
        while any(entry["flight"] is not None for entry in self.tasks):
            for entry in list(self.tasks):
                if entry["flight"] is not None:
                    self.resume(entry, entry["flight"])


def idle(values, slots):
    for _ in range(slots):
        values = yield list(values)
    return values


def permuted_value(keep, send, background, hold):
    (received,) = yield [swap_cores(send)]
    (received,) = yield from idle([received], hold)
    rows = keep.shape[1] // 2

    def summed(slots, side):
        return sum_pair(keep[slots, side], received[slots, side])

    top, low = slice(0, rows), slice(rows, 2 * rows)
    by_x, by_y = yield [
        background.across(summed(slice(1, 4, 2), top), 1),
        background.across(summed(slice(2, 4), low), 2),
    ]
    first = sum_pair(summed(slice(0, 4, 2), top), by_x)
    second = sum_pair(summed(slice(0, 2), low), by_y)
    flight = [background.across(first[1], 2), background.across(second[1], 1)]
    background.links.setdefault("sums", first)
    by_y, by_x = yield flight
    return jnp.concatenate([sum_pair(first[0], by_y), sum_pair(second[0], by_x)])


def early_task0(keep, send, background, column):
    value = yield from permuted_value(keep, send, background, 0)
    other = background.add("D", ctx_task(value[:, column:], 0, background, 1))
    mine = yield from ctx_task(value[:, :column], 0, background)
    return mine, other


def late_task0(keep, send, background):
    value = yield from permuted_value(keep, send, background, 0)
    return (yield from ctx_task(value, 0, background))


def early_task1(pack, background, column):
    value = lax.psum_scatter(pack, SHARDS, scatter_dimension=0, tiled=True)
    (value,) = yield [value]
    (value,) = yield [value]
    other = background.add("E", ctx_task(value[:, column:], 1, background))
    mine = yield from ctx_task(value[:, :column], 1, background, 1)
    return mine, other


def late_task1(keep, send, background):
    value = yield from permuted_value(keep, send, background, 2)
    return (yield from ctx_task(value, 1, background))


def ctx_task(value, layer, background, before=0):
    (value,) = yield from idle([value], before)
    if lax.axis_size("ctx") == 4:
        index = lax.axis_index("ctx")
        (received,) = yield [background.send("in", value, "ctx", [(0, 1), (3, 2)])]
        value = sum_pair(value, received)
        (received,) = yield [background.send("mid", value, "ctx", [(1, 2), (2, 1)])]
        value = sum_pair(value, received)
        (received,) = yield [background.send("out", value, "ctx", [(1, 0), (2, 3)])]
        value = jnp.where((index == 0) | (index == 3), received, value)
    else:
        value = lax.psum(value, "ctx")
    (other,) = yield [lax.ppermute(value, "section", [(1 - layer, layer)])]
    return value, other


def return_task(value, layer, pause, background=None):
    (value,) = yield from idle([value], pause)
    flight = yield return_rows(value, layer, background)
    return flight


def sum_pair(a, b):
    return (a.astype(F32) + b.astype(F32)).astype(BF)


def body(
    tokens, cotangent, span_order, w_qkv, w_out, w_up, w_down, norm_gains, bias_rows, bias_hidden
):
    core = lax.axis_index("section")
    ctx = lax.axis_size("ctx")
    cores = lax.axis_size("section")
    shards = lax.axis_size("fsdp")
    half = ctx // cores
    base = lax.axis_index("ctx") // half
    member = core * half + lax.axis_index("ctx") % half
    depth = w_qkv.shape[1]
    width = depth * shards
    ratio = bias_hidden.shape[1] // depth
    size = width // HEADS
    gain_count, shift_count = norm_gains.shape[1], bias_rows.shape[1]

    steps = jnp.arange(ctx, dtype=jnp.int32)
    came, goes = (member - steps) % ctx, (member + steps) % ctx
    shard = lax.axis_index("fsdp")
    slots = [shard ^ k for k in range(shards)] + [core, 1 - core]
    ids = jnp.concatenate([goes, came, jnp.stack(slots)]).astype(jnp.int32)
    order = jnp.concatenate([span_order[came], span_order[goes]])

    small = jnp.concatenate([norm_gains[0], bias_rows[0], bias_hidden[0].reshape(ratio, depth)]).T
    small = jnp.pad(small, ((0, 0), (0, LANES - small.shape[1])))
    first = jnp.concatenate([w_qkv[0], small], axis=1)
    rest = jnp.concatenate([w_out[0], w_up[0]] + blocks_to_columns(w_down[0], ratio), axis=1)
    first0, first1 = split_layers(first, core)
    x = bring_rows(tokens[:, 0], core, base)
    rest0, rest1 = split_layers(rest, core)
    first0, first1 = gather_pieces(first0), gather_pieces(first1)
    rest0, rest1 = gather(rest0), gather(rest1)
    sizes = (ids, order, ctx, size, shards, ratio)
    out0, saved0, _ = layer_forward(x, first0, rest0, *sizes)
    late_cot, out0 = lax.optimization_barrier((cotangent[:, 0], out0))
    out1, saved1, back_out0 = layer_forward(out0, first1, rest1, *sizes, out0)
    cot = bring_rows(late_cot, core, base)
    background = Background()
    grad1, early1, late1, back_out1 = layer_backward(
        saved1, cot, rest1, *sizes, 1, background, out1
    )
    back1 = background.add("A", return_task(grad1, 1, 0))
    grad0, early0, late0, _ = layer_backward(saved0, grad1, rest0, *sizes, 0, background)
    back0 = background.add("A", return_task(grad0, 0, 5, background))
    background.finish()

    def chosen(values0, values1):
        return jnp.stack([jnp.where(core == 0, a, b) for a, b in zip(values0, values1)])

    layer_outputs = chosen(back_out0, back_out1["result"])
    input_grads = chosen(back0["result"], back1["result"]).astype(F32)

    def joined(pair0, pair1):
        return jnp.where(
            core == 0,
            jnp.concatenate([pair0[0], pair0[1]]),
            jnp.concatenate([pair1[1], pair1[0]]),
        ).astype(F32)

    (up0, down0), (up1, down1) = early0["result"], early1["result"]
    early = joined(up0, up1)
    late = joined(late0["result"], late1["result"])
    down = joined(down0["result"], down1["result"])
    table = late[:, 3 * width :].T
    return (
        layer_outputs[None, :, None],
        input_grads[None, :, None],
        late[None, :, : 3 * width],
        early[None, :, :width],
        early[None, :, width:],
        jnp.concatenate([down[:, j * width : (j + 1) * width] for j in range(ratio)])[None],
        table[None, :gain_count],
        table[None, gain_count : gain_count + shift_count],
        table[gain_count + shift_count : gain_count + shift_count + ratio].reshape(1, -1),
    )


def solution(mesh):
    return jax.shard_map(
        body,
        mesh=mesh,
        in_specs=(
            P(None, "fsdp", "ctx", None),
            P(None, "fsdp", "ctx", None),
            P(),
            P("section", "fsdp", None),
            P("section", "fsdp", None),
            P("section", "fsdp", None),
            P("section", "fsdp", None),
            P("section", None, "fsdp"),
            P("section", None, "fsdp"),
            P("section", "fsdp"),
        ),
        out_specs=(
            P("section", None, "fsdp", "ctx", None),
            P("section", None, "fsdp", "ctx", None),
            P("section", "fsdp", None),
            P("section", "fsdp", None),
            P("section", "fsdp", None),
            P("section", "fsdp", None),
            P("section", None, "fsdp"),
            P("section", None, "fsdp"),
            P("section", "fsdp"),
        ),
        check_vma=False,
    )
```

```python
import functools

import jax
import jax.numpy as jnp
from jax import lax
from jax.experimental import pallas as pl
from jax.experimental.pallas import tpu as pltpu
from jax.sharding import PartitionSpec as P

HEADS = 12
EPS = 1e-05
GELU_C = 0.7978845608
GELU_A = 0.044715
LANES = 128
BF = jnp.bfloat16
F32 = jnp.float32
VMEM = pl.BlockSpec(memory_space=pltpu.VMEM)
SMEM = pl.BlockSpec(memory_space=pltpu.SMEM)
HBM = pl.BlockSpec(memory_space=pl.ANY)
PARAMS = pltpu.CompilerParams(vmem_limit_bytes=56 * 1024 * 1024)
GROUP = ("section", "ctx")
SHARDS = ("fsdp", "section")


def dot(a, b, ca, cb):
    return lax.dot_general(a, b, (((ca,), (cb,)), ((), ())), preferred_element_type=F32)


def shape(dims, dtype):
    return jax.ShapeDtypeStruct(dims, dtype)


def place_of(core, ctx_index):
    return core * lax.axis_size("ctx") + ctx_index


def exchange(pieces):
    ctx, cores = lax.axis_size("ctx"), lax.axis_size("section")
    half = ctx // cores
    moved = [pieces[0]]
    for d in range(1, ctx):
        pairs = []
        for base in range(cores):
            for g in range(ctx):
                t = (g + d) % ctx
                pairs.append(
                    (
                        place_of(g // half, base * half + g % half),
                        place_of(t // half, base * half + t % half),
                    )
                )
        moved.append(lax.ppermute(pieces[d], GROUP, pairs))
    return moved


def bring_rows(both, core, base):
    ctx, cores = lax.axis_size("ctx"), lax.axis_size("section")
    half = ctx // cores
    pairs = [
        (place_of(c, c * half + i), place_of(c, (1 - c) * half + i))
        for c in range(cores)
        for i in range(half)
    ]
    received = lax.ppermute(jnp.where(core == 0, both[1], both[0]), GROUP, pairs)
    own = jnp.where(core == 0, both[0], both[1])
    return jnp.where(core == base, own, received)


def return_rows(value, layer, background=None):
    ctx, cores = lax.axis_size("ctx"), lax.axis_size("section")
    half = ctx // cores
    if background is not None and "mid" in background.links:
        value, _ = lax.optimization_barrier((value, background.links["mid"]))
    return [
        lax.ppermute(
            value,
            GROUP,
            [(place_of(z // half, m * half + z % half), place_of(layer, z)) for z in range(ctx)],
        )
        for m in range(cores)
    ]


def normalised(values):
    centred = values - jnp.mean(values, axis=-1, keepdims=True)
    scale = lax.rsqrt(jnp.mean(centred * centred, axis=-1, keepdims=True) + EPS)
    return centred * scale, scale


def norm_back(unit, scale, upstream, gain):
    w = upstream * gain
    return (
        w - jnp.mean(w, axis=-1, keepdims=True) - unit * jnp.mean(w * unit, axis=-1, keepdims=True)
    ) * scale


def piece_places(ids_ref, parts, depth, slots):
    first = 2 * parts
    rows = depth // 2
    places = []
    for side in range(2):
        core = ids_ref[first + slots + side]
        for slot, start, count in (
            (0, 0, rows),
            (1, 0, rows),
            (2, 0, rows),
            (3, 0, rows // 2),
            (3, rows // 2, rows // 2),
        ):
            place = ids_ref[first + slot] * depth + core * rows + start
            places.append((pl.multiple_of(place, 16), count))
    return places


def qkv_kernel(ids_ref, x_ref, *refs, parts, size, shards):
    packs, refs = refs[:10], refs[10:]
    outs, (weight_ref, vec_ref), refs = refs[:parts], refs[parts : parts + 2], refs[parts + 2 :]
    weight, small, whole, sems = refs
    width = x_ref.shape[1]
    copies = []
    for i, (place, count) in enumerate(piece_places(ids_ref, parts, width // shards, shards)):
        for j, target, cols in (
            (0, small, slice(3 * width, 3 * width + LANES)),
            (1, weight, slice(0, 3 * width)),
        ):
            copies.append(
                pltpu.make_async_copy(
                    packs[i].at[:, cols], target.at[pl.ds(place, count)], sems.at[2 * i + j]
                )
            )
    for copy in copies:
        copy.start()
    unit, _ = normalised(x_ref[...].astype(F32))
    for copy in copies:
        copy.wait()
    keep = pltpu.make_async_copy(weight, weight_ref, sems.at[20])
    keep.start()
    vec = small[...].astype(F32).T
    vec_ref[...] = vec[:16]
    normed = (unit * vec[0:1] + vec[2:3]).astype(BF)
    held = outs[0].shape[0] // 3
    if parts * held != width:
        whole[...] = jnp.zeros_like(whole)
    for b in range(3):
        block = dot(normed, weight[:, b * width : (b + 1) * width], 1, 0)
        if b == 0:
            block = block + vec[3:4]
        if b == 2:
            block = block + vec[4:5]
        whole[b * parts * held : b * parts * held + width] = block.T.astype(BF)
    for d in range(parts):
        for b in range(3):
            first = pl.multiple_of(b * parts * held + ids_ref[d] * held, size)
            outs[d][b * held : (b + 1) * held] = whole[pl.ds(first, held)]
    keep.wait()


def qkv_project(ids, x, packs, parts, size, shards):
    rows, width = x.shape
    held = pl.cdiv(HEADS, parts) * size
    results = pl.pallas_call(
        functools.partial(qkv_kernel, parts=parts, size=size, shards=shards),
        in_specs=[SMEM, VMEM] + [HBM] * 10,
        out_specs=[VMEM] * parts + [HBM, VMEM],
        out_shape=[shape((3 * held, rows), BF)] * parts
        + [shape((width, 3 * width), BF), shape((16, width), F32)],
        scratch_shapes=[
            pltpu.VMEM((width, 3 * width), BF),
            pltpu.VMEM((width, LANES), BF),
            pltpu.VMEM((3 * parts * held, rows), BF),
            pltpu.SemaphoreType.DMA((21,)),
        ],
        compiler_params=PARAMS,
        name="qkv_project",
    )(ids, x, *packs)
    return results[:parts], results[parts], results[parts + 1]


def spans_of(order_ref, which, count, span):
    first = order_ref[which]
    return (
        (0, pl.multiple_of(first * span, span)),
        (1, pl.multiple_of((2 * count - 1 - first) * span, span)),
    )


def causal(scores, width, fill):
    depth = scores.shape[0]
    keys = lax.broadcasted_iota(jnp.int32, (width, width), 0)
    rows = lax.broadcasted_iota(jnp.int32, (width, width), 1)
    last = jnp.where(keys <= rows, scores[depth - width :], fill)
    if depth == width:
        return last
    return jnp.concatenate([scores[: depth - width], last], axis=0)


def sort_in(order_ref, pieces, target):
    count = len(pieces)
    span = pieces[0].shape[1] // 2
    for d in range(count):
        for side, place in spans_of(order_ref, d, count, span):
            target[:, pl.ds(place, span)] = pieces[d][:, side * span : (side + 1) * span]


def sort_out(order_ref, source, pieces):
    count = len(pieces)
    span = pieces[0].shape[1] // 2
    for d in range(count):
        for side, place in spans_of(order_ref, count + d, count, span):
            pieces[d][:, side * span : (side + 1) * span] = source[:, pl.ds(place, span)]


def attn_fwd_kernel(order_ref, *refs, parts, heads, size, block):
    pieces, mixed, (sorted_ref, out_ref, lse_ref) = refs[:parts], refs[parts : 2 * parts], refs[2 * parts :]
    feats = heads * size
    seq = sorted_ref.shape[1]
    sort_in(order_ref, pieces, sorted_ref)
    lse_ref[...] = jnp.zeros_like(lse_ref)
    for h in range(heads):
        for start in range(0, seq, block):
            end = start + block
            q = sorted_ref[h * size : (h + 1) * size, start:end]
            k = sorted_ref[feats + h * size : feats + (h + 1) * size, :end]
            v = sorted_ref[2 * feats + h * size : 2 * feats + (h + 1) * size, :end]
            scores = causal(dot(k, q, 0, 0) * 0.125, block, -1e30)
            top = jnp.max(scores, axis=0, keepdims=True)
            weights = jnp.exp(scores - top)
            total = jnp.sum(weights, axis=0, keepdims=True)
            mixed_part = dot(v, weights.astype(BF), 1, 0) / total
            out_ref[h * size : (h + 1) * size, start:end] = mixed_part.astype(BF)
            lse_ref[h : h + 1, start:end] = top + jnp.log(total)
    sort_out(order_ref, out_ref, mixed)


def attn_bwd_kernel(order_ref, *refs, parts, heads, size, block):
    pieces, (sorted_ref, out_ref, lse_ref) = refs[:parts], refs[parts : parts + 3]
    grads, (dsort, gsort, gk, gv) = refs[parts + 3 : 2 * parts + 3], refs[2 * parts + 3 :]
    feats = heads * size
    seq = sorted_ref.shape[1]
    sort_in(order_ref, pieces, dsort)
    for h in range(heads):
        own = slice(h * size, (h + 1) * size)
        gk[...] = jnp.zeros_like(gk)
        gv[...] = jnp.zeros_like(gv)
        for start in range(0, seq, block):
            end = start + block
            q = sorted_ref[own, start:end]
            k = sorted_ref[feats + h * size : feats + (h + 1) * size, :end]
            v = sorted_ref[2 * feats + h * size : 2 * feats + (h + 1) * size, :end]
            dout = dsort[own, start:end]
            delta = jnp.sum(
                dout.astype(F32) * out_ref[own, start:end].astype(F32), axis=0, keepdims=True
            )
            scores = dot(k, q, 0, 0) * 0.125 - lse_ref[h : h + 1, start:end]
            probs = jnp.exp(causal(scores, block, -1e30))
            dprobs = dot(v, dout, 0, 0)
            dscores = (probs * (dprobs - delta)).astype(BF)
            gsort[own, start:end] = (dot(k, dscores, 1, 0) * 0.125).astype(BF)
            gk[:, :end] += dot(q, dscores, 1, 1)
            gv[:, :end] += dot(dout, probs.astype(BF), 1, 1)
        gsort[feats + h * size : feats + (h + 1) * size, :] = (gk[...] * 0.125).astype(BF)
        gsort[2 * feats + h * size : 2 * feats + (h + 1) * size, :] = gv[...].astype(BF)
    sort_out(order_ref, gsort, grads)


def widen(pieces, order):
    count = len(pieces)
    span = pieces[0].shape[1] // 2
    came = order[:count]
    holder = jnp.stack([came, 2 * count - 1 - came], axis=1).reshape(-1)
    place = jnp.argsort(holder)
    flat = jnp.concatenate(pieces, axis=1).reshape(-1, 2 * count, span)
    return [jnp.take(flat, place, axis=1).reshape(flat.shape[0], -1)]


def narrow(wide, order, count):
    feats, seq = wide.shape
    span = seq // (2 * count)
    goes = order[count:]
    holder = jnp.stack([goes, 2 * count - 1 - goes], axis=1).reshape(-1)
    flat = jnp.take(wide.reshape(feats, 2 * count, span), holder, axis=1)
    flat = flat.reshape(feats, count, 2 * span)
    return [flat[:, d] for d in range(count)]


def attention_forward(pieces, order, size):
    parts, rows = len(pieces), pieces[0].shape[1]
    seq = parts * rows
    heads = pieces[0].shape[0] // (3 * size)
    narrow_spans = (rows // 2) % LANES != 0
    ids, given = order, parts
    if narrow_spans:
        pieces, ids, given = widen(pieces, order), jnp.zeros((2,), jnp.int32), 1
    results = pl.pallas_call(
        functools.partial(
            attn_fwd_kernel, parts=given, heads=heads, size=size, block=min(256, seq // 2)
        ),
        in_specs=[SMEM] + [VMEM] * given,
        out_specs=[VMEM] * (given + 3),
        out_shape=[shape((heads * size, pieces[0].shape[1]), BF)] * given
        + [
            shape((3 * heads * size, seq), BF),
            shape((heads * size, seq), BF),
            shape((8 * pl.cdiv(heads, 8), seq), F32),
        ],
        compiler_params=PARAMS,
        name="attn_fwd",
    )(ids, *pieces)
    mixed = results[:given]
    if narrow_spans:
        mixed = narrow(mixed[0], order, parts)
    return mixed, tuple(results[given:])


def attention_backward(pieces, saved, order, size):
    parts, rows = len(pieces), pieces[0].shape[1]
    seq = parts * rows
    heads = pieces[0].shape[0] // size
    narrow_spans = (rows // 2) % LANES != 0
    ids, given = order, parts
    if narrow_spans:
        pieces, ids, given = widen(pieces, order), jnp.zeros((2,), jnp.int32), 1
    grads = pl.pallas_call(
        functools.partial(
            attn_bwd_kernel, parts=given, heads=heads, size=size, block=min(256, seq // 2)
        ),
        in_specs=[SMEM] + [VMEM] * (given + 3),
        out_specs=[VMEM] * given,
        out_shape=[shape((3 * heads * size, pieces[0].shape[1]), BF)] * given,
        scratch_shapes=[
            pltpu.VMEM((heads * size, seq), BF),
            pltpu.VMEM((3 * heads * size, seq), BF),
            pltpu.VMEM((size, seq), F32),
            pltpu.VMEM((size, seq), F32),
        ],
        compiler_params=PARAMS,
        name="attn_bwd",
    )(ids, *pieces, *saved)
    if narrow_spans:
        grads = narrow(grads[0], order, parts)
    return grads


def down_blocks(shards, ratio, depth):
    width = shards * depth
    for f in range(shards):
        for j in range(ratio):
            first = (f * ratio + j) * depth
            yield slice(first, first + depth), slice(f * depth, (f + 1) * depth), j * width


def rest_copies(pack, w_out, w_up, w_down, sems, shards, ratio):
    width = w_out.shape[0]
    depth = width // shards
    hidden = w_up.shape[1]
    out = [pltpu.make_async_copy(pack.at[:, :width], w_out, sems.at[0])]
    up = [pltpu.make_async_copy(pack.at[:, width : width + hidden], w_up, sems.at[1])]
    down = []
    for i, (rows, packed, column) in enumerate(down_blocks(shards, ratio, depth)):
        start = width + hidden + column
        down.append(
            pltpu.make_async_copy(
                pack.at[packed, start : start + width], w_down.at[rows], sems.at[2 + i]
            )
        )
    return out, up, down


def put_pieces(ids_ref, first, pieces, target):
    held = pieces[0].shape[0]
    for d, piece in enumerate(pieces):
        place = pl.multiple_of(ids_ref[first + d] * held, held)
        target[pl.ds(place, held)] = piece[...]


def mlp_kernel(ids_ref, x_ref, vec_ref, bias_ref, pack_ref, *refs, parts, shards, ratio):
    pieces = refs[:parts]
    result_ref, inner_ref, hidden_ref, mixed_ref = refs[parts : parts + 4]
    w_out, w_up, w_down, whole, sems = refs[parts + 4 :]
    width = x_ref.shape[1]
    out, up, down = rest_copies(pack_ref, w_out, w_up, w_down, sems, shards, ratio)
    for copy in out + up + down:
        copy.start()
    put_pieces(ids_ref, parts, pieces, whole)
    mixed_ref[...] = whole[:width]
    out[0].wait()
    inner = x_ref[...].astype(F32) + dot(whole[:width], w_out[...], 0, 0) + vec_ref[5:6]
    inner_ref[...] = inner
    unit, _ = normalised(inner)
    middle = (unit * vec_ref[1:2] + vec_ref[6:7]).astype(BF)
    up[0].wait()
    for copy in down:
        copy.wait()
    total = inner + vec_ref[7:8]
    for start in range(0, w_up.shape[1], width):
        cols = slice(start, start + width)
        hidden = dot(middle, w_up[:, cols], 1, 0) + bias_ref[:, cols]
        hidden_ref[:, cols] = hidden
        act = 0.5 * hidden * (1.0 + jnp.tanh(GELU_C * (hidden + GELU_A * hidden * hidden * hidden)))
        total = total + dot(act.astype(BF), w_down[cols], 1, 0)
    result_ref[...] = total.astype(BF)


def rest_scratch(width, hidden, shards, ratio):
    return [
        pltpu.VMEM((width, width), BF),
        pltpu.VMEM((width, hidden), BF),
        pltpu.VMEM((hidden, width), BF),
    ]


def mlp_forward(ids, x, vec, bias, pack, pieces, shards, ratio):
    parts = len(pieces)
    rows, width = x.shape
    hidden = ratio * width
    return pl.pallas_call(
        functools.partial(mlp_kernel, parts=parts, shards=shards, ratio=ratio),
        in_specs=[SMEM, VMEM, VMEM, VMEM, HBM] + [VMEM] * parts,
        out_specs=[VMEM] * 4,
        out_shape=[
            shape((rows, width), BF),
            shape((rows, width), F32),
            shape((rows, hidden), F32),
            shape((width, rows), BF),
        ],
        scratch_shapes=rest_scratch(width, hidden, shards, ratio)
        + [
            pltpu.VMEM((parts * pieces[0].shape[0], rows), BF),
            pltpu.SemaphoreType.DMA((2 + shards * ratio,)),
        ],
        compiler_params=PARAMS,
        name="mlp_forward",
    )(ids, x, vec, bias, pack, *pieces)


def mlp_back_kernel(
    ids_ref, grad_ref, inner_ref, hidden_ref, vec_ref, pack_ref, *refs, parts, shards, ratio
):
    outs = refs[:parts]
    ginner_ref, gattn_ref, ghid_ref, act_ref, middle_ref, table_ref = refs[parts : parts + 6]
    w_out, w_up, w_down, whole, sems = refs[parts + 6 :]
    width = grad_ref.shape[1]
    out, up, down = rest_copies(pack_ref, w_out, w_up, w_down, sems, shards, ratio)
    for copy in down + up + out:
        copy.start()
    grad_low = grad_ref[...].astype(BF)
    unit, scale = normalised(inner_ref[...])
    middle_ref[...] = (unit * vec_ref[1:2] + vec_ref[6:7]).astype(BF)
    for copy in down:
        copy.wait()
    up[0].wait()
    up_mid = jnp.zeros(unit.shape, F32)
    depth = width // shards
    table_ref[...] = jnp.zeros_like(table_ref)
    for start in range(0, w_up.shape[1], width):
        cols = slice(start, start + width)
        hidden = hidden_ref[:, cols]
        th = jnp.tanh(GELU_C * (hidden + GELU_A * hidden * hidden * hidden))
        act_ref[:, cols] = (0.5 * hidden * (1.0 + th)).astype(BF)
        slope = 0.5 * (1.0 + th) + 0.5 * hidden * (1.0 - th * th) * GELU_C * (
            1.0 + 3.0 * GELU_A * hidden * hidden
        )
        grad_hid = (dot(grad_low, w_down[cols], 1, 1) * slope).astype(BF)
        ghid_ref[:, cols] = grad_hid
        sums = jnp.sum(grad_hid.astype(F32), axis=0, keepdims=True)
        for i in range(width // depth):
            f, j = divmod(start // depth + i, ratio)
            table_ref[8 + j : 9 + j, f * depth : (f + 1) * depth] = sums[:, i * depth : (i + 1) * depth]
        up_mid = up_mid + dot(grad_hid, w_up[:, cols], 1, 1)
    grad_inner = grad_ref[...].astype(F32) + norm_back(unit, scale, up_mid, vec_ref[1:2])
    ginner_ref[...] = grad_inner
    grad_attn = grad_inner.astype(BF)
    gattn_ref[...] = grad_attn
    out[0].wait()
    held = outs[0].shape[0]
    if parts * held != width:
        whole[...] = jnp.zeros_like(whole)
    whole[:width] = dot(w_out[...], grad_attn, 1, 1).astype(BF)
    for d in range(parts):
        outs[d][...] = whole[pl.ds(pl.multiple_of(ids_ref[d] * held, held), held)]
    table_ref[1:2] = jnp.sum(up_mid * unit, axis=0, keepdims=True)
    table_ref[5:6] = jnp.sum(grad_attn.astype(F32), axis=0, keepdims=True)
    table_ref[6:7] = jnp.sum(up_mid, axis=0, keepdims=True)
    table_ref[7:8] = jnp.sum(grad_low.astype(F32), axis=0, keepdims=True)


def mlp_backward(ids, grad, inner, hidden, vec, pack, parts, size, shards, ratio):
    rows, width = inner.shape
    held = pl.cdiv(HEADS, parts) * size
    wide = ratio * width
    results = pl.pallas_call(
        functools.partial(mlp_back_kernel, parts=parts, shards=shards, ratio=ratio),
        in_specs=[SMEM, VMEM, VMEM, VMEM, VMEM, HBM],
        out_specs=[VMEM] * (parts + 6),
        out_shape=[shape((held, rows), BF)] * parts
        + [
            shape((rows, width), F32),
            shape((rows, width), BF),
            shape((rows, wide), BF),
            shape((rows, wide), BF),
            shape((rows, width), BF),
            shape((LANES, width), F32),
        ],
        scratch_shapes=rest_scratch(width, wide, shards, ratio)
        + [
            pltpu.VMEM((parts * held, rows), BF),
            pltpu.SemaphoreType.DMA((2 + shards * ratio,)),
        ],
        compiler_params=PARAMS,
        name="mlp_backward",
    )(ids, grad, inner, hidden, vec, pack)
    return results[:parts], results[parts:]


def write_down(act_ref, glow_ref, pack, start, shards, ratio):
    width = glow_ref.shape[1]
    depth = width // shards
    glow = glow_ref[...].astype(BF)
    for f in range(shards):
        block = dot(act_ref[:, f * ratio * depth : (f + 1) * ratio * depth], glow, 0, 0).astype(BF)
        for j in range(ratio):
            first = start + j * width
            pack[f * depth : (f + 1) * depth, first : first + width] = block[
                j * depth : (j + 1) * depth
            ]


def send_sides(ids_ref, first, pack, start, count, targets, sems, offset, shards):
    depth = pack.shape[0] // shards
    rows = depth // 2
    copies = []
    for side in range(2):
        core = ids_ref[first + shards + side]
        for k in range(shards):
            place = pl.multiple_of(ids_ref[first + k] * depth + core * rows, 16)
            copies.append(
                pltpu.make_async_copy(
                    pack.at[pl.ds(place, rows), start : start + count],
                    targets[side].at[k],
                    sems.at[offset + side * shards + k],
                )
            )
    for copy in copies:
        copy.start()
    return copies


def early_kernel(
    ids_ref, middle_ref, ghid_ref, mixed_ref, gattn_ref, act_ref, glow_ref, *refs, parts, shards, ratio, apart
):
    if apart:
        outs, (scratch, sems) = refs[:2], refs[2:]
    else:
        pack_ref, scratch, sems = refs
    width = middle_ref.shape[1]
    main = (1 + ratio) * width
    copies = []

    def send(columns, i):
        copy = pltpu.make_async_copy(scratch.at[:, columns], pack_ref.at[:, columns], sems.at[i])
        copy.start()
        copies.append(copy)

    scratch[:, :width] = dot(mixed_ref[...], gattn_ref[...], 1, 0).astype(BF)
    for i in range(ratio):
        cols = slice(i * width, (i + 1) * width)
        block = dot(middle_ref[...], ghid_ref[:, cols], 0, 0).astype(BF)
        scratch[:, (i + 1) * width : (i + 2) * width] = block
    if not apart:
        send(slice(0, main), 0)
    write_down(act_ref, glow_ref, scratch, main, shards, ratio)
    if apart:
        copies += send_sides(
            ids_ref, 2 * parts, scratch, 0, main + ratio * width, outs, sems, 0, shards
        )
    else:
        send(slice(main, main + ratio * width), 1)
    for copy in copies:
        copy.wait()


def early_grads(ids, middle, ghid, mixed, gattn, act, grad, parts, shards, ratio, apart):
    width = middle.shape[1]
    main, hidden = (1 + ratio) * width, ratio * width
    rows = width // shards // 2
    side = shape((shards, rows, main + hidden), BF)
    return pl.pallas_call(
        functools.partial(early_kernel, parts=parts, shards=shards, ratio=ratio, apart=apart),
        in_specs=[SMEM] + [VMEM] * 6,
        out_specs=[HBM] * (2 if apart else 1),
        out_shape=[side, side] if apart else [shape((width, main + hidden), BF)],
        scratch_shapes=[
            pltpu.VMEM((width, main + hidden), BF),
            pltpu.SemaphoreType.DMA((2 + 2 * shards,)),
        ],
        compiler_params=PARAMS,
        name="early_grads",
    )(ids, middle, ghid, mixed, gattn, act, grad)


def qkv_back_kernel(
    ids_ref, x_ref, ginner_ref, vec_ref, table_ref, weight_hbm, *refs, parts, shards
):
    pieces, refs = refs[:parts], refs[parts:]
    gx_ref, *outs, weight, whole, pack, sem = refs
    width = x_ref.shape[1]
    main = 3 * width + LANES
    copies = []
    copy = pltpu.make_async_copy(weight_hbm, weight, sem.at[0])
    copy.start()
    held = pieces[0].shape[0] // 3
    padded = parts * held
    for d, piece in enumerate(pieces):
        for b in range(3):
            place = pl.multiple_of(b * padded + ids_ref[parts + d] * held, held)
            whole[pl.ds(place, held)] = piece[b * held : (b + 1) * held]
    unit, scale = normalised(x_ref[...].astype(F32))
    normed = (unit * vec_ref[0:1] + vec_ref[2:3]).T.astype(BF)
    copy.wait()
    up_norm = jnp.zeros((width, x_ref.shape[0]), F32)
    sums = []
    for b in range(3):
        grads = whole[b * padded : b * padded + width]
        cols = slice(b * width, (b + 1) * width)
        up_norm = up_norm + dot(weight[:, cols], grads, 1, 0)
        pack[:, cols] = dot(normed, grads, 1, 1).astype(BF)
        sums.append(jnp.sum(grads.astype(F32), axis=1, keepdims=True))
    up_norm = up_norm.T
    gx_ref[...] = (ginner_ref[...] + norm_back(unit, scale, up_norm, vec_ref[0:1])).astype(BF)
    line = lax.broadcasted_iota(jnp.int32, table_ref.shape, 0)
    table = jnp.where(
        line == 0,
        jnp.sum(up_norm * unit, axis=0, keepdims=True),
        jnp.where(line == 2, jnp.sum(up_norm, axis=0, keepdims=True), table_ref[...]),
    ).T
    lane = lax.broadcasted_iota(jnp.int32, table.shape, 1)
    table = jnp.where(lane == 3, sums[0], jnp.where(lane == 4, sums[2], table))
    pack[:, 3 * width : main] = table.astype(BF)
    copies += send_sides(ids_ref, 2 * parts, pack, 0, main, outs, sem, 1, shards)
    for copy in copies:
        copy.wait()


def qkv_backward(ids, x, ginner, vec, table, weight, pieces, shards):
    parts = len(pieces)
    rows, width = x.shape
    total = 3 * width + LANES
    part = shape((shards, width // shards // 2, total), BF)
    return pl.pallas_call(
        functools.partial(qkv_back_kernel, parts=parts, shards=shards),
        in_specs=[SMEM, VMEM, VMEM, VMEM, VMEM, HBM] + [VMEM] * parts,
        out_specs=[VMEM, HBM, HBM],
        out_shape=[shape((rows, width), BF), part, part],
        scratch_shapes=[
            pltpu.VMEM((width, 3 * width), BF),
            pltpu.VMEM((parts * pieces[0].shape[0], rows), BF),
            pltpu.VMEM((width, total), BF),
            pltpu.SemaphoreType.DMA((1 + 2 * shards,)),
        ],
        compiler_params=PARAMS,
        name="qkv_backward",
    )(ids, x, ginner, vec, table, weight, *pieces)


def layer_forward(x, packs, rest, ids, order, parts, size, shards, ratio, back=None):
    sent, weight, vec = qkv_project(ids, x, packs, parts, size, shards)
    width = x.shape[1]
    depth = width // shards
    bias = vec[8 : 8 + ratio].reshape(ratio, shards, depth).transpose(1, 0, 2).reshape(1, -1)
    received = exchange(sent)
    returned = None
    if back is not None:
        *received, back = lax.optimization_barrier((*received, back))
        returned = return_rows(back, 0)
    mixed, attn_saved = attention_forward(received, order, size)
    received = exchange(mixed)
    if back is not None:
        tied = lax.optimization_barrier((*received, *returned))
        received, returned = tied[:parts], tied[parts:]
    result, inner, hidden, mixed = mlp_forward(
        ids, x, vec, bias, rest, received, shards, ratio
    )
    return result, (x, weight, vec, attn_saved, inner, hidden, mixed), returned


def layer_backward(
    saved, grad, rest, ids, order, parts, size, shards, ratio, layer, background, result=None
):
    x, weight, vec, attn_saved, inner, hidden, mixed = saved
    last = layer == 0
    column = (1 + ratio) * x.shape[1]
    sent, (ginner, gattn, ghid, act, middle, table) = mlp_backward(
        ids, grad, inner, hidden, vec, rest, parts, size, shards, ratio
    )
    received = exchange(background.slot("AD", sent))
    early = early_grads(ids, middle, ghid, mixed, gattn, act, grad, parts, shards, ratio, last)
    tied = lax.optimization_barrier((*received, *early, result if result is not None else grad))
    received, early = tied[:parts], tied[parts:-1]
    returned = None
    if last:
        first = background.add("B", early_task0(*early, background, column))
    else:
        first = background.add("C", early_task1(*early, background, column))
        returned = background.add("A", return_task(tied[-1], layer, 0))
    sent = attention_backward(received, attn_saved, order, size)
    sent = background.slot("BC" if last else "A", sent)
    received = exchange(sent)
    if last:
        received = background.slot("CD", received)
    grad_x, *late = lax.optimization_barrier(
        tuple(qkv_backward(ids, x, ginner, vec, table, weight, received, shards))
    )
    if last:
        for lane in "EB":
            background.slot(lane, [grad_x])
        second = background.add("A", late_task0(*late, background))
    else:
        second = background.add("D", late_task1(*late, background))
    return grad_x, first, second, returned


def blocks_to_columns(value, parts):
    depth = value.shape[0] // parts
    return [value[i * depth : (i + 1) * depth] for i in range(parts)]


def split_layers(pack, core):
    rows = pack.shape[0] // 2
    first, second = pack[:rows], pack[rows:]
    other = lax.ppermute(jnp.where(core == 0, second, first), "section", [(0, 1), (1, 0)])
    return jnp.where(core == 0, first, other), jnp.where(core == 0, other, second)


def gather(part):
    return lax.all_gather(part, SHARDS, axis=0, tiled=True)


def across(value, bit):
    count = lax.axis_size("fsdp")
    return lax.ppermute(value, "fsdp", [(i, i ^ bit) for i in range(count)])


def swap_cores(value):
    return lax.ppermute(value, "section", [(0, 1), (1, 0)])


def gather_pieces(part):
    rows = part.shape[0] // 2
    by_x, by_y = across(part, 1), across(part, 2)
    pieces = [part, by_x, by_y, across(by_x[:rows], 2), across(by_y[rows:], 1)]
    return pieces + [swap_cores(piece) for piece in pieces]


class Background:
    def __init__(self):
        self.tasks = []
        self.links = {}

    def send(self, link, value, axis, pairs):
        if link in self.links:
            value, _ = lax.optimization_barrier((value, self.links[link]))
        moved = lax.ppermute(value, axis, pairs)
        self.links[link] = moved
        return moved

    def across(self, value, bit):
        count = lax.axis_size("fsdp")
        return self.send(bit, value, "fsdp", [(i, i ^ bit) for i in range(count)])

    def add(self, lane, task):
        entry = {"lane": lane, "task": task, "result": None}
        entry["flight"] = next(task)
        self.tasks.append(entry)
        return entry

    def resume(self, entry, flight):
        try:
            entry["flight"] = entry["task"].send(flight)
        except StopIteration as stop:
            entry["flight"], entry["result"] = None, stop.value

    def slot(self, lanes, values=()):
        waiting = [e for e in self.tasks if e["flight"] is not None and e["lane"] in lanes]
        flat = list(values)
        for entry in waiting:
            flat += entry["flight"]
        if len(flat) > 0:
            flat = list(lax.optimization_barrier(tuple(flat)))
        values, flat = flat[: len(values)], flat[len(values) :]
        for entry in waiting:
            count = len(entry["flight"])
            self.resume(entry, flat[:count])
            flat = flat[count:]
        return values

    def finish(self):
        while any(entry["flight"] is not None for entry in self.tasks):
            for entry in list(self.tasks):
                if entry["flight"] is not None:
                    self.resume(entry, entry["flight"])


def idle(values, slots):
    for _ in range(slots):
        values = yield list(values)
    return values


def permuted_value(keep, send, background, hold):
    (received,) = yield [swap_cores(send)]
    (received,) = yield from idle([received], hold)
    rows = keep.shape[1] // 2

    def summed(slots, side):
        return sum_pair(keep[slots, side], received[slots, side])

    top, low = slice(0, rows), slice(rows, 2 * rows)
    by_x, by_y = yield [
        background.across(summed(slice(1, 4, 2), top), 1),
        background.across(summed(slice(2, 4), low), 2),
    ]
    first = sum_pair(summed(slice(0, 4, 2), top), by_x)
    second = sum_pair(summed(slice(0, 2), low), by_y)
    by_y, by_x = yield [background.across(first[1], 2), background.across(second[1], 1)]
    return jnp.concatenate([sum_pair(first[0], by_y), sum_pair(second[0], by_x)])


def early_task0(keep, send, background, column):
    value = yield from permuted_value(keep, send, background, 0)
    other = background.add("D", ctx_task(value[:, column:], 0, background, 1))
    mine = yield from ctx_task(value[:, :column], 0, background)
    return mine, other


def late_task0(keep, send, background):
    value = yield from permuted_value(keep, send, background, 0)
    return (yield from ctx_task(value, 0, background))


def early_task1(pack, background, column):
    value = lax.psum_scatter(pack, SHARDS, scatter_dimension=0, tiled=True)
    (value,) = yield [value]
    (value,) = yield [value]
    other = background.add("E", ctx_task(value[:, column:], 1, background))
    mine = yield from ctx_task(value[:, :column], 1, background)
    return mine, other


def late_task1(keep, send, background):
    value = yield from permuted_value(keep, send, background, 2)
    return (yield from ctx_task(value, 1, background))


def ctx_task(value, layer, background, before=0):
    (value,) = yield from idle([value], before)
    if lax.axis_size("ctx") == 4:
        index = lax.axis_index("ctx")
        (received,) = yield [background.send("in", value, "ctx", [(0, 1), (3, 2)])]
        value = sum_pair(value, received)
        (received,) = yield [background.send("mid", value, "ctx", [(1, 2), (2, 1)])]
        value = sum_pair(value, received)
        (received,) = yield [background.send("out", value, "ctx", [(1, 0), (2, 3)])]
        value = jnp.where((index == 0) | (index == 3), received, value)
    else:
        value = lax.psum(value, "ctx")
    (other,) = yield [lax.ppermute(value, "section", [(1 - layer, layer)])]
    return value, other


def return_task(value, layer, pause, background=None):
    (value,) = yield from idle([value], pause)
    flight = yield return_rows(value, layer, background)
    return flight


def sum_pair(a, b):
    return (a.astype(F32) + b.astype(F32)).astype(BF)


def body(
    tokens, cotangent, span_order, w_qkv, w_out, w_up, w_down, norm_gains, bias_rows, bias_hidden
):
    core = lax.axis_index("section")
    ctx = lax.axis_size("ctx")
    cores = lax.axis_size("section")
    shards = lax.axis_size("fsdp")
    half = ctx // cores
    base = lax.axis_index("ctx") // half
    member = core * half + lax.axis_index("ctx") % half
    depth = w_qkv.shape[1]
    width = depth * shards
    ratio = bias_hidden.shape[1] // depth
    size = width // HEADS
    gain_count, shift_count = norm_gains.shape[1], bias_rows.shape[1]

    steps = jnp.arange(ctx, dtype=jnp.int32)
    came, goes = (member - steps) % ctx, (member + steps) % ctx
    shard = lax.axis_index("fsdp")
    slots = [shard ^ k for k in range(shards)] + [core, 1 - core]
    ids = jnp.concatenate([goes, came, jnp.stack(slots)]).astype(jnp.int32)
    order = jnp.concatenate([span_order[came], span_order[goes]])

    small = jnp.concatenate([norm_gains[0], bias_rows[0], bias_hidden[0].reshape(ratio, depth)]).T
    small = jnp.pad(small, ((0, 0), (0, LANES - small.shape[1])))
    first = jnp.concatenate([w_qkv[0], small], axis=1)
    rest = jnp.concatenate([w_out[0], w_up[0]] + blocks_to_columns(w_down[0], ratio), axis=1)
    first0, first1 = split_layers(first, core)
    x = bring_rows(tokens[:, 0], core, base)
    rest0, rest1 = split_layers(rest, core)
    first0, first1 = gather_pieces(first0), gather_pieces(first1)
    rest0, rest1 = gather(rest0), gather(rest1)
    sizes = (ids, order, ctx, size, shards, ratio)
    out0, saved0, _ = layer_forward(x, first0, rest0, *sizes)
    late_cot, out0 = lax.optimization_barrier((cotangent[:, 0], out0))
    out1, saved1, back_out0 = layer_forward(out0, first1, rest1, *sizes, out0)
    cot = bring_rows(late_cot, core, base)
    background = Background()
    grad1, early1, late1, back_out1 = layer_backward(
        saved1, cot, rest1, *sizes, 1, background, out1
    )
    back1 = background.add("A", return_task(grad1, 1, 0))
    grad0, early0, late0, _ = layer_backward(saved0, grad1, rest0, *sizes, 0, background)
    back0 = background.add("A", return_task(grad0, 0, 1, background))
    background.finish()

    def chosen(values0, values1):
        return jnp.stack([jnp.where(core == 0, a, b) for a, b in zip(values0, values1)])

    layer_outputs = chosen(back_out0, back_out1["result"])
    input_grads = chosen(back0["result"], back1["result"]).astype(F32)

    def joined(pair0, pair1):
        return jnp.where(
            core == 0,
            jnp.concatenate([pair0[0], pair0[1]]),
            jnp.concatenate([pair1[1], pair1[0]]),
        ).astype(F32)

    (up0, down0), (up1, down1) = early0["result"], early1["result"]
    early = joined(up0, up1)
    late = joined(late0["result"], late1["result"])
    down = joined(down0["result"], down1["result"])
    table = late[:, 3 * width :].T
    return (
        layer_outputs[None, :, None],
        input_grads[None, :, None],
        late[None, :, : 3 * width],
        early[None, :, :width],
        early[None, :, width:],
        jnp.concatenate([down[:, j * width : (j + 1) * width] for j in range(ratio)])[None],
        table[None, :gain_count],
        table[None, gain_count : gain_count + shift_count],
        table[gain_count + shift_count : gain_count + shift_count + ratio].reshape(1, -1),
    )


def solution(mesh):
    return jax.shard_map(
        body,
        mesh=mesh,
        in_specs=(
            P(None, "fsdp", "ctx", None),
            P(None, "fsdp", "ctx", None),
            P(),
            P("section", "fsdp", None),
            P("section", "fsdp", None),
            P("section", "fsdp", None),
            P("section", "fsdp", None),
            P("section", None, "fsdp"),
            P("section", None, "fsdp"),
            P("section", "fsdp"),
        ),
        out_specs=(
            P("section", None, "fsdp", "ctx", None),
            P("section", None, "fsdp", "ctx", None),
            P("section", "fsdp", None),
            P("section", "fsdp", None),
            P("section", "fsdp", None),
            P("section", "fsdp", None),
            P("section", None, "fsdp"),
            P("section", None, "fsdp"),
            P("section", "fsdp"),
        ),
        check_vma=False,
    )
```
